32 devices in a mesh: sx: 4 (over z), sy: 4 (over x, core), fq: 2 (over y).
Axes of the slice: x: 2, y: 2, z: 4, core: 2. Of those that a mesh axis runs over, the one named last changes fastest.
Arguments:
- spectra: bfloat16 [16, 2, 128, 64, 512], P('fq', None, 'sx', 'sy'), may hold values from -0.125 to 0.125
- noise_weight: float32 [512, 32], P(('sx', 'sy')), may hold values from 0.5 to 2
- class_map: int32 [128, 64], P('sx', 'sy'), may hold values from 0 to 7
- class_kappa: float32 [8], replicated, may hold values from 0.25 to 4
- solution: float32 [16, 512, 32], P('fq', ('sx', 'sy')), may hold values from -6 to 6
- residual: float32 [16, 512, 32], P('fq', ('sx', 'sy')), may hold values from -6 to 6
- direction: float32 [16, 512, 32], P('fq', ('sx', 'sy')), may hold values from -6 to 6
- step_length: float32 [16], P('fq'), may hold values from 0.2 to 1
- old_norm: float32 [16], P('fq'), may hold values from 16384 to 65536
Outputs:
- new_solution: float32 [16, 512, 32], P('fq', ('sx', 'sy'))
- new_residual: float32 [16, 512, 32], P('fq', ('sx', 'sy'))
- new_direction: float32 [16, 512, 32], P('fq', ('sx', 'sy'))
- new_norm: float32 [16], P('fq')
The draws below stay inside these ranges and needn't reach their ends.
All inputs are finite; a program needn't handle non-finite values.
Results may differ from the reference program's by a relative error of at most 0.0022.
Values may be sent and summed in bfloat16 or wider, within the bound.
No kernel may reach another device: no remote copies, remote signals or barrier semaphores. Data moves between devices by JAX's collectives and lax.ppermute only.
A program may use at most 128 MiB of HBM per device.

```python
import math
import jax
import jax.numpy as jnp
from jax import lax

SENS = 512
SWEEPS = 4
NCLS = 8
NX = 128
NY = 64
FREQ = 16
NT = 32
COLS = 16


def set_ends(array, rng, low, top_value):
    extent = array.shape
    index_at = [jax.random.randint(jax.random.fold_in(rng, axis), (), 0, extent[axis]) for axis in range(len(extent))]
    array = array.at[tuple(index_at)].set(low)
    longest = extent.index(max(extent))
    index_at[longest] = (index_at[longest] + 1) % extent[longest]
    return array.at[tuple(index_at)].set(top_value)


def block_levels(stream_key, shape, shards, low, high):
    gain = 1.0
    for dim, shards_of in shards:
        steps = jax.random.uniform(jax.random.fold_in(jax.random.fold_in(stream_key, 6), dim), (shards_of,), jnp.float32, low / len(shards), high / len(shards))
        gain = gain * jnp.repeat(jnp.exp(steps), shape[dim] // shards_of).reshape((-1,) + (1,) * (len(shape) - 1 - dim))
    return gain


def bell_draw(own_key, shape, width, most, pieces=(), kind=jnp.bfloat16):
    entries = jax.random.normal(own_key, shape, jnp.float32) * width
    if len(pieces) > 0:
        entries = block_levels(own_key, shape, pieces, -0.22, 0.18) * entries
    return jnp.clip(entries, min=-most, max=most).astype(kind)


def setup_inputs(seed: int = 0) -> dict:
    seeds = jax.random.split(jax.random.key(seed), 10)
    spectra = bell_draw(seeds[0], (FREQ, 2, NX, NY, SENS), (4 * SENS) ** -0.5, 0.125, ((0, 2), (2, 4), (3, 4)))
    noise_weight = jnp.clip(jnp.exp(math.log(2.0) - 1.3862944 * jax.random.uniform(seeds[1], (SENS, NT), jnp.float32) ** block_levels(seeds[1], (SENS, NT), ((0, 16),), -0.2, 0.2)), 0.5, 2.0)
    class_map = set_ends(jax.random.randint(seeds[2], (NX, NY), 0, NCLS), jax.random.fold_in(seeds[2], 1), 0, NCLS - 1).astype(jnp.int32)
    class_kappa = jnp.clip(jnp.exp(jax.random.uniform(seeds[3], (NCLS,), jnp.float32, math.log(0.25), math.log(4.0))), 0.25, 4.0)
    solution = bell_draw(seeds[4], (COLS, SENS, NT), 1.0, 6.0, ((0, 2), (1, 16)), jnp.float32)
    residual = bell_draw(seeds[5], (COLS, SENS, NT), 1.0, 6.0, ((0, 2), (1, 16)), jnp.float32)
    direction = bell_draw(seeds[6], (COLS, SENS, NT), 1.0, 6.0, ((0, 2), (1, 16)), jnp.float32)
    step_length = jnp.clip(jnp.exp(math.log(1.0) - 1.609438 * jax.random.uniform(seeds[7], (COLS,), jnp.float32) ** block_levels(seeds[7], (COLS,), ((0, 2),), -0.2, 0.2)), 0.2, 1.0)
    old_norm = jnp.clip(jnp.exp(math.log(65536.0) - 1.3862944 * jax.random.uniform(seeds[8], (COLS,), jnp.float32) ** block_levels(seeds[8], (COLS,), ((0, 2),), -0.2, 0.2)), 16384.0, 65536.0)
    return {"spectra": spectra, "noise_weight": noise_weight, "class_map": class_map, "class_kappa": class_kappa, "solution": solution, "residual": residual, "direction": direction, "step_length": step_length, "old_norm": old_norm}


HIGHEST = lax.Precision.HIGHEST

def tables(freq_count, time_steps):
    freq_index = jnp.arange(freq_count, dtype=jnp.int32)[:, None]
    step_index = jnp.arange(time_steps, dtype=jnp.int32)[None, :]
    phases = (freq_index * step_index % time_steps).astype(jnp.float32) * (2.0 * math.pi / time_steps)
    factor = 1.0 / math.sqrt(time_steps)
    cosine_table = jnp.cos(phases) * factor
    sine_table = jnp.sin(phases) * factor
    doubling = jnp.where(jnp.arange(freq_count, dtype=jnp.int32) == 0, 1.0, 2.0).astype(jnp.float32)
    return (cosine_table, sine_table, doubling)

def neighbours(padded):
    return padded[2:, 1:-1] + padded[:-2, 1:-1] + padded[1:-1, 2:] + padded[1:-1, :-2]

def reference(spectra, noise_weight, class_map, class_kappa, solution, residual, direction, step_length, old_norm):
    cosine_table, sine_table, doubling = tables(FREQ, NT)
    weighted = noise_weight[None] * direction
    spec_real = jnp.einsum('kst,ft->fks', weighted, cosine_table, precision=HIGHEST).astype(jnp.bfloat16)
    spec_imag = (-jnp.einsum('kst,ft->fks', weighted, sine_table, precision=HIGHEST)).astype(jnp.bfloat16)
    kappa_cells = class_kappa[class_map][:, :, None]
    denom = 1.0 + 4.0 * kappa_cells

    def one_freq(inputs):
        weights, query_real, query_imag = inputs
        real_part = weights[0].astype(jnp.float32)
        imag_part = weights[1].astype(jnp.float32)
        query_real = query_real.astype(jnp.float32)
        query_imag = query_imag.astype(jnp.float32)
        pattern = 'xys,ks->xyk'
        adjoint_real = jnp.einsum(pattern, real_part, query_real) + jnp.einsum(pattern, imag_part, query_imag)
        adjoint_imag = jnp.einsum(pattern, real_part, query_imag) - jnp.einsum(pattern, imag_part, query_real)
        source = jnp.concatenate([adjoint_real, adjoint_imag], axis=2)
        smooth = source / denom
        for sweep_index in range(SWEEPS - 1):
            padded = jnp.pad(smooth, ((1, 1), (1, 1), (0, 0)))
            smooth = (source + kappa_cells * neighbours(padded)) / denom
        field_half = lax.optimization_barrier(smooth.astype(jnp.bfloat16))
        field_full = field_half.astype(jnp.float32)
        field_real = field_full[:, :, :COLS]
        field_imag = field_full[:, :, COLS:]
        forward = 'xys,xyk->sk'
        out_real = jnp.einsum(forward, real_part, field_real) - jnp.einsum(forward, imag_part, field_imag)
        out_imag = jnp.einsum(forward, real_part, field_imag) + jnp.einsum(forward, imag_part, field_real)
        return (out_real, out_imag)
    sums_real, sums_imag = lax.map(one_freq, (spectra, spec_real, spec_imag))
    scaled_real = sums_real * doubling[:, None, None]
    scaled_imag = sums_imag * doubling[:, None, None]
    returned = jnp.einsum('fsk,ft->kst', scaled_real, cosine_table, precision=HIGHEST) - jnp.einsum('fsk,ft->kst', scaled_imag, sine_table, precision=HIGHEST)
    product = direction + noise_weight[None] * returned
    new_solution = solution + step_length[:, None, None] * direction
    new_residual = residual - step_length[:, None, None] * product
    new_norm = lax.optimization_barrier(jnp.sum(new_residual * new_residual, axis=(1, 2)))
    new_direction = new_residual + (new_norm / old_norm)[:, None, None] * direction
    return (new_solution, new_residual, new_direction, new_norm)
```

```python
import functools
import math

import jax
import jax.numpy as jnp
from jax import lax
from jax.experimental import pallas as pl
from jax.experimental.pallas import tpu as pltpu
from jax.sharding import PartitionSpec as P
import numpy as np

SWEEPS = 4
DEPTH = SWEEPS - 1
HIGHEST = lax.Precision.HIGHEST
F32 = jnp.float32
BF16 = jnp.bfloat16
GRID_AXES = ("sx", "sy")
ALL_AXES = ("sx", "sy", "fq")
LANES = 128
VMEM_LIMIT = 48 * 1024 * 1024
VMEM = pl.BlockSpec(memory_space=pltpu.VMEM)
SMEM = pl.BlockSpec(memory_space=pltpu.SMEM)
ANY = pl.BlockSpec(memory_space=pl.ANY)


def params():
    return pltpu.CompilerParams(vmem_limit_bytes=VMEM_LIMIT)


def tables(freq_count, local_freqs, local_cols, time_steps):
    freq = np.arange(freq_count)[:, None]
    step = np.arange(time_steps)[None, :]
    phases = (freq * step % time_steps) * (2.0 * math.pi / time_steps)
    factor = 1.0 / math.sqrt(time_steps)
    pair = np.stack([np.cos(phases) * factor, -np.sin(phases) * factor], 1)
    forward = np.repeat(pair.reshape(2 * freq_count, time_steps), local_cols, 0)
    doubling = np.where(np.arange(freq_count) == 0, 1.0, 2.0)[:, None, None]
    inverse = np.repeat((pair * doubling).reshape(2 * freq_count, time_steps), local_cols, 0)
    return forward.T.astype(np.float32), inverse.astype(np.float32)


def lane_ids(lanes):
    return lax.broadcasted_iota(jnp.int32, (1, lanes), 1)


def spectrum_kernel(tiles, fq_blocks, direction_ref, noise_ref, table_ref, out_ref):
    cols, sensors, steps = direction_ref.shape
    lanes = table_ref.shape[1]
    weighted = (noise_ref[...][None] * direction_ref[...]).reshape(cols * sensors, steps)
    full = jnp.dot(weighted, table_ref[...], precision=HIGHEST, preferred_element_type=F32)
    col_of = lane_ids(lanes) % cols
    spec = full[0:sensors]
    for col in range(1, cols):
        spec = jnp.where(col_of == col, full[col * sensors : (col + 1) * sensors], spec)
    spec = spec.astype(BF16)
    block = lanes // fq_blocks
    for b in range(fq_blocks):
        part = spec[:, b * block : (b + 1) * block]
        out_ref[:, b] = jnp.broadcast_to(part[None], (tiles, sensors, block))


def adjoint_kernel(
    freqs, cols, spectra_ref, spec_ref, class_ref, out_ref, low_ref, high_ref, ends_ref, held, sems
):
    _, _, cells_x, cells_y, all_sensors = spectra_ref.shape
    cells = cells_x * cells_y
    stride = out_ref.shape[2] // cells_x
    lanes = spec_ref.shape[1] * spec_ref.shape[3]

    def fetch(f):
        return pltpu.make_async_copy(spectra_ref.at[f], held.at[f], sems.at[f])

    @pl.when(pl.program_id(0) == 0)
    def _():
        for f in range(freqs):
            fetch(f).start()

    parts = [
        spec_ref[:, b].reshape(all_sensors, spec_ref.shape[3]) for b in range(spec_ref.shape[1])
    ]
    direct = jnp.concatenate(parts, axis=1)
    wide = direct.astype(F32)
    is_real = (lane_ids(lanes) // cols) % 2 == 0
    turned = jnp.where(
        is_real, pltpu.roll(wide, lanes - cols, 1), -pltpu.roll(wide, cols, 1)
    ).astype(BF16)
    stacked = jnp.concatenate([direct, turned], axis=0)
    freq_of = (lane_ids(lanes) // (2 * cols)) % freqs

    row = lax.broadcasted_iota(jnp.int32, (cells, cells_x), 0)
    pick = (row // cells_y == lax.broadcasted_iota(jnp.int32, (cells, cells_x), 1)).astype(F32)
    by_row = jnp.dot(pick, class_ref[...].astype(F32) + 1.0, preferred_element_type=F32)
    at = lax.broadcasted_iota(jnp.int32, (cells, cells_y), 0) % cells_y
    own = (at == lax.broadcasted_iota(jnp.int32, (cells, cells_y), 1)).astype(F32)
    classes = jnp.dot(
        by_row * own, jnp.ones((cells_y, LANES), F32), preferred_element_type=F32
    )

    acc = None
    for f in range(freqs):

        @pl.when(pl.program_id(0) == 0)
        def _():
            fetch(f).wait()

        both = held[f].reshape(2, cells, all_sensors)
        both = jnp.concatenate([both[0], both[1]], axis=1)
        got = jnp.dot(both, stacked, preferred_element_type=F32)
        acc = got if acc is None else jnp.where(freq_of == f, got, acc)
    for k in range(out_ref.shape[1]):
        part = classes if k * LANES == lanes else acc[:, k * LANES : (k + 1) * LANES]
        for x in range(cells_x):
            base = x * stride
            out_ref[0, k, base : base + cells_y] = part[x * cells_y : (x + 1) * cells_y]
            out_ref[0, k, base + cells_y : base + stride] = jnp.zeros((stride - cells_y, LANES), F32)
        at = slice(k * LANES, (k + 1) * LANES)
        for j in range(DEPTH):
            low = out_ref[0, k, pl.ds(j, cells_x, stride=stride), :]
            high = out_ref[0, k, pl.ds(cells_y - DEPTH + j, cells_x, stride=stride), :]
            low_ref[0, j * cells_x : (j + 1) * cells_x, at] = low.astype(BF16)
            high_ref[0, j * cells_x : (j + 1) * cells_x, at] = high.astype(BF16)
        ends_ref[0, 0, :, at] = out_ref[0, k, 0 : DEPTH * stride]
        ends_ref[0, 1, :, at] = out_ref[0, k, (cells_x - DEPTH) * stride : cells_x * stride]


def ends_kernel(ends_ref, before_ref, after_ref, top_ref, bottom_ref, held):
    span = ends_ref.shape[2]
    stride = span // DEPTH
    cells_x = before_ref.shape[1] // DEPTH
    cells_y = stride - 8
    before = before_ref[0].astype(F32)
    after = after_ref[0].astype(F32)
    for side, out in ((0, top_ref), (1, bottom_ref)):
        held[...] = jnp.zeros_like(held)
        held[8 : 8 + span] = ends_ref[0, side]
        first = 0 if side == 0 else cells_x - DEPTH
        for x in range(DEPTH):
            for j in range(DEPTH):
                take = j * cells_x + first + x
                to = 8 + x * stride
                held[to + cells_y + j : to + cells_y + j + 1] = after[take : take + 1]
                held[to - DEPTH + j : to - DEPTH + j + 1] = before[take : take + 1]
        out[0] = held[8 - DEPTH : 8 - DEPTH + span].astype(BF16)


def field_kernel(
    freqs,
    cols,
    spectra_ref,
    source_ref,
    before_ref,
    after_ref,
    above_ref,
    below_ref,
    kappa_ref,
    out_ref,
    held,
    sems,
    wide,
    gain,
    one,
    two,
    sums,
):
    _, _, cells_x, cells_y, all_sensors = spectra_ref.shape
    cells = cells_x * cells_y
    stride = source_ref.shape[2] // cells_x
    slabs = one.shape[0]
    lanes = slabs * LANES
    start = (DEPTH + 1) * stride
    rows = cells_x * stride
    span = DEPTH * stride

    def fetch(f):
        return pltpu.make_async_copy(spectra_ref.at[f], held.at[f], sems.at[f])

    @pl.when(pl.program_id(0) == 0)
    def _():
        for f in range(freqs):
            fetch(f).start()

    total = wide.shape[1]
    lo, hi = start - span - 8, start + rows + span
    for k in range(slabs + 1):
        at = slice(k * LANES, (k + 1) * LANES)
        wide[k, 0:start] = jnp.zeros((start, LANES), F32)
        wide[k, start + rows : total] = jnp.zeros((total - start - rows, LANES), F32)
        wide[k, start : start + rows] = source_ref[0, k]
        before = before_ref[0, :, at].astype(F32)
        after = after_ref[0, :, at].astype(F32)
        for j in range(DEPTH):
            part = slice(j * cells_x, (j + 1) * cells_x)
            wide[k, pl.ds(start + cells_y + j, cells_x, stride=stride), :] = after[part]
            wide[k, pl.ds(start - DEPTH + j, cells_x, stride=stride), :] = before[part]
        wide[k, start - span - DEPTH : start - DEPTH] = above_ref[0, :, at].astype(F32)
        wide[k, start + rows - DEPTH : start + rows + span - DEPTH] = below_ref[0, :, at].astype(F32)

    classes = wide[slabs, lo:hi]
    kappa = jnp.zeros_like(classes)
    for n in range(kappa_ref.shape[0]):
        kappa = jnp.where(classes == n + 1.0, kappa_ref[n], kappa)
    scale = jnp.where(classes > 0.0, 1.0 / (1.0 + 4.0 * kappa), 0.0)
    gain[lo:hi] = kappa * scale

    def sweep(k, old, new, margin):
        first = start - margin * stride - 8
        last = start + rows + margin * stride
        near = (
            old[k, first - stride : last - stride]
            + old[k, first + stride : last + stride]
            + old[k, first - 1 : last - 1]
            + old[k, first + 1 : last + 1]
        )
        new[k, first:last] = wide[k, first:last] + gain[first:last] * near

    turned = []
    for k in range(slabs):
        wide[k, lo:hi] = wide[k, lo:hi] * scale
        one[k] = wide[k]
        old, new = one, two
        for margin in range(DEPTH - 1, -1, -1):
            sweep(k, old, new, margin)
            old, new = new, old
        field = old[k, start : start + rows].reshape(cells_x, stride, LANES)[:, 0:cells_y]
        turned.append(field.reshape(cells, LANES).T)
    turned = jnp.concatenate(turned, axis=0)
    blocks = lanes // (2 * cols)
    pair = turned.reshape(blocks, 2, cols, cells)
    plain = pair.astype(BF16).reshape(blocks, 2 * cols, cells)
    crossed = jnp.stack([-pair[:, 1], pair[:, 0]], axis=1)
    crossed = crossed.astype(BF16).reshape(blocks, 2 * cols, cells)
    groups = blocks // freqs
    for f in range(freqs):

        @pl.when(pl.program_id(0) == 0)
        def _():
            fetch(f).wait()

        ours = [
            jnp.concatenate([plain[g * freqs + f], crossed[g * freqs + f]], axis=1)
            for g in range(groups)
        ]
        left = jnp.concatenate(ours, axis=0)
        got = jnp.dot(
            left, held[f].reshape(2 * cells, all_sensors), preferred_element_type=F32
        )
        for g in range(groups):
            at = (g * freqs + f) * 2 * cols
            sums[at : at + 2 * cols] = got[g * 2 * cols : (g + 1) * 2 * cols]
    back = sums[...].T.astype(BF16)
    tiles, _, sensors, block = out_ref.shape
    for g in range(groups):
        out_ref[:, g] = back[:, g * block : (g + 1) * block].reshape(tiles, sensors, block)


def residual_kernel(
    terms_ref,
    table_ref,
    noise_ref,
    solution_ref,
    residual_ref,
    direction_ref,
    step_ref,
    new_solution_ref,
    new_residual_ref,
    norm_ref,
):
    cols, sensors, steps = direction_ref.shape
    parts = []
    for b in range(terms_ref.shape[1]):
        parts.append(jnp.sum(terms_ref[:, b].astype(F32), axis=0))
    spectrum = jnp.concatenate(parts, axis=1)
    col_of = lane_ids(spectrum.shape[1]) % cols
    left = jnp.concatenate([jnp.where(col_of == c, spectrum, 0.0) for c in range(cols)], axis=0)
    returned = jnp.dot(left, table_ref[...], precision=HIGHEST, preferred_element_type=F32)
    for c in range(cols):
        direction = direction_ref[c]
        product = direction + noise_ref[...] * returned[c * sensors : (c + 1) * sensors]
        new_solution_ref[c] = solution_ref[c] + step_ref[c] * direction
        new_residual = residual_ref[c] - step_ref[c] * product
        new_residual_ref[c] = new_residual
        norm_ref[c : c + 1] = jnp.sum(
            jnp.sum(new_residual * new_residual, axis=0, keepdims=True), axis=1, keepdims=True
        ) + jnp.zeros((1, norm_ref.shape[1]), F32)


def direction_kernel(norms_ref, residual_ref, direction_ref, old_ref, out_ref, norm_ref):
    cols, sensors, steps = direction_ref.shape
    norm = jnp.sum(norms_ref[...], axis=0)
    for c in range(cols):
        out_ref[c] = residual_ref[c] + (norm[c : c + 1, 0:1] / old_ref[c]) * direction_ref[c]
        norm_ref[c] = jnp.max(norm[c : c + 1])


def swap(axis, toward_partner, toward_other):
    count = lax.axis_size(axis)
    near = [(i, i ^ 1) for i in range(count) if (i ^ 1) < count]
    far = [(i, i + 1 if i % 2 else i - 1) for i in range(1, count - 1 + count % 2)]
    second = lax.ppermute(toward_other, axis, far)
    first = lax.ppermute(toward_partner, axis, near)
    return first, second


def exchange(axis, low, high):
    even = lax.axis_index(axis) % 2 == 0
    first, second = swap(axis, jnp.where(even, high, low), jnp.where(even, low, high))
    return jnp.where(even, second, first), jnp.where(even, first, second)


def on_device(
    spectra,
    noise_weight,
    class_map,
    class_kappa,
    solution,
    residual,
    direction,
    step_length,
    old_norm,
):
    local_freqs, _, cells_x, cells_y, all_sensors = spectra.shape
    cols, sensors, steps = direction.shape
    fq_blocks = lax.axis_size("fq")
    tiles = lax.axis_size("sx") * lax.axis_size("sy")
    block = 2 * local_freqs * cols
    lanes = block * fq_blocks
    forward, inverse = tables(local_freqs * fq_blocks, local_freqs, cols, steps)
    group = 2 if fq_blocks % 2 == 0 else 1
    chunks = fq_blocks // group
    width = group * block
    stride = cells_y + 8
    wide = width + LANES
    cells = cells_x * cells_y

    spec = pl.pallas_call(
        functools.partial(spectrum_kernel, tiles, fq_blocks),
        out_shape=jax.ShapeDtypeStruct((tiles, fq_blocks, sensors, block), BF16),
        in_specs=[VMEM] * 3,
        out_specs=VMEM,
        compiler_params=params(),
        name="spectrum",
    )(direction, noise_weight, forward)
    spec = lax.all_to_all(
        spec.reshape(tiles * fq_blocks, sensors, block), ALL_AXES, 0, 0, tiled=True
    ).reshape(tiles, fq_blocks, sensors, block)

    def chunked(*shape):
        return pl.BlockSpec((1,) + shape, lambda i: (i,) + (0,) * len(shape))

    by_block = pl.BlockSpec((tiles, group, sensors, block), lambda i: (0, i, 0, 0))
    held = [
        pltpu.VMEM((local_freqs, 2, cells_x, cells_y, all_sensors), BF16),
        pltpu.SemaphoreType.DMA((local_freqs,)),
    ]
    source, low, high, ends = pl.pallas_call(
        functools.partial(adjoint_kernel, local_freqs, cols),
        grid=(chunks,),
        out_shape=(
            jax.ShapeDtypeStruct((chunks, wide // LANES, cells_x * stride, LANES), F32),
            jax.ShapeDtypeStruct((chunks, DEPTH * cells_x, wide), BF16),
            jax.ShapeDtypeStruct((chunks, DEPTH * cells_x, wide), BF16),
            jax.ShapeDtypeStruct((chunks, 2, DEPTH * stride, wide), F32),
        ),
        in_specs=[ANY, by_block, pl.BlockSpec((cells_x, cells_y), lambda i: (0, 0))],
        out_specs=(
            chunked(wide // LANES, cells_x * stride, LANES),
            chunked(DEPTH * cells_x, wide),
            chunked(DEPTH * cells_x, wide),
            chunked(2, DEPTH * stride, wide),
        ),
        scratch_shapes=held,
        compiler_params=params(),
        name="adjoint",
    )(spectra, spec, class_map)
    before, after = exchange("sy", low, high)
    top, bottom = pl.pallas_call(
        ends_kernel,
        grid=(chunks,),
        out_shape=(jax.ShapeDtypeStruct((chunks, DEPTH * stride, wide), BF16),) * 2,
        in_specs=[
            chunked(2, DEPTH * stride, wide),
            chunked(DEPTH * cells_x, wide),
            chunked(DEPTH * cells_x, wide),
        ],
        out_specs=(chunked(DEPTH * stride, wide),) * 2,
        scratch_shapes=[pltpu.VMEM((DEPTH * stride + 16, wide), F32)],
        compiler_params=params(),
        name="ends",
    )(ends, before, after)
    above, below = exchange("sx", top, bottom)
    total = (cells_x + 2 * DEPTH + 2) * stride
    terms = pl.pallas_call(
        functools.partial(field_kernel, local_freqs, cols),
        grid=(chunks,),
        out_shape=jax.ShapeDtypeStruct((tiles, fq_blocks, sensors, block), BF16),
        in_specs=[
            ANY,
            chunked(wide // LANES, cells_x * stride, LANES),
            chunked(DEPTH * cells_x, wide),
            chunked(DEPTH * cells_x, wide),
            chunked(DEPTH * stride, wide),
            chunked(DEPTH * stride, wide),
            SMEM,
        ],
        out_specs=by_block,
        scratch_shapes=held
        + [
            pltpu.VMEM((wide // LANES, total, LANES), F32),
            pltpu.VMEM((total, LANES), F32),
            pltpu.VMEM((width // LANES, total, LANES), F32),
            pltpu.VMEM((width // LANES, total, LANES), F32),
            pltpu.VMEM((width, all_sensors), F32),
        ],
        compiler_params=params(),
        name="field",
    )(spectra, source, before, after, above, below, class_kappa)
    terms = lax.all_to_all(
        terms.reshape(tiles * fq_blocks, sensors, block), ALL_AXES, 0, 0, tiled=True
    ).reshape(tiles, fq_blocks, sensors, block)
    held_shape = jax.ShapeDtypeStruct(direction.shape, F32)
    new_solution, new_residual, norm = pl.pallas_call(
        residual_kernel,
        out_shape=(held_shape, held_shape, jax.ShapeDtypeStruct((cols, 128), F32)),
        in_specs=[VMEM] * 6 + [SMEM],
        out_specs=(VMEM,) * 3,
        compiler_params=params(),
        name="residual",
    )(terms, inverse, noise_weight, solution, residual, direction, step_length)
    norms = lax.all_to_all(
        jnp.broadcast_to(norm[None], (tiles, cols, 128)), GRID_AXES, 0, 0, tiled=True
    )
    new_direction, new_norm = pl.pallas_call(
        direction_kernel,
        out_shape=(held_shape, jax.ShapeDtypeStruct((cols,), F32)),
        in_specs=[VMEM] * 3 + [SMEM],
        out_specs=(VMEM, SMEM),
        compiler_params=params(),
        name="direction",
    )(norms, new_residual, direction, old_norm)
    return (new_solution, new_residual, new_direction, new_norm)


def solution(mesh):
    return jax.shard_map(
        on_device,
        mesh=mesh,
        in_specs=(
            P("fq", None, "sx", "sy", None),
            P(("sx", "sy"), None),
            P("sx", "sy"),
            P(),
            P("fq", ("sx", "sy"), None),
            P("fq", ("sx", "sy"), None),
            P("fq", ("sx", "sy"), None),
            P("fq"),
            P("fq"),
        ),
        out_specs=(
            P("fq", ("sx", "sy"), None),
            P("fq", ("sx", "sy"), None),
            P("fq", ("sx", "sy"), None),
            P("fq"),
        ),
        check_vma=False,
    )
```

```python
import functools
import math

import jax
import jax.numpy as jnp
from jax import lax
from jax.experimental import pallas as pl
from jax.experimental.pallas import tpu as pltpu
from jax.sharding import PartitionSpec as P
import numpy as np

SWEEPS = 4
DEPTH = SWEEPS - 1
HIGHEST = lax.Precision.HIGHEST
F32 = jnp.float32
BF16 = jnp.bfloat16
GRID_AXES = ("sx", "sy")
ALL_AXES = ("sx", "sy", "fq")
LANES = 128
MIB = 1024 * 1024
VMEM = pl.BlockSpec(memory_space=pltpu.VMEM)
SMEM = pl.BlockSpec(memory_space=pltpu.SMEM)
HBM = pl.BlockSpec(memory_space=pltpu.HBM)


def params(mib=24):
    return pltpu.CompilerParams(vmem_limit_bytes=mib * MIB)


def tables(freq_count, local_freqs, local_cols, time_steps):
    freq = np.arange(freq_count)[:, None]
    step = np.arange(time_steps)[None, :]
    phases = (freq * step % time_steps) * (2.0 * math.pi / time_steps)
    factor = 1.0 / math.sqrt(time_steps)
    pair = np.stack([np.cos(phases) * factor, -np.sin(phases) * factor], 1)
    forward = np.repeat(pair.reshape(2 * freq_count, time_steps), local_cols, 0)
    doubling = np.where(np.arange(freq_count) == 0, 1.0, 2.0)[:, None, None]
    inverse = np.repeat((pair * doubling).reshape(2 * freq_count, time_steps), local_cols, 0)
    return forward.T.astype(np.float32), inverse.astype(np.float32)


def by_side(axis, low, high):
    even = lax.axis_index(axis) % 2 == 0
    return jnp.where(even, high, low), jnp.where(even, low, high)


def lane_ids(lanes):
    return lax.broadcasted_iota(jnp.int32, (1, lanes), 1)


def fetch_all(pairs, sems):
    copies = [pltpu.make_async_copy(a, b, sems.at[i]) for i, (a, b) in enumerate(pairs)]
    for copy in copies:
        copy.start()
    for copy in copies:
        copy.wait()


def spectrum_kernel(
    tiles, fq_blocks, direction_in, noise_in, table_in, out_ref, direction_ref, noise_ref, table_ref, sems
):
    fetch_all(
        ((direction_in, direction_ref), (noise_in, noise_ref), (table_in, table_ref)), sems
    )
    cols, sensors, steps = direction_ref.shape
    lanes = table_ref.shape[1]
    weighted = (noise_ref[...][None] * direction_ref[...]).reshape(cols * sensors, steps)
    full = jnp.dot(weighted, table_ref[...], precision=HIGHEST, preferred_element_type=F32)
    col_of = lane_ids(lanes) % cols
    spec = full[0:sensors]
    for col in range(1, cols):
        spec = jnp.where(col_of == col, full[col * sensors : (col + 1) * sensors], spec)
    spec = spec.astype(BF16)
    block = lanes // fq_blocks
    for b in range(fq_blocks):
        part = spec[:, b * block : (b + 1) * block]
        out_ref[:, b] = jnp.broadcast_to(part[None], (tiles, sensors, block))


def class_rows(class_ref):
    cells_y, cells_x = class_ref.shape
    cells = cells_x * cells_y
    row = lax.broadcasted_iota(jnp.int32, (cells, cells_x), 0)
    pick = (row // cells_y == lax.broadcasted_iota(jnp.int32, (cells, cells_x), 1)).astype(F32)
    by_row = lax.dot_general(
        pick,
        class_ref[...].astype(F32) + 1.0,
        (((1,), (1,)), ((), ())),
        preferred_element_type=F32,
    )
    at = lax.broadcasted_iota(jnp.int32, (cells, cells_y), 0) % cells_y
    own = (at == lax.broadcasted_iota(jnp.int32, (cells, cells_y), 1)).astype(F32)
    return jnp.dot(by_row * own, jnp.ones((cells_y, LANES), F32), preferred_element_type=F32)


def adjoint_kernel(
    freqs, cols, spectra_ref, spec_ref, class_ref, out_ref, near_ref, far_ref, ends_ref
):
    _, _, cells_x, cells_y, all_sensors = spectra_ref.shape
    cells = cells_x * cells_y
    stride = out_ref.shape[1] // cells_x
    lanes = spec_ref.shape[1] * spec_ref.shape[3]

    parts = [
        spec_ref[:, b].reshape(all_sensors, spec_ref.shape[3]) for b in range(spec_ref.shape[1])
    ]
    direct = jnp.concatenate(parts, axis=1)
    wide = direct.astype(F32)
    is_real = (lane_ids(lanes) // cols) % 2 == 0
    turned = jnp.where(
        is_real, pltpu.roll(wide, lanes - cols, 1), -pltpu.roll(wide, cols, 1)
    ).astype(BF16)
    stacked = jnp.concatenate([direct, turned], axis=0)
    freq_of = (lane_ids(lanes) // (2 * cols)) % freqs

    classes = class_rows(class_ref)
    acc = None
    for f in range(freqs):
        both = spectra_ref[f].reshape(2, cells, all_sensors)
        both = jnp.concatenate([both[0], both[1]], axis=1)
        got = jnp.dot(both, stacked, preferred_element_type=F32)
        acc = got if acc is None else jnp.where(freq_of == f, got, acc)
    for k in range(out_ref.shape[0]):
        part = classes if k * LANES == lanes else acc[:, k * LANES : (k + 1) * LANES]
        for x in range(cells_x):
            base = x * stride
            out_ref[k, base : base + cells_y] = part[x * cells_y : (x + 1) * cells_y]
            out_ref[k, base + cells_y : base + stride] = jnp.zeros((stride - cells_y, LANES), F32)
        at = slice(k * LANES, (k + 1) * LANES)
        for j in range(DEPTH):
            low = out_ref[k, pl.ds(j, cells_x, stride=stride), :]
            high = out_ref[k, pl.ds(cells_y - DEPTH + j, cells_x, stride=stride), :]
            near, far = by_side("sy", low, high)
            near_ref[j * cells_x : (j + 1) * cells_x, at] = near.astype(BF16)
            far_ref[j * cells_x : (j + 1) * cells_x, at] = far.astype(BF16)
        ends_ref[0, :, at] = out_ref[k, 0 : DEPTH * stride]
        ends_ref[1, :, at] = out_ref[k, (cells_x - DEPTH) * stride : cells_x * stride]


def ends_kernel(ends_ref, near_ref, far_ref, near_out, far_out, held):
    span = ends_ref.shape[1]
    stride = span // DEPTH
    cells_x = near_ref.shape[0] // DEPTH
    cells_y = stride - 8
    after, before = by_side("sy", far_ref[...].astype(F32), near_ref[...].astype(F32))
    built = []
    for side in range(2):
        held[...] = jnp.zeros_like(held)
        held[8 : 8 + span] = ends_ref[side]
        first = 0 if side == 0 else cells_x - DEPTH
        for x in range(DEPTH):
            for j in range(DEPTH):
                take = j * cells_x + first + x
                to = 8 + x * stride
                held[to + cells_y + j : to + cells_y + j + 1] = after[take : take + 1]
                held[to - DEPTH + j : to - DEPTH + j + 1] = before[take : take + 1]
        built.append(held[8 - DEPTH : 8 - DEPTH + span])
    near, far = by_side("sx", built[0], built[1])
    near_out[...] = near.astype(BF16)
    far_out[...] = far.astype(BF16)


def field_kernel(
    freqs,
    cols,
    spectra_ref,
    source_ref,
    near_y_ref,
    far_y_ref,
    near_x_ref,
    far_x_ref,
    kappa_ref,
    out_ref,
    wide,
    gain,
    one,
    two,
    sums,
):
    _, _, cells_x, cells_y, all_sensors = spectra_ref.shape
    cells = cells_x * cells_y
    stride = source_ref.shape[1] // cells_x
    slabs = one.shape[0]
    lanes = slabs * LANES
    start = (DEPTH + 1) * stride
    rows = cells_x * stride
    span = DEPTH * stride

    total = wide.shape[1]
    lo, hi = start - span - 8, start + rows + span
    for k in range(slabs + 1):
        at = slice(k * LANES, (k + 1) * LANES)
        wide[k, 0:start] = jnp.zeros((start, LANES), F32)
        wide[k, start + rows : total] = jnp.zeros((total - start - rows, LANES), F32)
        wide[k, start : start + rows] = source_ref[k]
        after, before = by_side("sy", far_y_ref[:, at].astype(F32), near_y_ref[:, at].astype(F32))
        below, above = by_side("sx", far_x_ref[:, at].astype(F32), near_x_ref[:, at].astype(F32))
        for j in range(DEPTH):
            part = slice(j * cells_x, (j + 1) * cells_x)
            wide[k, pl.ds(start + cells_y + j, cells_x, stride=stride), :] = after[part]
            wide[k, pl.ds(start - DEPTH + j, cells_x, stride=stride), :] = before[part]
        wide[k, start - span - DEPTH : start - DEPTH] = above
        wide[k, start + rows - DEPTH : start + rows + span - DEPTH] = below

    classes = wide[slabs, lo:hi]
    kappa = jnp.zeros_like(classes)
    for n in range(kappa_ref.shape[0]):
        kappa = jnp.where(classes == n + 1.0, kappa_ref[n], kappa)
    scale = jnp.where(classes > 0.0, 1.0 / (1.0 + 4.0 * kappa), 0.0)
    gain[lo:hi] = kappa * scale

    def sweep(k, old, new, margin):
        first = start - margin * stride - 8
        last = start + rows + margin * stride
        near = (
            old[k, first - stride : last - stride]
            + old[k, first + stride : last + stride]
            + old[k, first - 1 : last - 1]
            + old[k, first + 1 : last + 1]
        )
        new[k, first:last] = wide[k, first:last] + gain[first:last] * near

    turned = []
    for k in range(slabs):
        wide[k, lo:hi] = wide[k, lo:hi] * scale
        one[k] = wide[k]
        old, new = one, two
        for margin in range(DEPTH - 1, -1, -1):
            sweep(k, old, new, margin)
            old, new = new, old
        field = old[k, start : start + rows].reshape(cells_x, stride, LANES)[:, 0:cells_y]
        turned.append(field.reshape(cells, LANES).T)
    turned = jnp.concatenate(turned, axis=0)
    blocks = lanes // (2 * cols)
    pair = turned.reshape(blocks, 2, cols, cells)
    plain = pair.astype(BF16).reshape(blocks, 2 * cols, cells)
    crossed = jnp.stack([-pair[:, 1], pair[:, 0]], axis=1)
    crossed = crossed.astype(BF16).reshape(blocks, 2 * cols, cells)
    groups = blocks // freqs
    for f in range(freqs):
        ours = [
            jnp.concatenate([plain[g * freqs + f], crossed[g * freqs + f]], axis=1)
            for g in range(groups)
        ]
        left = jnp.concatenate(ours, axis=0)
        got = jnp.dot(
            left, spectra_ref[f].reshape(2 * cells, all_sensors), preferred_element_type=F32
        )
        for g in range(groups):
            at = (g * freqs + f) * 2 * cols
            sums[at : at + 2 * cols] = got[g * 2 * cols : (g + 1) * 2 * cols]
    back = sums[...].T.astype(BF16)
    tiles, _, sensors, block = out_ref.shape
    for g in range(groups):
        out_ref[:, g] = back[:, g * block : (g + 1) * block].reshape(tiles, sensors, block)


def solution_kernel(solution_in, direction_in, step_ref, out_ref, solution_ref, direction_ref, sems):
    fetch_all(((solution_in, solution_ref), (direction_in, direction_ref)), sems)
    for c in range(solution_ref.shape[0]):
        out_ref[c] = solution_ref[c] + step_ref[c] * direction_ref[c]


def residual_kernel(
    terms_ref, table_ref, noise_ref, residual_ref, direction_ref, step_ref, new_residual_ref, norm_ref
):
    cols, sensors, steps = direction_ref.shape
    parts = []
    for b in range(terms_ref.shape[1]):
        parts.append(jnp.sum(terms_ref[:, b].astype(F32), axis=0))
    spectrum = jnp.concatenate(parts, axis=1)
    col_of = lane_ids(spectrum.shape[1]) % cols
    left = jnp.concatenate([jnp.where(col_of == c, spectrum, 0.0) for c in range(cols)], axis=0)
    returned = jnp.dot(left, table_ref[...], precision=HIGHEST, preferred_element_type=F32)
    for c in range(cols):
        product = direction_ref[c] + noise_ref[...] * returned[c * sensors : (c + 1) * sensors]
        new_residual = residual_ref[c] - step_ref[c] * product
        new_residual_ref[c] = new_residual
        norm = jnp.sum(
            jnp.sum(new_residual * new_residual, axis=0, keepdims=True), axis=1, keepdims=True
        )
        norm_ref[:, c : c + 1] = jnp.broadcast_to(norm[None], (norm_ref.shape[0], 1, LANES))


def direction_kernel(
    norms_ref, residual_ref, direction_ref, old_ref, residual_out, direction_out, norm_ref, held, sems
):
    cols, sensors, steps = direction_ref.shape
    first = pltpu.make_async_copy(residual_ref, residual_out, sems.at[0])
    first.start()
    norm = jnp.sum(norms_ref[...], axis=0)
    for c in range(cols):
        held[c] = residual_ref[c] + (norm[c : c + 1, 0:1] / old_ref[c]) * direction_ref[c]
    second = pltpu.make_async_copy(held, direction_out, sems.at[1])
    second.start()
    for c in range(cols):
        norm_ref[c] = jnp.max(norm[c : c + 1])
    first.wait()
    second.wait()


def swap(axis, toward_partner, toward_other):
    count = lax.axis_size(axis)
    near = [(i, i ^ 1) for i in range(count) if (i ^ 1) < count]
    far = [(i, i + 1 if i % 2 else i - 1) for i in range(1, count - 1 + count % 2)]
    second = lax.ppermute(toward_other, axis, far)
    first = lax.ppermute(toward_partner, axis, near)
    return first, second


def on_device(
    spectra,
    noise_weight,
    class_map,
    class_kappa,
    solution,
    residual,
    direction,
    step_length,
    old_norm,
):
    local_freqs, _, cells_x, cells_y, all_sensors = spectra.shape
    cols, sensors, steps = direction.shape
    fq_blocks = lax.axis_size("fq")
    tiles = lax.axis_size("sx") * lax.axis_size("sy")
    block = 2 * local_freqs * cols
    lanes = block * fq_blocks
    forward, inverse = tables(local_freqs * fq_blocks, local_freqs, cols, steps)
    group = 2 if fq_blocks % 2 == 0 else 1
    chunks = fq_blocks // group
    width = group * block
    stride = cells_y + 8
    wide = width + LANES
    cells = cells_x * cells_y

    like = jax.ShapeDtypeStruct(direction.shape, F32)
    held = pltpu.VMEM(direction.shape, F32)
    spec = pl.pallas_call(
        functools.partial(spectrum_kernel, tiles, fq_blocks),
        out_shape=jax.ShapeDtypeStruct((tiles, fq_blocks, sensors, block), BF16),
        in_specs=[HBM] * 3,
        out_specs=VMEM,
        scratch_shapes=[
            held,
            pltpu.VMEM(noise_weight.shape, F32),
            pltpu.VMEM(forward.shape, F32),
            pltpu.SemaphoreType.DMA((3,)),
        ],
        compiler_params=params(62),
        cost_estimate=pl.CostEstimate(
            flops=2 * spectra.size, bytes_accessed=4 * spectra.size, transcendentals=0
        ),
        name="spectrum",
    )(direction, noise_weight, forward)
    spec = lax.all_to_all(
        spec.reshape(tiles * fq_blocks, sensors, block), ALL_AXES, 0, 0, tiled=True
    ).reshape(tiles, fq_blocks, sensors, block)
    new_solution = pl.pallas_call(
        solution_kernel,
        out_shape=like,
        in_specs=[HBM, HBM, SMEM],
        out_specs=VMEM,
        scratch_shapes=[held, held, pltpu.SemaphoreType.DMA((2,))],
        compiler_params=params(),
        name="solution",
    )(solution, direction, step_length)

    edge = jax.ShapeDtypeStruct((DEPTH * cells_x, wide), BF16)
    end = jax.ShapeDtypeStruct((DEPTH * stride, wide), BF16)
    total = (cells_x + 2 * DEPTH + 2) * stride
    slabs = width // LANES
    pieces = []
    for i in range(chunks):
        source, near_y, far_y, ends = pl.pallas_call(
            functools.partial(adjoint_kernel, local_freqs, cols),
            out_shape=(
                jax.ShapeDtypeStruct((slabs + 1, cells_x * stride, LANES), F32),
                edge,
                edge,
                jax.ShapeDtypeStruct((2, DEPTH * stride, wide), F32),
            ),
            in_specs=[VMEM] * 3,
            out_specs=(VMEM,) * 4,
            compiler_params=params(),
            name="adjoint",
        )(spectra, spec[:, i * group : (i + 1) * group], class_map.T)
        near_y, far_y = swap("sy", near_y, far_y)
        near_x, far_x = pl.pallas_call(
            ends_kernel,
            out_shape=(end, end),
            in_specs=[VMEM] * 3,
            out_specs=(VMEM,) * 2,
            scratch_shapes=[pltpu.VMEM((DEPTH * stride + 16, wide), F32)],
            compiler_params=params(),
            name="ends",
        )(ends, near_y, far_y)
        near_x, far_x = swap("sx", near_x, far_x)
        pieces.append(
            pl.pallas_call(
                functools.partial(field_kernel, local_freqs, cols),
                out_shape=jax.ShapeDtypeStruct((tiles, group, sensors, block), BF16),
                in_specs=[VMEM] * 6 + [SMEM],
                out_specs=VMEM,
                scratch_shapes=[
                    pltpu.VMEM((slabs + 1, total, LANES), F32),
                    pltpu.VMEM((total, LANES), F32),
                    pltpu.VMEM((slabs, total, LANES), F32),
                    pltpu.VMEM((slabs, total, LANES), F32),
                    pltpu.VMEM((width, all_sensors), F32),
                ],
                compiler_params=params(),
                name="field",
            )(spectra, source, near_y, far_y, near_x, far_x, class_kappa)
        )
    terms = jnp.concatenate(pieces, axis=1)
    terms = lax.all_to_all(
        terms.reshape(tiles * fq_blocks, sensors, block), ALL_AXES, 0, 0, tiled=True
    ).reshape(tiles, fq_blocks, sensors, block)
    new_residual, norms = pl.pallas_call(
        residual_kernel,
        out_shape=(like, jax.ShapeDtypeStruct((tiles, cols, LANES), F32)),
        in_specs=[VMEM] * 5 + [SMEM],
        out_specs=(VMEM,) * 2,
        compiler_params=params(),
        name="residual",
    )(terms, inverse, noise_weight, residual, direction, step_length)
    norms = lax.all_to_all(norms, GRID_AXES, 0, 0, tiled=True)
    new_residual, new_direction, new_norm = pl.pallas_call(
        direction_kernel,
        out_shape=(like, like, jax.ShapeDtypeStruct((cols,), F32)),
        in_specs=[VMEM] * 3 + [SMEM],
        out_specs=(HBM, HBM, SMEM),
        scratch_shapes=[held, pltpu.SemaphoreType.DMA((2,))],
        compiler_params=params(),
        name="direction",
    )(norms, new_residual, direction, old_norm)
    return (new_solution, new_residual, new_direction, new_norm)


def solution(mesh):
    return jax.shard_map(
        on_device,
        mesh=mesh,
        in_specs=(
            P("fq", None, "sx", "sy", None),
            P(("sx", "sy"), None),
            P("sx", "sy"),
            P(),
            P("fq", ("sx", "sy"), None),
            P("fq", ("sx", "sy"), None),
            P("fq", ("sx", "sy"), None),
            P("fq"),
            P("fq"),
        ),
        out_specs=(
            P("fq", ("sx", "sy"), None),
            P("fq", ("sx", "sy"), None),
            P("fq", ("sx", "sy"), None),
            P("fq"),
        ),
        check_vma=False,
    )
```

```python
import functools
import math

import jax
import jax.numpy as jnp
from jax import lax
from jax.experimental import pallas as pl
from jax.experimental.pallas import tpu as pltpu
from jax.sharding import PartitionSpec as P
import numpy as np

SWEEPS = 4
DEPTH = SWEEPS - 1
HIGHEST = lax.Precision.HIGHEST
F32 = jnp.float32
BF16 = jnp.bfloat16
GRID_AXES = ("sx", "sy")
ALL_AXES = ("sx", "sy", "fq")
LANES = 128
MIB = 1024 * 1024
VMEM = pl.BlockSpec(memory_space=pltpu.VMEM)
SMEM = pl.BlockSpec(memory_space=pltpu.SMEM)
HBM = pl.BlockSpec(memory_space=pltpu.HBM)


def params(mib=24):
    return pltpu.CompilerParams(vmem_limit_bytes=mib * MIB)


def tables(freq_count, local_freqs, local_cols, time_steps):
    freq = np.arange(freq_count)[:, None]
    step = np.arange(time_steps)[None, :]
    phases = (freq * step % time_steps) * (2.0 * math.pi / time_steps)
    factor = 1.0 / math.sqrt(time_steps)
    pair = np.stack([np.cos(phases) * factor, -np.sin(phases) * factor], 1)
    forward = np.repeat(pair.reshape(2 * freq_count, time_steps), local_cols, 0)
    doubling = np.where(np.arange(freq_count) == 0, 1.0, 2.0)[:, None, None]
    inverse = np.repeat((pair * doubling).reshape(2 * freq_count, time_steps), local_cols, 0)
    return forward.T.astype(np.float32), inverse.astype(np.float32)


def by_side(axis, low, high):
    even = lax.axis_index(axis) % 2 == 0
    return jnp.where(even, high, low), jnp.where(even, low, high)


def by_parity(axis, mine, other):
    even = lax.axis_index(axis) % 2 == 0
    return jnp.where(even, mine, other), jnp.where(even, other, mine)


def lane_ids(lanes):
    return lax.broadcasted_iota(jnp.int32, (1, lanes), 1)


def fetch_all(pairs, sems):
    copies = [pltpu.make_async_copy(a, b, sems.at[i]) for i, (a, b) in enumerate(pairs)]
    for copy in copies:
        copy.start()
    for copy in copies:
        copy.wait()


def spectrum_kernel(
    tiles, fq_blocks, direction_in, noise_in, table_in, out_ref, direction_ref, noise_ref, table_ref, sems
):
    fetch_all(
        ((direction_in, direction_ref), (noise_in, noise_ref), (table_in, table_ref)), sems
    )
    cols, sensors, steps = direction_ref.shape
    lanes = table_ref.shape[1]
    weighted = (noise_ref[...][None] * direction_ref[...]).reshape(cols * sensors, steps)
    full = jnp.dot(weighted, table_ref[...], precision=HIGHEST, preferred_element_type=F32)
    col_of = lane_ids(lanes) % cols
    spec = full[0:sensors]
    for col in range(1, cols):
        spec = jnp.where(col_of == col, full[col * sensors : (col + 1) * sensors], spec)
    spec = spec.astype(BF16)
    block = lanes // fq_blocks
    for b in range(fq_blocks):
        part = spec[:, b * block : (b + 1) * block]
        out_ref[:, b] = jnp.broadcast_to(part[None], (tiles, sensors, block))


def class_rows(class_ref):
    cells_y, cells_x = class_ref.shape
    cells = cells_x * cells_y
    row = lax.broadcasted_iota(jnp.int32, (cells, cells_x), 0)
    pick = (row // cells_y == lax.broadcasted_iota(jnp.int32, (cells, cells_x), 1)).astype(F32)
    by_row = lax.dot_general(
        pick,
        class_ref[...].astype(F32) + 1.0,
        (((1,), (1,)), ((), ())),
        preferred_element_type=F32,
    )
    at = lax.broadcasted_iota(jnp.int32, (cells, cells_y), 0) % cells_y
    own = (at == lax.broadcasted_iota(jnp.int32, (cells, cells_y), 1)).astype(F32)
    return jnp.dot(by_row * own, jnp.ones((cells_y, LANES), F32), preferred_element_type=F32)


def adjoint_of(part, stacked):
    _, cells_x, cells_y, all_sensors = part.shape
    both = part.reshape(2, cells_x * cells_y, all_sensors)
    both = jnp.concatenate([both[0], both[1]], axis=1)
    return jnp.dot(both, stacked, preferred_element_type=F32)


def freq_lanes(lanes, cols, freqs):
    return (lane_ids(lanes) // (2 * cols)) % freqs


def order_kernel(cols, spectra_in, mine_ref, other_ref, stacked_ref):
    halves, group, sensors, block = mine_ref.shape
    lanes = group * block
    parts = []
    for b in range(group):
        pair = by_parity("sy", mine_ref[:, b], other_ref[:, b])
        parts.append(jnp.stack(pair, axis=1).reshape(2 * halves * sensors, block))
    direct = jnp.concatenate(parts, axis=1)
    wide = direct.astype(F32)
    is_real = (lane_ids(lanes) // cols) % 2 == 0
    turned = jnp.where(
        is_real, pltpu.roll(wide, lanes - cols, 1), -pltpu.roll(wide, cols, 1)
    ).astype(BF16)
    stacked_ref[...] = jnp.concatenate([direct, turned], axis=0)


def adjoint_kernel(
    freqs, cols, spectra_ref, stacked_ref, class_ref, out_ref, near_ref, far_ref, ends_ref
):
    _, _, cells_x, cells_y, all_sensors = spectra_ref.shape
    stride = out_ref.shape[1] // cells_x
    lanes = stacked_ref.shape[1]
    freq_of = freq_lanes(lanes, cols, freqs)
    classes = class_rows(class_ref)
    stacked = stacked_ref[...]
    acc = adjoint_of(spectra_ref[0], stacked)
    for f in range(1, freqs):
        acc = jnp.where(freq_of == f, adjoint_of(spectra_ref[f], stacked), acc)
    for k in range(out_ref.shape[0]):
        part = classes if k * LANES == lanes else acc[:, k * LANES : (k + 1) * LANES]
        for x in range(cells_x):
            base = x * stride
            out_ref[k, base : base + cells_y] = part[x * cells_y : (x + 1) * cells_y]
            out_ref[k, base + cells_y : base + stride] = jnp.zeros((stride - cells_y, LANES), F32)
        at = slice(k * LANES, (k + 1) * LANES)
        for j in range(DEPTH):
            low = out_ref[k, pl.ds(j, cells_x, stride=stride), :]
            high = out_ref[k, pl.ds(cells_y - DEPTH + j, cells_x, stride=stride), :]
            near, far = by_side("sy", low, high)
            near_ref[j * cells_x : (j + 1) * cells_x, at] = near.astype(BF16)
            far_ref[j * cells_x : (j + 1) * cells_x, at] = far.astype(BF16)
        ends_ref[0, :, at] = out_ref[k, 0 : DEPTH * stride]
        ends_ref[1, :, at] = out_ref[k, (cells_x - DEPTH) * stride : cells_x * stride]


def ends_kernel(ends_ref, near_ref, far_ref, near_out, far_out, held):
    span = ends_ref.shape[1]
    stride = span // DEPTH
    cells_x = near_ref.shape[0] // DEPTH
    cells_y = stride - 8
    after, before = by_side("sy", far_ref[...].astype(F32), near_ref[...].astype(F32))
    built = []
    for side in range(2):
        held[...] = jnp.zeros_like(held)
        held[8 : 8 + span] = ends_ref[side]
        first = 0 if side == 0 else cells_x - DEPTH
        for x in range(DEPTH):
            for j in range(DEPTH):
                take = j * cells_x + first + x
                to = 8 + x * stride
                held[to + cells_y + j : to + cells_y + j + 1] = after[take : take + 1]
                held[to - DEPTH + j : to - DEPTH + j + 1] = before[take : take + 1]
        built.append(held[8 - DEPTH : 8 - DEPTH + span])
    near, far = by_side("sx", built[0], built[1])
    near_out[...] = near.astype(BF16)
    far_out[...] = far.astype(BF16)


def field_kernel(
    freqs,
    cols,
    spectra_ref,
    source_ref,
    near_y_ref,
    far_y_ref,
    near_x_ref,
    far_x_ref,
    kappa_ref,
    keep_ref,
    send_ref,
    wide,
    gain,
    one,
    two,
    sums,
):
    _, _, cells_x, cells_y, all_sensors = spectra_ref.shape
    cells = cells_x * cells_y
    stride = source_ref.shape[1] // cells_x
    slabs = one.shape[0]
    lanes = slabs * LANES
    start = (DEPTH + 1) * stride
    rows = cells_x * stride
    span = DEPTH * stride

    total = wide.shape[1]
    lo, hi = start - span - 8, start + rows + span
    for k in range(slabs + 1):
        at = slice(k * LANES, (k + 1) * LANES)
        wide[k, 0:start] = jnp.zeros((start, LANES), F32)
        wide[k, start + rows : total] = jnp.zeros((total - start - rows, LANES), F32)
        wide[k, start : start + rows] = source_ref[k]
        after, before = by_side("sy", far_y_ref[:, at].astype(F32), near_y_ref[:, at].astype(F32))
        below, above = by_side("sx", far_x_ref[:, at].astype(F32), near_x_ref[:, at].astype(F32))
        for j in range(DEPTH):
            part = slice(j * cells_x, (j + 1) * cells_x)
            wide[k, pl.ds(start + cells_y + j, cells_x, stride=stride), :] = after[part]
            wide[k, pl.ds(start - DEPTH + j, cells_x, stride=stride), :] = before[part]
        wide[k, start - span - DEPTH : start - DEPTH] = above
        wide[k, start + rows - DEPTH : start + rows + span - DEPTH] = below

    classes = wide[slabs, lo:hi]
    kappa = jnp.zeros_like(classes)
    for n in range(kappa_ref.shape[0]):
        kappa = jnp.where(classes == n + 1.0, kappa_ref[n], kappa)
    scale = jnp.where(classes > 0.0, 1.0 / (1.0 + 4.0 * kappa), 0.0)
    gain[lo:hi] = kappa * scale

    def sweep(k, old, new, margin):
        first = start - margin * stride - 8
        last = start + rows + margin * stride
        near = (
            old[k, first - stride : last - stride]
            + old[k, first + stride : last + stride]
            + old[k, first - 1 : last - 1]
            + old[k, first + 1 : last + 1]
        )
        new[k, first:last] = wide[k, first:last] + gain[first:last] * near

    turned = []
    for k in range(slabs):
        wide[k, lo:hi] = wide[k, lo:hi] * scale
        one[k] = wide[k]
        old, new = one, two
        for margin in range(DEPTH - 1, -1, -1):
            sweep(k, old, new, margin)
            old, new = new, old
        field = old[k, start : start + rows].reshape(cells_x, stride, LANES)[:, 0:cells_y]
        turned.append(field.reshape(cells, LANES).T)
    turned = jnp.concatenate(turned, axis=0)
    blocks = lanes // (2 * cols)
    pair = turned.reshape(blocks, 2, cols, cells)
    plain = pair.astype(BF16).reshape(blocks, 2 * cols, cells)
    crossed = jnp.stack([-pair[:, 1], pair[:, 0]], axis=1)
    crossed = crossed.astype(BF16).reshape(blocks, 2 * cols, cells)
    groups = blocks // freqs
    for f in range(freqs):
        ours = [
            jnp.concatenate([plain[g * freqs + f], crossed[g * freqs + f]], axis=1)
            for g in range(groups)
        ]
        left = jnp.concatenate(ours, axis=0)
        got = jnp.dot(
            left, spectra_ref[f].reshape(2 * cells, all_sensors), preferred_element_type=F32
        )
        for g in range(groups):
            at = (g * freqs + f) * 2 * cols
            sums[at : at + 2 * cols] = got[g * 2 * cols : (g + 1) * 2 * cols]
    back = sums[...].T
    halves, _, sensors, block = keep_ref.shape
    for g in range(groups):
        pair = back[:, g * block : (g + 1) * block].reshape(halves, 2, sensors, block)
        keep, send = by_parity("sy", pair[:, 0], pair[:, 1])
        keep_ref[:, g] = keep
        send_ref[:, g] = send.astype(BF16)


def residual_kernel(
    terms_ref,
    table_ref,
    noise_ref,
    solution_ref,
    residual_ref,
    direction_ref,
    step_ref,
    new_solution_ref,
    new_residual_ref,
    norm_ref,
):
    cols, sensors, steps = direction_ref.shape
    parts = []
    for b in range(terms_ref.shape[1]):
        parts.append(jnp.sum(terms_ref[:, b].astype(F32), axis=0))
    spectrum = jnp.concatenate(parts, axis=1)
    col_of = lane_ids(spectrum.shape[1]) % cols
    left = jnp.concatenate([jnp.where(col_of == c, spectrum, 0.0) for c in range(cols)], axis=0)
    returned = jnp.dot(left, table_ref[...], precision=HIGHEST, preferred_element_type=F32)
    for c in range(cols):
        product = direction_ref[c] + noise_ref[...] * returned[c * sensors : (c + 1) * sensors]
        new_residual = residual_ref[c] - step_ref[c] * product
        new_residual_ref[c] = new_residual
        new_solution_ref[c] = solution_ref[c] + step_ref[c] * direction_ref[c]
        norm = jnp.sum(
            jnp.sum(new_residual * new_residual, axis=0, keepdims=True), axis=1, keepdims=True
        )
        norm_ref[:, c : c + 1] = jnp.broadcast_to(norm[None], (norm_ref.shape[0], 1, LANES))


def direction_kernel(
    norms_ref,
    solution_ref,
    residual_ref,
    direction_ref,
    old_ref,
    solution_out,
    residual_out,
    direction_out,
    norm_ref,
    held,
    sems,
):
    cols, sensors, steps = direction_ref.shape
    early = [
        pltpu.make_async_copy(solution_ref, solution_out, sems.at[0]),
        pltpu.make_async_copy(residual_ref, residual_out, sems.at[1]),
    ]
    for copy in early:
        copy.start()
    norm = jnp.sum(norms_ref[...], axis=0)
    for c in range(cols):
        held[c] = residual_ref[c] + (norm[c : c + 1, 0:1] / old_ref[c]) * direction_ref[c]
    last = pltpu.make_async_copy(held, direction_out, sems.at[2])
    last.start()
    for c in range(cols):
        norm_ref[c] = jnp.max(norm[c : c + 1])
    for copy in (*early, last):
        copy.wait()


def swap(axis, toward_partner, toward_other):
    count = lax.axis_size(axis)
    near = [(i, i ^ 1) for i in range(count) if (i ^ 1) < count]
    far = [(i, i + 1 if i % 2 else i - 1) for i in range(1, count - 1 + count % 2)]
    second = lax.ppermute(toward_other, axis, far)
    first = lax.ppermute(toward_partner, axis, near)
    return first, second


def partners(axis):
    return [(i, i ^ 1) for i in range(lax.axis_size(axis))]


def exchange_half(blocks):
    sx, sy, fq = (lax.axis_size(axis) for axis in ALL_AXES)
    groups = [
        [(x * sy + y) * fq + f for x in range(sx) for y in range(parity, sy, 2) for f in range(fq)]
        for parity in range(2)
    ]
    flat = blocks.reshape((-1,) + blocks.shape[2:])
    return lax.all_to_all(flat, ALL_AXES, 0, 0, axis_index_groups=groups, tiled=True).reshape(
        blocks.shape
    )


def on_device(
    spectra,
    noise_weight,
    class_map,
    class_kappa,
    solution,
    residual,
    direction,
    step_length,
    old_norm,
):
    local_freqs, _, cells_x, cells_y, all_sensors = spectra.shape
    cols, sensors, steps = direction.shape
    fq_blocks = lax.axis_size("fq")
    tiles = lax.axis_size("sx") * lax.axis_size("sy")
    halves = tiles // 2
    block = 2 * local_freqs * cols
    lanes = block * fq_blocks
    forward, inverse = tables(local_freqs * fq_blocks, local_freqs, cols, steps)
    group = 2 if fq_blocks % 2 == 0 else 1
    chunks = fq_blocks // group
    width = group * block
    stride = cells_y + 8
    wide = width + LANES
    cells = cells_x * cells_y

    like = jax.ShapeDtypeStruct(direction.shape, F32)
    held = pltpu.VMEM(direction.shape, F32)
    spec = pl.pallas_call(
        functools.partial(spectrum_kernel, halves, fq_blocks),
        out_shape=jax.ShapeDtypeStruct((halves, fq_blocks, sensors, block), BF16),
        in_specs=[HBM] * 3,
        out_specs=VMEM,
        scratch_shapes=[
            held,
            pltpu.VMEM(noise_weight.shape, F32),
            pltpu.VMEM(forward.shape, F32),
            pltpu.SemaphoreType.DMA((3,)),
        ],
        compiler_params=params(62),
        cost_estimate=pl.CostEstimate(
            flops=2 * spectra.size, bytes_accessed=4 * spectra.size, transcendentals=0
        ),
        name="spectrum",
    )(direction, noise_weight, forward)
    mine = exchange_half(spec)
    other = lax.ppermute(mine, "sy", partners("sy"))

    edge = jax.ShapeDtypeStruct((DEPTH * cells_x, wide), BF16)
    end = jax.ShapeDtypeStruct((DEPTH * stride, wide), BF16)
    total = (cells_x + 2 * DEPTH + 2) * stride
    slabs = width // LANES
    pieces = []
    for i in range(chunks):
        at = slice(i * group, (i + 1) * group)
        stacked = pl.pallas_call(
            functools.partial(order_kernel, cols),
            out_shape=jax.ShapeDtypeStruct((2 * all_sensors, width), BF16),
            in_specs=[HBM, VMEM, VMEM],
            out_specs=VMEM,
            compiler_params=params(48),
            cost_estimate=pl.CostEstimate(
                flops=2 * spectra.size, bytes_accessed=4 * spectra.size, transcendentals=0
            ),
            name="order",
        )(spectra, mine[:, at], other[:, at])
        source, near_y, far_y, ends = pl.pallas_call(
            functools.partial(adjoint_kernel, local_freqs, cols),
            out_shape=(
                jax.ShapeDtypeStruct((slabs + 1, cells_x * stride, LANES), F32),
                edge,
                edge,
                jax.ShapeDtypeStruct((2, DEPTH * stride, wide), F32),
            ),
            in_specs=[VMEM] * 3,
            out_specs=(VMEM,) * 4,
            compiler_params=params(),
            name="adjoint",
        )(spectra, stacked, class_map.T)
        near_y, far_y = swap("sy", near_y, far_y)
        near_x, far_x = pl.pallas_call(
            ends_kernel,
            out_shape=(end, end),
            in_specs=[VMEM] * 3,
            out_specs=(VMEM,) * 2,
            scratch_shapes=[pltpu.VMEM((DEPTH * stride + 16, wide), F32)],
            compiler_params=params(),
            name="ends",
        )(ends, near_y, far_y)
        near_x, far_x = swap("sx", near_x, far_x)
        pieces.append(
            pl.pallas_call(
                functools.partial(field_kernel, local_freqs, cols),
                out_shape=(
                    jax.ShapeDtypeStruct((halves, group, sensors, block), F32),
                    jax.ShapeDtypeStruct((halves, group, sensors, block), BF16),
                ),
                in_specs=[VMEM] * 6 + [SMEM],
                out_specs=(VMEM,) * 2,
                scratch_shapes=[
                    pltpu.VMEM((slabs + 1, total, LANES), F32),
                    pltpu.VMEM((total, LANES), F32),
                    pltpu.VMEM((slabs, total, LANES), F32),
                    pltpu.VMEM((slabs, total, LANES), F32),
                    pltpu.VMEM((width, all_sensors), F32),
                ],
                compiler_params=params(),
                name="field",
            )(spectra, source, near_y, far_y, near_x, far_x, class_kappa)
        )
    keep = jnp.concatenate([piece[0] for piece in pieces], axis=1)
    send = jnp.concatenate([piece[1] for piece in pieces], axis=1)
    taken = lax.ppermute(send, "sy", partners("sy"))
    terms = exchange_half((keep + taken.astype(F32)).astype(BF16))
    new_solution, new_residual, norms = pl.pallas_call(
        residual_kernel,
        out_shape=(like, like, jax.ShapeDtypeStruct((tiles, cols, LANES), F32)),
        in_specs=[VMEM] * 6 + [SMEM],
        out_specs=(VMEM,) * 3,
        compiler_params=params(),
        name="residual",
    )(terms, inverse, noise_weight, solution, residual, direction, step_length)
    norms = lax.all_to_all(norms, GRID_AXES, 0, 0, tiled=True)
    new_solution, new_residual, new_direction, new_norm = pl.pallas_call(
        direction_kernel,
        out_shape=(like, like, like, jax.ShapeDtypeStruct((cols,), F32)),
        in_specs=[VMEM] * 4 + [SMEM],
        out_specs=(HBM, HBM, HBM, SMEM),
        scratch_shapes=[held, pltpu.SemaphoreType.DMA((3,))],
        compiler_params=params(),
        name="direction",
    )(norms, new_solution, new_residual, direction, old_norm)
    return (new_solution, new_residual, new_direction, new_norm)


def solution(mesh):
    return jax.shard_map(
        on_device,
        mesh=mesh,
        in_specs=(
            P("fq", None, "sx", "sy", None),
            P(("sx", "sy"), None),
            P("sx", "sy"),
            P(),
            P("fq", ("sx", "sy"), None),
            P("fq", ("sx", "sy"), None),
            P("fq", ("sx", "sy"), None),
            P("fq"),
            P("fq"),
        ),
        out_specs=(
            P("fq", ("sx", "sy"), None),
            P("fq", ("sx", "sy"), None),
            P("fq", ("sx", "sy"), None),
            P("fq"),
        ),
        check_vma=False,
    )
```

```python
import functools
import math

import jax
import jax.numpy as jnp
from jax import lax
from jax.experimental import pallas as pl
from jax.experimental.pallas import tpu as pltpu
from jax.sharding import PartitionSpec as P
import numpy as np

SWEEPS = 4
DEPTH = SWEEPS - 1
HIGHEST = lax.Precision.HIGHEST
F32 = jnp.float32
BF16 = jnp.bfloat16
GRID_AXES = ("sx", "sy")
ALL_AXES = ("sx", "sy", "fq")
LANES = 128
MIB = 1024 * 1024
VMEM = pl.BlockSpec(memory_space=pltpu.VMEM)
SMEM = pl.BlockSpec(memory_space=pltpu.SMEM)
HBM = pl.BlockSpec(memory_space=pltpu.HBM)


def params(mib=24):
    return pltpu.CompilerParams(vmem_limit_bytes=mib * MIB)


def tables(freq_count, local_freqs, local_cols, time_steps):
    freq = np.arange(freq_count)[:, None]
    step = np.arange(time_steps)[None, :]
    phases = (freq * step % time_steps) * (2.0 * math.pi / time_steps)
    factor = 1.0 / math.sqrt(time_steps)
    pair = np.stack([np.cos(phases) * factor, -np.sin(phases) * factor], 1)
    forward = np.repeat(pair.reshape(2 * freq_count, time_steps), local_cols, 0)
    doubling = np.where(np.arange(freq_count) == 0, 1.0, 2.0)[:, None, None]
    inverse = np.repeat((pair * doubling).reshape(2 * freq_count, time_steps), local_cols, 0)
    return forward.T.astype(np.float32), inverse.astype(np.float32)


def by_side(axis, low, high):
    even = lax.axis_index(axis) % 2 == 0
    return jnp.where(even, high, low), jnp.where(even, low, high)


def by_parity(axis, mine, other):
    even = lax.axis_index(axis) % 2 == 0
    return jnp.where(even, mine, other), jnp.where(even, other, mine)


def lane_ids(lanes):
    return lax.broadcasted_iota(jnp.int32, (1, lanes), 1)


def fetch_all(pairs, sems):
    copies = [pltpu.make_async_copy(a, b, sems.at[i]) for i, (a, b) in enumerate(pairs)]
    for copy in copies:
        copy.start()
    for copy in copies:
        copy.wait()


def spectrum_kernel(
    tiles, fq_blocks, direction_in, noise_in, table_in, out_ref, direction_ref, noise_ref, table_ref, sems
):
    fetch_all(
        ((direction_in, direction_ref), (noise_in, noise_ref), (table_in, table_ref)), sems
    )
    cols, sensors, steps = direction_ref.shape
    lanes = table_ref.shape[1]
    weighted = (noise_ref[...][None] * direction_ref[...]).reshape(cols * sensors, steps)
    full = jnp.dot(weighted, table_ref[...], precision=HIGHEST, preferred_element_type=F32)
    col_of = lane_ids(lanes) % cols
    spec = full[0:sensors]
    for col in range(1, cols):
        spec = jnp.where(col_of == col, full[col * sensors : (col + 1) * sensors], spec)
    spec = spec.astype(BF16)
    block = lanes // fq_blocks
    for b in range(fq_blocks):
        part = spec[:, b * block : (b + 1) * block]
        out_ref[:, b] = jnp.broadcast_to(part[None], (tiles, sensors, block))


def class_rows(class_ref):
    cells_y, cells_x = class_ref.shape
    cells = cells_x * cells_y
    row = lax.broadcasted_iota(jnp.int32, (cells, cells_x), 0)
    pick = (row // cells_y == lax.broadcasted_iota(jnp.int32, (cells, cells_x), 1)).astype(F32)
    by_row = lax.dot_general(
        pick,
        class_ref[...].astype(F32) + 1.0,
        (((1,), (1,)), ((), ())),
        preferred_element_type=F32,
    )
    at = lax.broadcasted_iota(jnp.int32, (cells, cells_y), 0) % cells_y
    own = (at == lax.broadcasted_iota(jnp.int32, (cells, cells_y), 1)).astype(F32)
    return jnp.dot(by_row * own, jnp.ones((cells_y, LANES), F32), preferred_element_type=F32)


def adjoint_of(part, stacked):
    _, cells_x, cells_y, all_sensors = part.shape
    both = part.reshape(2, cells_x * cells_y, all_sensors)
    both = jnp.concatenate([both[0], both[1]], axis=1)
    return jnp.dot(both, stacked, preferred_element_type=F32)


def freq_lanes(lanes, cols, freqs):
    return (lane_ids(lanes) // (2 * cols)) % freqs


def order_kernel(cols, spectra_in, mine_ref, other_ref, stacked_ref):
    halves, group, sensors, block = mine_ref.shape
    lanes = group * block
    parts = []
    for b in range(group):
        pair = by_parity("sy", mine_ref[:, b], other_ref[:, b])
        parts.append(jnp.stack(pair, axis=1).reshape(2 * halves * sensors, block))
    direct = jnp.concatenate(parts, axis=1)
    wide = direct.astype(F32)
    is_real = (lane_ids(lanes) // cols) % 2 == 0
    turned = jnp.where(
        is_real, pltpu.roll(wide, lanes - cols, 1), -pltpu.roll(wide, cols, 1)
    ).astype(BF16)
    stacked_ref[...] = jnp.concatenate([direct, turned], axis=0)


def adjoint_kernel(
    freqs, cols, spectra_ref, stacked_ref, class_ref, out_ref, far_ref, near_ref, ends_ref
):
    _, _, cells_x, cells_y, all_sensors = spectra_ref.shape
    stride = out_ref.shape[1] // cells_x
    lanes = stacked_ref.shape[1]
    freq_of = freq_lanes(lanes, cols, freqs)
    classes = class_rows(class_ref)
    stacked = stacked_ref[...]
    acc = adjoint_of(spectra_ref[0], stacked)
    for f in range(1, freqs):
        acc = jnp.where(freq_of == f, adjoint_of(spectra_ref[f], stacked), acc)
    for k in range(out_ref.shape[0]):
        part = classes if k * LANES == lanes else acc[:, k * LANES : (k + 1) * LANES]
        for x in range(cells_x):
            base = x * stride
            out_ref[k, base : base + cells_y] = part[x * cells_y : (x + 1) * cells_y]
            out_ref[k, base + cells_y : base + stride] = jnp.zeros((stride - cells_y, LANES), F32)
        at = slice(k * LANES, (k + 1) * LANES)
        for j in range(DEPTH):
            low = out_ref[k, pl.ds(j, cells_x, stride=stride), :]
            high = out_ref[k, pl.ds(cells_y - DEPTH + j, cells_x, stride=stride), :]
            near, far = by_side("sy", low, high)
            near_ref[j * cells_x : (j + 1) * cells_x, at] = near.astype(BF16)
            far_ref[j * cells_x : (j + 1) * cells_x, at] = far.astype(BF16)
        ends_ref[0, :, at] = out_ref[k, 0 : DEPTH * stride]
        ends_ref[1, :, at] = out_ref[k, (cells_x - DEPTH) * stride : cells_x * stride]


def ends_kernel(ends_ref, far_ref, near_ref, far_out, near_out, held):
    span = ends_ref.shape[1]
    stride = span // DEPTH
    cells_x = near_ref.shape[0] // DEPTH
    cells_y = stride - 8
    after, before = by_side("sy", far_ref[...].astype(F32), near_ref[...].astype(F32))
    built = []
    for side in range(2):
        held[...] = jnp.zeros_like(held)
        held[8 : 8 + span] = ends_ref[side]
        first = 0 if side == 0 else cells_x - DEPTH
        for x in range(DEPTH):
            for j in range(DEPTH):
                take = j * cells_x + first + x
                to = 8 + x * stride
                held[to + cells_y + j : to + cells_y + j + 1] = after[take : take + 1]
                held[to - DEPTH + j : to - DEPTH + j + 1] = before[take : take + 1]
        built.append(held[8 - DEPTH : 8 - DEPTH + span])
    near, far = by_side("sx", built[0], built[1])
    near_out[...] = near.astype(BF16)
    far_out[...] = far.astype(BF16)


def coefficients(classes, kappa_ref):
    kappa = jnp.zeros_like(classes)
    for n in range(kappa_ref.shape[0]):
        kappa = jnp.where(classes == n + 1.0, kappa_ref[n], kappa)
    scale = jnp.where(classes > 0.0, 1.0 / (1.0 + 4.0 * kappa), 0.0)
    return scale, kappa * scale


def sweep(source, gain, old, new, first, last, stride):
    near = (
        old[first - stride : last - stride]
        + old[first + stride : last + stride]
        + old[first - 1 : last - 1]
        + old[first + 1 : last + 1]
    )
    new[first:last] = source[first:last] + gain[first:last] * near


def both_forms(turned, cols):
    blocks, cells = turned.shape[0] // (2 * cols), turned.shape[1]
    pair = turned.reshape(blocks, 2, cols, cells)
    plain = pair.astype(BF16).reshape(blocks, 2 * cols, cells)
    crossed = jnp.stack([-pair[:, 1], pair[:, 0]], axis=1)
    crossed = crossed.astype(BF16).reshape(blocks, 2 * cols, cells)
    return jnp.concatenate([plain, crossed], axis=2)


def rows_of(forms, f, freqs):
    return jnp.concatenate([forms[b] for b in range(f, forms.shape[0], freqs)], axis=0)


def inner_kernel(
    freqs, cols, spectra_ref, source_ref, far_y_ref, near_y_ref, kappa_ref, sums_ref, wide, gain, one, two
):
    _, _, cells_x, cells_y, all_sensors = spectra_ref.shape
    cells = cells_x * cells_y
    stride = source_ref.shape[1] // cells_x
    slabs = one.shape[0]
    start = 2 * stride
    rows = cells_x * stride
    total = wide.shape[1]
    for k in range(slabs + 1):
        at = slice(k * LANES, (k + 1) * LANES)
        wide[k, 0:start] = jnp.zeros((start, LANES), F32)
        wide[k, start + rows : total] = jnp.zeros((total - start - rows, LANES), F32)
        wide[k, start : start + rows] = source_ref[k]
        after, before = by_side("sy", far_y_ref[:, at].astype(F32), near_y_ref[:, at].astype(F32))
        for j in range(DEPTH):
            part = slice(j * cells_x, (j + 1) * cells_x)
            wide[k, pl.ds(start + cells_y + j, cells_x, stride=stride), :] = after[part]
            wide[k, pl.ds(start - DEPTH + j, cells_x, stride=stride), :] = before[part]
    lo, hi = start - 8, start + rows
    scale, gain[lo:hi] = coefficients(wide[slabs, lo:hi], kappa_ref)
    turned = []
    for k in range(slabs):
        wide[k, lo:hi] = wide[k, lo:hi] * scale
        old, new = wide.at[k], one.at[k]
        for x in range(1, DEPTH + 1):
            first, last = start + x * stride - 8, start + rows - x * stride
            sweep(wide.at[k], gain, old, new, first, last, stride)
            old, new = new, (two.at[k] if x % 2 else one.at[k])
        inner = old[start + DEPTH * stride : start + rows - DEPTH * stride]
        inner = inner.reshape(cells_x - 2 * DEPTH, stride, LANES)[:, 0:cells_y]
        edge = jnp.zeros((DEPTH * cells_y, LANES), F32)
        turned.append(
            jnp.concatenate([edge, inner.reshape(cells - 2 * DEPTH * cells_y, LANES), edge], axis=0).T
        )
    forms = both_forms(jnp.concatenate(turned, axis=0), cols)
    groups = forms.shape[0] // freqs
    for f in range(freqs):
        right = spectra_ref[f].reshape(2 * cells, all_sensors)
        got = jnp.dot(rows_of(forms, f, freqs), right, preferred_element_type=F32)
        for g in range(groups):
            at = (g * freqs + f) * 2 * cols
            sums_ref[at : at + 2 * cols] = got[g * 2 * cols : (g + 1) * 2 * cols]


def field_kernel(
    freqs,
    cols,
    spectra_ref,
    source_ref,
    sums_ref,
    far_y_ref,
    near_y_ref,
    far_x_ref,
    near_x_ref,
    kappa_ref,
    keep_ref,
    send_ref,
    wide,
    gain,
    one,
    two,
    sums,
):
    _, _, cells_x, cells_y, all_sensors = spectra_ref.shape
    stride = source_ref.shape[1] // cells_x
    rows = cells_x * stride
    slabs = one.shape[1]
    start = stride + 8
    deep = 2 * DEPTH
    total = wide.shape[2]

    def base(x):
        return start + x * stride

    for k in range(slabs + 1):
        at = slice(k * LANES, (k + 1) * LANES)
        after, before = by_side("sy", far_y_ref[:, at].astype(F32), near_y_ref[:, at].astype(F32))
        below, above = by_side("sx", far_x_ref[:, at].astype(F32), near_x_ref[:, at].astype(F32))
        for end in range(2):
            own, outer = (DEPTH, 0) if end == 0 else (0, deep)
            inside = 0 if end == 0 else cells_x - deep
            wide[end, k] = jnp.zeros((total, LANES), F32)
            wide[end, k, base(own) : base(own + deep)] = source_ref[
                k, inside * stride : (inside + deep) * stride
            ]
            for j in range(DEPTH):
                part = slice(j * cells_x + inside, j * cells_x + inside + deep)
                wide[end, k, pl.ds(base(own) + cells_y + j, deep, stride=stride), :] = after[part]
                wide[end, k, pl.ds(base(own) - DEPTH + j, deep, stride=stride), :] = before[part]
            wide[end, k, base(outer) - DEPTH : base(outer + DEPTH) - DEPTH] = above if end == 0 else below
    lo, hi = base(0) - 8, base(3 * DEPTH)
    turned = []
    filler = -(deep * cells_y) % LANES
    for end in range(2):
        scale, gain[end, lo:hi] = coefficients(wide[end, slabs, lo:hi], kappa_ref)
        for k in range(slabs):
            wide[end, k, lo:hi] = wide[end, k, lo:hi] * scale
    for k in range(slabs):
        fields = []
        for end in range(2):
            source = wide.at[end, k]
            old, new = source, one.at[end, k]
            for x in range(1, DEPTH + 1):
                sweep(source, gain.at[end], old, new, base(x) - 8, base(3 * DEPTH - x), stride)
                old, new = new, (two.at[end, k] if x % 2 else one.at[end, k])
            field = old[base(DEPTH) : base(deep)].reshape(DEPTH, stride, LANES)[:, 0:cells_y]
            fields.append(field.reshape(DEPTH * cells_y, LANES))
        fields.append(jnp.zeros((filler, LANES), F32))
        turned.append(jnp.concatenate(fields, axis=0).T)
    forms = both_forms(jnp.concatenate(turned, axis=0), cols)
    groups = forms.shape[0] // freqs
    blank = jnp.zeros((filler, all_sensors), BF16)
    for f in range(freqs):
        right = []
        for part in range(2):
            for x in (0, cells_x - DEPTH):
                rows_here = spectra_ref[f, part, x : x + DEPTH]
                right.append(rows_here.reshape(DEPTH * cells_y, all_sensors))
            right.append(blank)
        got = jnp.dot(
            rows_of(forms, f, freqs), jnp.concatenate(right, axis=0), preferred_element_type=F32
        )
        for g in range(groups):
            at = (g * freqs + f) * 2 * cols
            sums[at : at + 2 * cols] = sums_ref[at : at + 2 * cols] + got[g * 2 * cols : (g + 1) * 2 * cols]
    back = sums[...].T
    halves, _, sensors, block = keep_ref.shape
    for g in range(groups):
        pair = back[:, g * block : (g + 1) * block].reshape(halves, 2, sensors, block)
        keep, send = by_parity("sy", pair[:, 0], pair[:, 1])
        keep_ref[:, g] = keep
        send_ref[:, g] = send.astype(BF16)


def residual_kernel(
    terms_ref,
    table_ref,
    noise_ref,
    solution_ref,
    residual_ref,
    direction_ref,
    step_ref,
    new_solution_ref,
    new_residual_ref,
    norm_ref,
):
    cols, sensors, steps = direction_ref.shape
    parts = []
    for b in range(terms_ref.shape[1]):
        parts.append(jnp.sum(terms_ref[:, b].astype(F32), axis=0))
    spectrum = jnp.concatenate(parts, axis=1)
    col_of = lane_ids(spectrum.shape[1]) % cols
    left = jnp.concatenate([jnp.where(col_of == c, spectrum, 0.0) for c in range(cols)], axis=0)
    returned = jnp.dot(left, table_ref[...], precision=HIGHEST, preferred_element_type=F32)
    lane = lane_ids(LANES)
    norms = jnp.zeros((1, LANES), F32)
    for c in range(cols):
        product = direction_ref[c] + noise_ref[...] * returned[c * sensors : (c + 1) * sensors]
        new_residual = residual_ref[c] - step_ref[c] * product
        new_residual_ref[c] = new_residual
        new_solution_ref[c] = solution_ref[c] + step_ref[c] * direction_ref[c]
        norm = jnp.sum(
            jnp.sum(new_residual * new_residual, axis=0, keepdims=True), axis=1, keepdims=True
        )
        norms = jnp.where(lane == c, norm, norms)
    norm_ref[...] = jnp.broadcast_to(norms[None], norm_ref.shape)


def direction_kernel(
    norms_ref,
    solution_ref,
    residual_ref,
    direction_ref,
    old_ref,
    solution_out,
    residual_out,
    direction_out,
    norm_out,
    held,
    norm_ref,
    sems,
):
    cols, sensors, steps = direction_ref.shape
    early = [
        pltpu.make_async_copy(solution_ref, solution_out, sems.at[0]),
        pltpu.make_async_copy(residual_ref, residual_out, sems.at[1]),
    ]
    for copy in early:
        copy.start()
    norm = jnp.sum(norms_ref[...], axis=0)
    norm_ref[...] = norm[0, 0:cols]
    final = pltpu.make_async_copy(norm_ref, norm_out, sems.at[3])
    final.start()
    for c in range(cols):
        held[c] = residual_ref[c] + (norm[:, c : c + 1] / old_ref[c]) * direction_ref[c]
    last = pltpu.make_async_copy(held, direction_out, sems.at[2])
    last.start()
    for copy in (*early, last, final):
        copy.wait()


def swap(axis, toward_partner, toward_other):
    count = lax.axis_size(axis)
    near = [(i, i ^ 1) for i in range(count) if (i ^ 1) < count]
    far = [(i, i + 1 if i % 2 else i - 1) for i in range(1, count - 1 + count % 2)]
    second = lax.ppermute(toward_other, axis, far)
    first = lax.ppermute(toward_partner, axis, near)
    return first, second


def partners(axis):
    return [(i, i ^ 1) for i in range(lax.axis_size(axis))]


def exchange_half(blocks):
    sx, sy, fq = (lax.axis_size(axis) for axis in ALL_AXES)
    groups = [
        [(x * sy + y) * fq + f for x in range(sx) for y in range(parity, sy, 2) for f in range(fq)]
        for parity in range(2)
    ]
    flat = blocks.reshape((-1,) + blocks.shape[2:])
    return lax.all_to_all(flat, ALL_AXES, 0, 0, axis_index_groups=groups, tiled=True).reshape(
        blocks.shape
    )


def on_device(
    spectra,
    noise_weight,
    class_map,
    class_kappa,
    solution,
    residual,
    direction,
    step_length,
    old_norm,
):
    local_freqs, _, cells_x, cells_y, all_sensors = spectra.shape
    cols, sensors, steps = direction.shape
    fq_blocks = lax.axis_size("fq")
    tiles = lax.axis_size("sx") * lax.axis_size("sy")
    halves = tiles // 2
    block = 2 * local_freqs * cols
    lanes = block * fq_blocks
    forward, inverse = tables(local_freqs * fq_blocks, local_freqs, cols, steps)
    group = 2 if fq_blocks % 2 == 0 else 1
    chunks = fq_blocks // group
    width = group * block
    stride = cells_y + 8
    wide = width + LANES
    cells = cells_x * cells_y

    like = jax.ShapeDtypeStruct(direction.shape, F32)
    held = pltpu.VMEM(direction.shape, F32)
    spec = pl.pallas_call(
        functools.partial(spectrum_kernel, halves, fq_blocks),
        out_shape=jax.ShapeDtypeStruct((halves, fq_blocks, sensors, block), BF16),
        in_specs=[HBM] * 3,
        out_specs=VMEM,
        scratch_shapes=[
            held,
            pltpu.VMEM(noise_weight.shape, F32),
            pltpu.VMEM(forward.shape, F32),
            pltpu.SemaphoreType.DMA((3,)),
        ],
        compiler_params=params(62),
        cost_estimate=pl.CostEstimate(
            flops=2 * spectra.size, bytes_accessed=4 * spectra.size, transcendentals=0
        ),
        name="spectrum",
    )(direction, noise_weight, forward)
    mine = exchange_half(spec)
    other = lax.ppermute(mine, "sy", partners("sy"))

    edge = jax.ShapeDtypeStruct((DEPTH * cells_x, wide), BF16)
    end = jax.ShapeDtypeStruct((DEPTH * stride, wide), BF16)
    total = (cells_x + 4) * stride
    strip = (3 * DEPTH + 2) * stride + 16
    slabs = width // LANES
    pieces = []
    for i in range(chunks):
        at = slice(i * group, (i + 1) * group)
        stacked = pl.pallas_call(
            functools.partial(order_kernel, cols),
            out_shape=jax.ShapeDtypeStruct((2 * all_sensors, width), BF16),
            in_specs=[HBM, VMEM, VMEM],
            out_specs=VMEM,
            compiler_params=params(48),
            cost_estimate=pl.CostEstimate(
                flops=2 * spectra.size, bytes_accessed=4 * spectra.size, transcendentals=0
            ),
            name="order",
        )(spectra, mine[:, at], other[:, at])
        source, far_y, near_y, ends = pl.pallas_call(
            functools.partial(adjoint_kernel, local_freqs, cols),
            out_shape=(
                jax.ShapeDtypeStruct((slabs + 1, cells_x * stride, LANES), F32),
                edge,
                edge,
                jax.ShapeDtypeStruct((2, DEPTH * stride, wide), F32),
            ),
            in_specs=[VMEM] * 3,
            out_specs=(VMEM,) * 4,
            compiler_params=params(),
            name="adjoint",
        )(spectra, stacked, class_map.T)
        near_y, far_y = swap("sy", near_y, far_y)
        far_x, near_x = pl.pallas_call(
            ends_kernel,
            out_shape=(end, end),
            in_specs=[VMEM] * 3,
            out_specs=(VMEM,) * 2,
            scratch_shapes=[pltpu.VMEM((DEPTH * stride + 16, wide), F32)],
            compiler_params=params(),
            name="ends",
        )(ends, far_y, near_y)
        near_x, far_x = swap("sx", near_x, far_x)
        sums = pl.pallas_call(
            functools.partial(inner_kernel, local_freqs, cols),
            out_shape=jax.ShapeDtypeStruct((width, all_sensors), F32),
            in_specs=[VMEM] * 4 + [SMEM],
            out_specs=VMEM,
            scratch_shapes=[
                pltpu.VMEM((slabs + 1, total, LANES), F32),
                pltpu.VMEM((total, LANES), F32),
                pltpu.VMEM((slabs, total, LANES), F32),
                pltpu.VMEM((slabs, total, LANES), F32),
            ],
            compiler_params=params(),
            cost_estimate=pl.CostEstimate(
                flops=4 * spectra.size * width, bytes_accessed=2 * spectra.size, transcendentals=0
            ),
            name="inner",
        )(spectra, source, far_y, near_y, class_kappa)
        pieces.append(
            pl.pallas_call(
                functools.partial(field_kernel, local_freqs, cols),
                out_shape=(
                    jax.ShapeDtypeStruct((halves, group, sensors, block), F32),
                    jax.ShapeDtypeStruct((halves, group, sensors, block), BF16),
                ),
                in_specs=[VMEM] * 7 + [SMEM],
                out_specs=(VMEM,) * 2,
                scratch_shapes=[
                    pltpu.VMEM((2, slabs + 1, strip, LANES), F32),
                    pltpu.VMEM((2, strip, LANES), F32),
                    pltpu.VMEM((2, slabs, strip, LANES), F32),
                    pltpu.VMEM((2, slabs, strip, LANES), F32),
                    pltpu.VMEM((width, all_sensors), F32),
                ],
                compiler_params=params(),
                name="field",
            )(spectra, source, sums, far_y, near_y, far_x, near_x, class_kappa)
        )
    keep = jnp.concatenate([piece[0] for piece in pieces], axis=1)
    send = jnp.concatenate([piece[1] for piece in pieces], axis=1)
    taken = lax.ppermute(send, "sy", partners("sy"))
    terms = exchange_half((keep + taken.astype(F32)).astype(BF16))
    new_solution, new_residual, norms = pl.pallas_call(
        residual_kernel,
        out_shape=(like, like, jax.ShapeDtypeStruct((tiles, 1, LANES), F32)),
        in_specs=[VMEM] * 6 + [SMEM],
        out_specs=(VMEM,) * 3,
        compiler_params=params(),
        name="residual",
    )(terms, inverse, noise_weight, solution, residual, direction, step_length)
    norms = lax.all_to_all(norms, GRID_AXES, 0, 0, tiled=True)
    new_solution, new_residual, new_direction, new_norm = pl.pallas_call(
        direction_kernel,
        out_shape=(like, like, like, jax.ShapeDtypeStruct((cols,), F32)),
        in_specs=[VMEM] * 4 + [SMEM],
        out_specs=(HBM,) * 4,
        scratch_shapes=[held, pltpu.VMEM((cols,), F32), pltpu.SemaphoreType.DMA((4,))],
        compiler_params=params(),
        name="direction",
    )(norms, new_solution, new_residual, direction, old_norm)
    return (new_solution, new_residual, new_direction, new_norm)


def solution(mesh):
    return jax.shard_map(
        on_device,
        mesh=mesh,
        in_specs=(
            P("fq", None, "sx", "sy", None),
            P(("sx", "sy"), None),
            P("sx", "sy"),
            P(),
            P("fq", ("sx", "sy"), None),
            P("fq", ("sx", "sy"), None),
            P("fq", ("sx", "sy"), None),
            P("fq"),
            P("fq"),
        ),
        out_specs=(
            P("fq", ("sx", "sy"), None),
            P("fq", ("sx", "sy"), None),
            P("fq", ("sx", "sy"), None),
            P("fq"),
        ),
        check_vma=False,
    )
```

```python
import functools
import math

import jax
import jax.numpy as jnp
from jax import lax
from jax.experimental import pallas as pl
from jax.experimental.pallas import tpu as pltpu
from jax.sharding import PartitionSpec as P
import numpy as np

SWEEPS = 4
DEPTH = SWEEPS - 1
HIGHEST = lax.Precision.HIGHEST
F32 = jnp.float32
BF16 = jnp.bfloat16
GRID_AXES = ("sx", "sy")
ALL_AXES = ("sx", "sy", "fq")
LANES = 128
MIB = 1024 * 1024
VMEM = pl.BlockSpec(memory_space=pltpu.VMEM)
SMEM = pl.BlockSpec(memory_space=pltpu.SMEM)
HBM = pl.BlockSpec(memory_space=pltpu.HBM)


def params(mib=24):
    return pltpu.CompilerParams(vmem_limit_bytes=mib * MIB)


def tables(freq_count, local_freqs, local_cols, time_steps):
    freq = np.arange(freq_count)[:, None]
    step = np.arange(time_steps)[None, :]
    phases = (freq * step % time_steps) * (2.0 * math.pi / time_steps)
    factor = 1.0 / math.sqrt(time_steps)
    pair = np.stack([np.cos(phases) * factor, -np.sin(phases) * factor], 1)
    forward = np.repeat(pair.reshape(2 * freq_count, time_steps), local_cols, 0)
    doubling = np.where(np.arange(freq_count) == 0, 1.0, 2.0)[:, None, None]
    inverse = np.repeat((pair * doubling).reshape(2 * freq_count, time_steps), local_cols, 0)
    return forward.T.astype(np.float32), inverse.astype(np.float32)


def by_side(axis, low, high):
    even = lax.axis_index(axis) % 2 == 0
    return jnp.where(even, high, low), jnp.where(even, low, high)


def by_parity(axis, mine, other):
    even = lax.axis_index(axis) % 2 == 0
    return jnp.where(even, mine, other), jnp.where(even, other, mine)


def lane_ids(lanes):
    return lax.broadcasted_iota(jnp.int32, (1, lanes), 1)


def fetch_all(pairs, sems):
    copies = [pltpu.make_async_copy(a, b, sems.at[i]) for i, (a, b) in enumerate(pairs)]
    for copy in copies:
        copy.start()
    for copy in copies:
        copy.wait()


def spectrum_kernel(
    tiles, fq_blocks, direction_in, noise_in, table_in, out_ref, direction_ref, noise_ref, table_ref, sems
):
    fetch_all(
        ((direction_in, direction_ref), (noise_in, noise_ref), (table_in, table_ref)), sems
    )
    cols, sensors, steps = direction_ref.shape
    lanes = table_ref.shape[1]
    weighted = (noise_ref[...][None] * direction_ref[...]).reshape(cols * sensors, steps)
    full = jnp.dot(weighted, table_ref[...], precision=HIGHEST, preferred_element_type=F32)
    col_of = lane_ids(lanes) % cols
    spec = full[0:sensors]
    for col in range(1, cols):
        spec = jnp.where(col_of == col, full[col * sensors : (col + 1) * sensors], spec)
    spec = spec.astype(BF16)
    block = lanes // fq_blocks
    for b in range(fq_blocks):
        part = spec[:, b * block : (b + 1) * block]
        out_ref[:, b] = jnp.broadcast_to(part[None], (tiles, sensors, block))


def class_rows(class_ref):
    cells_y, cells_x = class_ref.shape
    cells = cells_x * cells_y
    row = lax.broadcasted_iota(jnp.int32, (cells, cells_x), 0)
    pick = (row // cells_y == lax.broadcasted_iota(jnp.int32, (cells, cells_x), 1)).astype(F32)
    by_row = lax.dot_general(
        pick,
        class_ref[...].astype(F32) + 1.0,
        (((1,), (1,)), ((), ())),
        preferred_element_type=F32,
    )
    at = lax.broadcasted_iota(jnp.int32, (cells, cells_y), 0) % cells_y
    own = (at == lax.broadcasted_iota(jnp.int32, (cells, cells_y), 1)).astype(F32)
    return jnp.dot(by_row * own, jnp.ones((cells_y, LANES), F32), preferred_element_type=F32)


def adjoint_of(part, stacked):
    _, cells_x, cells_y, all_sensors = part.shape
    both = part.reshape(2, cells_x * cells_y, all_sensors)
    both = jnp.concatenate([both[0], both[1]], axis=1)
    return jnp.dot(both, stacked, preferred_element_type=F32)


def freq_lanes(lanes, cols, freqs):
    return (lane_ids(lanes) // (2 * cols)) % freqs


def order_kernel(cols, spectra_in, mine_ref, other_ref, stacked_ref):
    halves, group, sensors, block = mine_ref.shape
    lanes = group * block
    parts = []
    for b in range(group):
        pair = by_parity("sy", mine_ref[:, b], other_ref[:, b])
        parts.append(jnp.stack(pair, axis=1).reshape(2 * halves * sensors, block))
    direct = jnp.concatenate(parts, axis=1)
    wide = direct.astype(F32)
    is_real = (lane_ids(lanes) // cols) % 2 == 0
    turned = jnp.where(
        is_real, pltpu.roll(wide, lanes - cols, 1), -pltpu.roll(wide, cols, 1)
    ).astype(BF16)
    stacked_ref[...] = jnp.concatenate([direct, turned], axis=0)


def adjoint_kernel(
    freqs, cols, spectra_ref, stacked_ref, class_ref, out_ref, far_ref, near_ref, ends_ref
):
    _, _, cells_x, cells_y, all_sensors = spectra_ref.shape
    stride = out_ref.shape[1] // cells_x
    lanes = stacked_ref.shape[1]
    freq_of = freq_lanes(lanes, cols, freqs)
    classes = class_rows(class_ref)
    stacked = stacked_ref[...]
    acc = adjoint_of(spectra_ref[0], stacked)
    for f in range(1, freqs):
        acc = jnp.where(freq_of == f, adjoint_of(spectra_ref[f], stacked), acc)
    for k in range(out_ref.shape[0]):
        part = classes if k * LANES == lanes else acc[:, k * LANES : (k + 1) * LANES]
        for x in range(cells_x):
            base = x * stride
            out_ref[k, base : base + cells_y] = part[x * cells_y : (x + 1) * cells_y]
            out_ref[k, base + cells_y : base + stride] = jnp.zeros((stride - cells_y, LANES), F32)
        at = slice(k * LANES, (k + 1) * LANES)
        for j in range(DEPTH):
            low = out_ref[k, pl.ds(j, cells_x, stride=stride), :]
            high = out_ref[k, pl.ds(cells_y - DEPTH + j, cells_x, stride=stride), :]
            near, far = by_side("sy", low, high)
            near_ref[j * cells_x : (j + 1) * cells_x, at] = near.astype(BF16)
            far_ref[j * cells_x : (j + 1) * cells_x, at] = far.astype(BF16)
        ends_ref[0, :, at] = out_ref[k, 0 : DEPTH * stride]
        ends_ref[1, :, at] = out_ref[k, (cells_x - DEPTH) * stride : cells_x * stride]


def ends_kernel(ends_ref, far_ref, near_ref, far_out, near_out, held):
    span = ends_ref.shape[1]
    stride = span // DEPTH
    cells_x = near_ref.shape[0] // DEPTH
    cells_y = stride - 8
    after, before = by_side("sy", far_ref[...].astype(F32), near_ref[...].astype(F32))
    built = []
    for side in range(2):
        held[...] = jnp.zeros_like(held)
        held[8 : 8 + span] = ends_ref[side]
        first = 0 if side == 0 else cells_x - DEPTH
        for x in range(DEPTH):
            for j in range(DEPTH):
                take = j * cells_x + first + x
                to = 8 + x * stride
                held[to + cells_y + j : to + cells_y + j + 1] = after[take : take + 1]
                held[to - DEPTH + j : to - DEPTH + j + 1] = before[take : take + 1]
        built.append(held[8 - DEPTH : 8 - DEPTH + span])
    near, far = by_side("sx", built[0], built[1])
    near_out[...] = near.astype(BF16)
    far_out[...] = far.astype(BF16)


def coefficients(classes, kappa_ref):
    kappa = jnp.zeros_like(classes)
    for n in range(kappa_ref.shape[0]):
        kappa = jnp.where(classes == n + 1.0, kappa_ref[n], kappa)
    scale = jnp.where(classes > 0.0, 1.0 / (1.0 + 4.0 * kappa), 0.0)
    return scale, kappa * scale


def sweep(source, gain, old, new, first, last, stride):
    near = (
        old[first - stride : last - stride]
        + old[first + stride : last + stride]
        + old[first - 1 : last - 1]
        + old[first + 1 : last + 1]
    )
    new[first:last] = source[first:last] + gain[first:last] * near


def both_forms(turned, cols):
    blocks, cells = turned.shape[0] // (2 * cols), turned.shape[1]
    pair = turned.reshape(blocks, 2, cols, cells)
    plain = pair.astype(BF16).reshape(blocks, 2 * cols, cells)
    crossed = jnp.stack([-pair[:, 1], pair[:, 0]], axis=1)
    crossed = crossed.astype(BF16).reshape(blocks, 2 * cols, cells)
    return jnp.concatenate([plain, crossed], axis=2)


def rows_of(forms, f, freqs):
    return jnp.concatenate([forms[b] for b in range(f, forms.shape[0], freqs)], axis=0)


def own_kernel(source_ref, kappa_ref, scaled_ref, gain_ref):
    slabs = scaled_ref.shape[0]
    scale, gain_ref[...] = coefficients(source_ref[slabs], kappa_ref)
    for k in range(slabs):
        scaled_ref[k] = source_ref[k] * scale


def inner_kernel(
    freqs,
    cols,
    spectra_ref,
    scaled_ref,
    own_gain_ref,
    far_y_ref,
    near_y_ref,
    kappa_ref,
    sums_ref,
    halo_ref,
    wide,
    gain,
    one,
    two,
):
    _, _, cells_x, cells_y, all_sensors = spectra_ref.shape
    cells = cells_x * cells_y
    slabs, rows, _ = scaled_ref.shape
    stride = rows // cells_x
    start = 2 * stride
    after, before = by_side("sy", far_y_ref[...].astype(F32), near_y_ref[...].astype(F32))
    gain[start - 8 : start] = jnp.zeros((8, LANES), F32)
    gain[start : start + rows] = own_gain_ref[...]
    for k in range(slabs):
        wide[k, start - 8 : start] = jnp.zeros((8, LANES), F32)
        wide[k, start : start + rows] = scaled_ref[k]
    for side, halo in ((0, before), (1, after)):
        scale, halo_ref[side, slabs] = coefficients(halo[:, slabs * LANES :], kappa_ref)
        for k in range(slabs):
            halo_ref[side, k] = halo[:, k * LANES : (k + 1) * LANES] * scale
        for j in range(DEPTH):
            part = slice(j * cells_x, (j + 1) * cells_x)
            to = pl.ds(start + j + (cells_y if side else -DEPTH), cells_x, stride=stride)
            gain[to, :] = halo_ref[side, slabs, part]
            for k in range(slabs):
                wide[k, to, :] = halo_ref[side, k, part]
    turned = []
    for k in range(slabs):
        old, new = wide.at[k], one.at[k]
        for x in range(1, DEPTH + 1):
            first, last = start + x * stride - 8, start + rows - x * stride
            sweep(wide.at[k], gain, old, new, first, last, stride)
            old, new = new, (two.at[k] if x % 2 else one.at[k])
        inner = old[start + DEPTH * stride : start + rows - DEPTH * stride]
        inner = inner.reshape(cells_x - 2 * DEPTH, stride, LANES)[:, 0:cells_y]
        edge = jnp.zeros((DEPTH * cells_y, LANES), F32)
        turned.append(
            jnp.concatenate([edge, inner.reshape(cells - 2 * DEPTH * cells_y, LANES), edge], axis=0).T
        )
    forms = both_forms(jnp.concatenate(turned, axis=0), cols)
    groups = forms.shape[0] // freqs
    for f in range(freqs):
        right = spectra_ref[f].reshape(2 * cells, all_sensors)
        got = jnp.dot(rows_of(forms, f, freqs), right, preferred_element_type=F32)
        for g in range(groups):
            at = (g * freqs + f) * 2 * cols
            sums_ref[at : at + 2 * cols] = got[g * 2 * cols : (g + 1) * 2 * cols]


def field_kernel(
    freqs,
    cols,
    spectra_ref,
    scaled_ref,
    own_gain_ref,
    halo_ref,
    sums_ref,
    far_x_ref,
    near_x_ref,
    kappa_ref,
    keep_ref,
    send_ref,
    wide,
    gain,
    one,
    two,
    sums,
):
    _, _, cells_x, cells_y, all_sensors = spectra_ref.shape
    slabs, rows, _ = scaled_ref.shape
    stride = rows // cells_x
    start = stride + 8
    deep = 2 * DEPTH

    def base(x):
        return start + x * stride

    below, above = by_side("sx", far_x_ref[...].astype(F32), near_x_ref[...].astype(F32))
    for end in range(2):
        own, outer = (DEPTH, 0) if end == 0 else (0, deep)
        inside = 0 if end == 0 else cells_x - deep
        beyond = above if end == 0 else below
        scale, beyond_gain = coefficients(beyond[:, slabs * LANES :], kappa_ref)
        for k in range(slabs + 1):
            to = wide.at[end, k] if k < slabs else gain.at[end]
            inner = scaled_ref.at[k] if k < slabs else own_gain_ref
            to[base(0) - 8 : base(0)] = jnp.zeros((8, LANES), F32)
            to[base(3 * DEPTH) - 8 : base(3 * DEPTH)] = jnp.zeros((8, LANES), F32)
            to[base(own) : base(own + deep)] = inner[inside * stride : (inside + deep) * stride]
            for j in range(DEPTH):
                part = slice(j * cells_x + inside, j * cells_x + inside + deep)
                to[pl.ds(base(own) - DEPTH + j, deep, stride=stride), :] = halo_ref[0, k, part]
                to[pl.ds(base(own) + cells_y + j, deep, stride=stride), :] = halo_ref[1, k, part]
            to[base(outer) - DEPTH : base(outer + DEPTH) - DEPTH] = (
                beyond[:, k * LANES : (k + 1) * LANES] * scale if k < slabs else beyond_gain
            )
    turned = []
    filler = -(deep * cells_y) % LANES
    for k in range(slabs):
        fields = []
        for end in range(2):
            source = wide.at[end, k]
            old, new = source, one.at[end, k]
            for x in range(1, DEPTH + 1):
                sweep(source, gain.at[end], old, new, base(x) - 8, base(3 * DEPTH - x), stride)
                old, new = new, (two.at[end, k] if x % 2 else one.at[end, k])
            field = old[base(DEPTH) : base(deep)].reshape(DEPTH, stride, LANES)[:, 0:cells_y]
            fields.append(field.reshape(DEPTH * cells_y, LANES))
        fields.append(jnp.zeros((filler, LANES), F32))
        turned.append(jnp.concatenate(fields, axis=0).T)
    forms = both_forms(jnp.concatenate(turned, axis=0), cols)
    groups = forms.shape[0] // freqs
    blank = jnp.zeros((filler, all_sensors), BF16)
    for f in range(freqs):
        right = []
        for part in range(2):
            for x in (0, cells_x - DEPTH):
                rows_here = spectra_ref[f, part, x : x + DEPTH]
                right.append(rows_here.reshape(DEPTH * cells_y, all_sensors))
            right.append(blank)
        got = jnp.dot(
            rows_of(forms, f, freqs), jnp.concatenate(right, axis=0), preferred_element_type=F32
        )
        for g in range(groups):
            at = (g * freqs + f) * 2 * cols
            sums[at : at + 2 * cols] = sums_ref[at : at + 2 * cols] + got[g * 2 * cols : (g + 1) * 2 * cols]
    back = sums[...].T
    halves, _, sensors, block = keep_ref.shape
    for g in range(groups):
        pair = back[:, g * block : (g + 1) * block].reshape(halves, 2, sensors, block)
        keep, send = by_parity("sy", pair[:, 0], pair[:, 1])
        keep_ref[:, g] = keep
        send_ref[:, g] = send.astype(BF16)


def residual_kernel(
    terms_ref,
    table_ref,
    noise_ref,
    solution_ref,
    residual_ref,
    direction_ref,
    step_ref,
    new_solution_ref,
    new_residual_ref,
    norm_ref,
):
    cols, sensors, steps = direction_ref.shape
    parts = []
    for b in range(terms_ref.shape[1]):
        parts.append(jnp.sum(terms_ref[:, b].astype(F32), axis=0))
    spectrum = jnp.concatenate(parts, axis=1)
    col_of = lane_ids(spectrum.shape[1]) % cols
    left = jnp.concatenate([jnp.where(col_of == c, spectrum, 0.0) for c in range(cols)], axis=0)
    returned = jnp.dot(left, table_ref[...], precision=HIGHEST, preferred_element_type=F32)
    lane = lane_ids(LANES)
    norms = jnp.zeros((1, LANES), F32)
    for c in range(cols):
        product = direction_ref[c] + noise_ref[...] * returned[c * sensors : (c + 1) * sensors]
        new_residual = residual_ref[c] - step_ref[c] * product
        new_residual_ref[c] = new_residual
        new_solution_ref[c] = solution_ref[c] + step_ref[c] * direction_ref[c]
        norm = jnp.sum(
            jnp.sum(new_residual * new_residual, axis=0, keepdims=True), axis=1, keepdims=True
        )
        norms = jnp.where(lane == c, norm, norms)
    norm_ref[...] = jnp.broadcast_to(norms[None], norm_ref.shape)


def direction_kernel(
    norms_ref,
    solution_ref,
    residual_ref,
    direction_ref,
    old_ref,
    solution_out,
    residual_out,
    direction_out,
    norm_out,
    held,
    norm_ref,
    sems,
):
    cols, sensors, steps = direction_ref.shape
    early = [
        pltpu.make_async_copy(solution_ref, solution_out, sems.at[0]),
        pltpu.make_async_copy(residual_ref, residual_out, sems.at[1]),
    ]
    for copy in early:
        copy.start()
    norm = jnp.sum(norms_ref[...], axis=0)
    norm_ref[...] = norm[0, 0:cols]
    final = pltpu.make_async_copy(norm_ref, norm_out, sems.at[3])
    final.start()
    for c in range(cols):
        held[c] = residual_ref[c] + (norm[:, c : c + 1] / old_ref[c]) * direction_ref[c]
    last = pltpu.make_async_copy(held, direction_out, sems.at[2])
    last.start()
    for copy in (*early, last, final):
        copy.wait()


def swap(axis, toward_partner, toward_other):
    count = lax.axis_size(axis)
    near = [(i, i ^ 1) for i in range(count) if (i ^ 1) < count]
    far = [(i, i + 1 if i % 2 else i - 1) for i in range(1, count - 1 + count % 2)]
    second = lax.ppermute(toward_other, axis, far)
    first = lax.ppermute(toward_partner, axis, near)
    return first, second


def partners(axis):
    return [(i, i ^ 1) for i in range(lax.axis_size(axis))]


def exchange_half(blocks):
    sx, sy, fq = (lax.axis_size(axis) for axis in ALL_AXES)
    groups = [
        [(x * sy + y) * fq + f for x in range(sx) for y in range(parity, sy, 2) for f in range(fq)]
        for parity in range(2)
    ]
    flat = blocks.reshape((-1,) + blocks.shape[2:])
    return lax.all_to_all(flat, ALL_AXES, 0, 0, axis_index_groups=groups, tiled=True).reshape(
        blocks.shape
    )


def on_device(
    spectra,
    noise_weight,
    class_map,
    class_kappa,
    solution,
    residual,
    direction,
    step_length,
    old_norm,
):
    local_freqs, _, cells_x, cells_y, all_sensors = spectra.shape
    cols, sensors, steps = direction.shape
    fq_blocks = lax.axis_size("fq")
    tiles = lax.axis_size("sx") * lax.axis_size("sy")
    halves = tiles // 2
    block = 2 * local_freqs * cols
    lanes = block * fq_blocks
    forward, inverse = tables(local_freqs * fq_blocks, local_freqs, cols, steps)
    group = 2 if fq_blocks % 2 == 0 else 1
    chunks = fq_blocks // group
    width = group * block
    stride = cells_y + 8
    wide = width + LANES
    cells = cells_x * cells_y

    like = jax.ShapeDtypeStruct(direction.shape, F32)
    held = pltpu.VMEM(direction.shape, F32)
    spec = pl.pallas_call(
        functools.partial(spectrum_kernel, halves, fq_blocks),
        out_shape=jax.ShapeDtypeStruct((halves, fq_blocks, sensors, block), BF16),
        in_specs=[HBM] * 3,
        out_specs=VMEM,
        scratch_shapes=[
            held,
            pltpu.VMEM(noise_weight.shape, F32),
            pltpu.VMEM(forward.shape, F32),
            pltpu.SemaphoreType.DMA((3,)),
        ],
        compiler_params=params(62),
        cost_estimate=pl.CostEstimate(
            flops=2 * spectra.size, bytes_accessed=4 * spectra.size, transcendentals=0
        ),
        name="spectrum",
    )(direction, noise_weight, forward)
    mine = exchange_half(spec)
    other = lax.ppermute(mine, "sy", partners("sy"))

    edge = jax.ShapeDtypeStruct((DEPTH * cells_x, wide), BF16)
    end = jax.ShapeDtypeStruct((DEPTH * stride, wide), BF16)
    total = (cells_x + 4) * stride
    strip = (3 * DEPTH + 2) * stride + 16
    slabs = width // LANES
    pieces = []
    for i in range(chunks):
        at = slice(i * group, (i + 1) * group)
        stacked = pl.pallas_call(
            functools.partial(order_kernel, cols),
            out_shape=jax.ShapeDtypeStruct((2 * all_sensors, width), BF16),
            in_specs=[HBM, VMEM, VMEM],
            out_specs=VMEM,
            compiler_params=params(48),
            cost_estimate=pl.CostEstimate(
                flops=2 * spectra.size, bytes_accessed=4 * spectra.size, transcendentals=0
            ),
            name="order",
        )(spectra, mine[:, at], other[:, at])
        source, far_y, near_y, ends = pl.pallas_call(
            functools.partial(adjoint_kernel, local_freqs, cols),
            out_shape=(
                jax.ShapeDtypeStruct((slabs + 1, cells_x * stride, LANES), F32),
                edge,
                edge,
                jax.ShapeDtypeStruct((2, DEPTH * stride, wide), F32),
            ),
            in_specs=[VMEM] * 3,
            out_specs=(VMEM,) * 4,
            compiler_params=params(),
            name="adjoint",
        )(spectra, stacked, class_map.T)
        near_y, far_y = swap("sy", near_y, far_y)
        far_x, near_x = pl.pallas_call(
            ends_kernel,
            out_shape=(end, end),
            in_specs=[VMEM] * 3,
            out_specs=(VMEM,) * 2,
            scratch_shapes=[pltpu.VMEM((DEPTH * stride + 16, wide), F32)],
            compiler_params=params(),
            name="ends",
        )(ends, far_y, near_y)
        near_x, far_x = swap("sx", near_x, far_x)
        scaled, own_gain = pl.pallas_call(
            own_kernel,
            out_shape=(
                jax.ShapeDtypeStruct((slabs, cells_x * stride, LANES), F32),
                jax.ShapeDtypeStruct((cells_x * stride, LANES), F32),
            ),
            in_specs=[VMEM, SMEM],
            out_specs=(VMEM,) * 2,
            compiler_params=params(),
            name="own",
        )(source, class_kappa)
        sums, halo = pl.pallas_call(
            functools.partial(inner_kernel, local_freqs, cols),
            out_shape=(
                jax.ShapeDtypeStruct((width, all_sensors), F32),
                jax.ShapeDtypeStruct((2, slabs + 1, DEPTH * cells_x, LANES), F32),
            ),
            in_specs=[VMEM] * 5 + [SMEM],
            out_specs=(VMEM,) * 2,
            scratch_shapes=[
                pltpu.VMEM((slabs, total, LANES), F32),
                pltpu.VMEM((total, LANES), F32),
                pltpu.VMEM((slabs, total, LANES), F32),
                pltpu.VMEM((slabs, total, LANES), F32),
            ],
            compiler_params=params(),
            cost_estimate=pl.CostEstimate(
                flops=4 * spectra.size * width, bytes_accessed=2 * spectra.size, transcendentals=0
            ),
            name="inner",
        )(spectra, scaled, own_gain, far_y, near_y, class_kappa)
        pieces.append(
            pl.pallas_call(
                functools.partial(field_kernel, local_freqs, cols),
                out_shape=(
                    jax.ShapeDtypeStruct((halves, group, sensors, block), F32),
                    jax.ShapeDtypeStruct((halves, group, sensors, block), BF16),
                ),
                in_specs=[VMEM] * 7 + [SMEM],
                out_specs=(VMEM,) * 2,
                scratch_shapes=[
                    pltpu.VMEM((2, slabs, strip, LANES), F32),
                    pltpu.VMEM((2, strip, LANES), F32),
                    pltpu.VMEM((2, slabs, strip, LANES), F32),
                    pltpu.VMEM((2, slabs, strip, LANES), F32),
                    pltpu.VMEM((width, all_sensors), F32),
                ],
                compiler_params=params(),
                name="field",
            )(spectra, scaled, own_gain, halo, sums, far_x, near_x, class_kappa)
        )
    keep = jnp.concatenate([piece[0] for piece in pieces], axis=1)
    send = jnp.concatenate([piece[1] for piece in pieces], axis=1)
    taken = lax.ppermute(send, "sy", partners("sy"))
    terms = exchange_half((keep + taken.astype(F32)).astype(BF16))
    new_solution, new_residual, norms = pl.pallas_call(
        residual_kernel,
        out_shape=(like, like, jax.ShapeDtypeStruct((tiles, 1, LANES), F32)),
        in_specs=[VMEM] * 6 + [SMEM],
        out_specs=(VMEM,) * 3,
        compiler_params=params(),
        name="residual",
    )(terms, inverse, noise_weight, solution, residual, direction, step_length)
    norms = lax.all_to_all(norms, GRID_AXES, 0, 0, tiled=True)
    new_solution, new_residual, new_direction, new_norm = pl.pallas_call(
        direction_kernel,
        out_shape=(like, like, like, jax.ShapeDtypeStruct((cols,), F32)),
        in_specs=[VMEM] * 4 + [SMEM],
        out_specs=(HBM,) * 4,
        scratch_shapes=[held, pltpu.VMEM((cols,), F32), pltpu.SemaphoreType.DMA((4,))],
        compiler_params=params(),
        name="direction",
    )(norms, new_solution, new_residual, direction, old_norm)
    return (new_solution, new_residual, new_direction, new_norm)


def solution(mesh):
    return jax.shard_map(
        on_device,
        mesh=mesh,
        in_specs=(
            P("fq", None, "sx", "sy", None),
            P(("sx", "sy"), None),
            P("sx", "sy"),
            P(),
            P("fq", ("sx", "sy"), None),
            P("fq", ("sx", "sy"), None),
            P("fq", ("sx", "sy"), None),
            P("fq"),
            P("fq"),
        ),
        out_specs=(
            P("fq", ("sx", "sy"), None),
            P("fq", ("sx", "sy"), None),
            P("fq", ("sx", "sy"), None),
            P("fq"),
        ),
        check_vma=False,
    )
```

```python
import functools
import math

import jax
import jax.numpy as jnp
from jax import lax
from jax.experimental import pallas as pl
from jax.experimental.pallas import tpu as pltpu
from jax.sharding import PartitionSpec as P
import numpy as np

SWEEPS = 4
DEPTH = SWEEPS - 1
HIGHEST = lax.Precision.HIGHEST
F32 = jnp.float32
BF16 = jnp.bfloat16
GRID_AXES = ("sx", "sy")
ALL_AXES = ("sx", "sy", "fq")
LANES = 128
MIB = 1024 * 1024
VMEM = pl.BlockSpec(memory_space=pltpu.VMEM)
SMEM = pl.BlockSpec(memory_space=pltpu.SMEM)
HBM = pl.BlockSpec(memory_space=pltpu.HBM)
ANY = pl.BlockSpec(memory_space=pl.ANY)


def params(mib=24):
    return pltpu.CompilerParams(vmem_limit_bytes=mib * MIB)


def tables(freq_count, local_freqs, local_cols, time_steps):
    freq = np.arange(freq_count)[:, None]
    step = np.arange(time_steps)[None, :]
    phases = (freq * step % time_steps) * (2.0 * math.pi / time_steps)
    factor = 1.0 / math.sqrt(time_steps)
    pair = np.stack([np.cos(phases) * factor, -np.sin(phases) * factor], 1)
    forward = np.repeat(pair.reshape(2 * freq_count, time_steps), local_cols, 0)
    doubling = np.where(np.arange(freq_count) == 0, 1.0, 2.0)[:, None, None]
    inverse = np.repeat((pair * doubling).reshape(2 * freq_count, time_steps), local_cols, 0)
    return forward.T.astype(np.float32), inverse.astype(np.float32)


def by_side(axis, low, high):
    even = lax.axis_index(axis) % 2 == 0
    return jnp.where(even, high, low), jnp.where(even, low, high)


def by_parity(axis, mine, other):
    even = lax.axis_index(axis) % 2 == 0
    return jnp.where(even, mine, other), jnp.where(even, other, mine)


def lane_ids(lanes):
    return lax.broadcasted_iota(jnp.int32, (1, lanes), 1)


def fetch_all(pairs, sems):
    copies = [pltpu.make_async_copy(a, b, sems.at[i]) for i, (a, b) in enumerate(pairs)]
    for copy in copies:
        copy.start()
    for copy in copies:
        copy.wait()


def spectrum_kernel(
    tiles, fq_blocks, direction_in, noise_in, table_in, out_ref, direction_ref, noise_ref, table_ref, sems
):
    fetch_all(
        ((direction_in, direction_ref), (noise_in, noise_ref), (table_in, table_ref)), sems
    )
    cols, sensors, steps = direction_ref.shape
    lanes = table_ref.shape[1]
    weighted = (noise_ref[...][None] * direction_ref[...]).reshape(cols * sensors, steps)
    full = jnp.dot(weighted, table_ref[...], precision=HIGHEST, preferred_element_type=F32)
    col_of = lane_ids(lanes) % cols
    spec = full[0:sensors]
    for col in range(1, cols):
        spec = jnp.where(col_of == col, full[col * sensors : (col + 1) * sensors], spec)
    spec = spec.astype(BF16)
    block = lanes // fq_blocks
    for b in range(fq_blocks):
        part = spec[:, b * block : (b + 1) * block]
        out_ref[:, b] = jnp.broadcast_to(part[None], (tiles, sensors, block))


def class_kernel(class_ref, after_ref, out_ref):
    cells_y, cells_x = class_ref.shape
    cells = cells_x * cells_y
    row = lax.broadcasted_iota(jnp.int32, (cells, cells_x), 0)
    pick = (row // cells_y == lax.broadcasted_iota(jnp.int32, (cells, cells_x), 1)).astype(F32)
    by_row = lax.dot_general(
        pick,
        class_ref[...].astype(F32) + 1.0,
        (((1,), (1,)), ((), ())),
        preferred_element_type=F32,
    )
    at = lax.broadcasted_iota(jnp.int32, (cells, cells_y), 0) % cells_y
    own = (at == lax.broadcasted_iota(jnp.int32, (cells, cells_y), 1)).astype(F32)
    out_ref[...] = jnp.dot(
        by_row * own, jnp.ones((cells_y, LANES), F32), preferred_element_type=F32
    )


def adjoint_of(part, stacked):
    _, cells_x, cells_y, all_sensors = part.shape
    both = part.reshape(2, cells_x * cells_y, all_sensors)
    both = jnp.concatenate([both[0], both[1]], axis=1)
    return jnp.dot(both, stacked, preferred_element_type=F32)


def freq_lanes(lanes, cols, freqs):
    return (lane_ids(lanes) // (2 * cols)) % freqs


def order_kernel(cols, spectra_in, mine_ref, other_ref, stacked_ref):
    halves, group, sensors, block = mine_ref.shape
    lanes = group * block
    parts = []
    for b in range(group):
        pair = by_parity("sy", mine_ref[:, b], other_ref[:, b])
        parts.append(jnp.stack(pair, axis=1).reshape(2 * halves * sensors, block))
    direct = jnp.concatenate(parts, axis=1)
    wide = direct.astype(F32)
    is_real = (lane_ids(lanes) // cols) % 2 == 0
    turned = jnp.where(
        is_real, pltpu.roll(wide, lanes - cols, 1), -pltpu.roll(wide, cols, 1)
    ).astype(BF16)
    stacked_ref[...] = jnp.concatenate([direct, turned], axis=0)


def adjoint_kernel(
    freqs, cols, spectra_ref, stacked_ref, class_ref, out_ref, far_ref, near_ref, ends_ref
):
    _, _, cells_x, cells_y, all_sensors = spectra_ref.shape
    stride = out_ref.shape[1] // cells_x
    lanes = stacked_ref.shape[1]
    freq_of = freq_lanes(lanes, cols, freqs)
    stacked = stacked_ref[...]
    acc = adjoint_of(spectra_ref[0], stacked)
    for f in range(1, freqs):
        acc = jnp.where(freq_of == f, adjoint_of(spectra_ref[f], stacked), acc)
    for k in range(out_ref.shape[0]):
        part = class_ref[...] if k * LANES == lanes else acc[:, k * LANES : (k + 1) * LANES]
        for x in range(cells_x):
            base = x * stride
            out_ref[k, base : base + cells_y] = part[x * cells_y : (x + 1) * cells_y]
            out_ref[k, base + cells_y : base + stride] = jnp.zeros((stride - cells_y, LANES), F32)
        at = slice(k * LANES, (k + 1) * LANES)
        for j in range(DEPTH):
            low = out_ref[k, pl.ds(j, cells_x, stride=stride), :]
            high = out_ref[k, pl.ds(cells_y - DEPTH + j, cells_x, stride=stride), :]
            near, far = by_side("sy", low, high)
            near_ref[j * cells_x : (j + 1) * cells_x, at] = near.astype(BF16)
            far_ref[j * cells_x : (j + 1) * cells_x, at] = far.astype(BF16)
        ends_ref[0, :, at] = out_ref[k, 0 : DEPTH * stride]
        ends_ref[1, :, at] = out_ref[k, (cells_x - DEPTH) * stride : cells_x * stride]


def ends_kernel(ends_ref, far_ref, near_ref, far_out, near_out, held):
    span = ends_ref.shape[1]
    stride = span // DEPTH
    cells_x = near_ref.shape[0] // DEPTH
    cells_y = stride - 8
    after, before = by_side("sy", far_ref[...].astype(F32), near_ref[...].astype(F32))
    built = []
    for side in range(2):
        held[...] = jnp.zeros_like(held)
        held[8 : 8 + span] = ends_ref[side]
        first = 0 if side == 0 else cells_x - DEPTH
        for x in range(DEPTH):
            for j in range(DEPTH):
                take = j * cells_x + first + x
                to = 8 + x * stride
                held[to + cells_y + j : to + cells_y + j + 1] = after[take : take + 1]
                held[to - DEPTH + j : to - DEPTH + j + 1] = before[take : take + 1]
        built.append(held[8 - DEPTH : 8 - DEPTH + span])
    near, far = by_side("sx", built[0], built[1])
    near_out[...] = near.astype(BF16)
    far_out[...] = far.astype(BF16)


def coefficients(classes, kappa_ref):
    kappa = jnp.zeros_like(classes)
    for n in range(kappa_ref.shape[0]):
        kappa = jnp.where(classes == n + 1.0, kappa_ref[n], kappa)
    scale = jnp.where(classes > 0.0, 1.0 / (1.0 + 4.0 * kappa), 0.0)
    return scale, kappa * scale


def sweep(source, gain, old, new, first, last, stride):
    near = (
        old[first - stride : last - stride]
        + old[first + stride : last + stride]
        + old[first - 1 : last - 1]
        + old[first + 1 : last + 1]
    )
    new[first:last] = source[first:last] + gain[first:last] * near


def both_forms(turned, cols):
    blocks, cells = turned.shape[0] // (2 * cols), turned.shape[1]
    pair = turned.reshape(blocks, 2, cols, cells)
    plain = pair.astype(BF16).reshape(blocks, 2 * cols, cells)
    crossed = jnp.stack([-pair[:, 1], pair[:, 0]], axis=1)
    crossed = crossed.astype(BF16).reshape(blocks, 2 * cols, cells)
    return jnp.concatenate([plain, crossed], axis=2)


def rows_of(forms, f, freqs):
    return jnp.concatenate([forms[b] for b in range(f, forms.shape[0], freqs)], axis=0)


def own_kernel(source_ref, kappa_ref, scaled_ref, gain_ref):
    slabs = scaled_ref.shape[0]
    scale, gain_ref[...] = coefficients(source_ref[slabs], kappa_ref)
    for k in range(slabs):
        scaled_ref[k] = source_ref[k] * scale


def inner_kernel(
    freqs,
    cols,
    spectra_ref,
    scaled_ref,
    own_gain_ref,
    far_y_ref,
    near_y_ref,
    kappa_ref,
    sums_ref,
    wide,
    gain,
    one,
    two,
):
    _, _, cells_x, cells_y, all_sensors = spectra_ref.shape
    cells = cells_x * cells_y
    slabs, rows, _ = scaled_ref.shape
    stride = rows // cells_x
    start = 2 * stride
    after, before = by_side("sy", far_y_ref[...].astype(F32), near_y_ref[...].astype(F32))
    gain[start - 8 : start] = jnp.zeros((8, LANES), F32)
    gain[start : start + rows] = own_gain_ref[...]
    for k in range(slabs):
        wide[k, start - 8 : start] = jnp.zeros((8, LANES), F32)
        wide[k, start : start + rows] = scaled_ref[k]
    for side, halo in ((0, before), (1, after)):
        scale, halo_gain = coefficients(halo[:, slabs * LANES :], kappa_ref)
        scaled = [halo[:, k * LANES : (k + 1) * LANES] * scale for k in range(slabs)]
        for j in range(DEPTH):
            part = slice(j * cells_x, (j + 1) * cells_x)
            to = pl.ds(start + j + (cells_y if side else -DEPTH), cells_x, stride=stride)
            gain[to, :] = halo_gain[part]
            for k in range(slabs):
                wide[k, to, :] = scaled[k][part]
    turned = []
    for k in range(slabs):
        old, new = wide.at[k], one.at[k]
        for x in range(1, DEPTH + 1):
            first, last = start + x * stride - 8, start + rows - x * stride
            sweep(wide.at[k], gain, old, new, first, last, stride)
            old, new = new, (two.at[k] if x % 2 else one.at[k])
        inner = old[start + DEPTH * stride : start + rows - DEPTH * stride]
        inner = inner.reshape(cells_x - 2 * DEPTH, stride, LANES)[:, 0:cells_y]
        edge = jnp.zeros((DEPTH * cells_y, LANES), F32)
        turned.append(
            jnp.concatenate([edge, inner.reshape(cells - 2 * DEPTH * cells_y, LANES), edge], axis=0).T
        )
    forms = both_forms(jnp.concatenate(turned, axis=0), cols)
    groups = forms.shape[0] // freqs
    for f in range(freqs):
        right = spectra_ref[f].reshape(2 * cells, all_sensors)
        got = jnp.dot(rows_of(forms, f, freqs), right, preferred_element_type=F32)
        for g in range(groups):
            at = (g * freqs + f) * 2 * cols
            sums_ref[at : at + 2 * cols] = got[g * 2 * cols : (g + 1) * 2 * cols]


def field_kernel(
    freqs,
    cols,
    spectra_ref,
    wide_ref,
    gain_ref,
    sums_ref,
    far_x_ref,
    near_x_ref,
    kappa_ref,
    keep_ref,
    send_ref,
    wide,
    gain,
    one,
    two,
    sums,
):
    _, _, cells_x, cells_y, all_sensors = spectra_ref.shape
    slabs = wide_ref.shape[0]
    stride = far_x_ref.shape[0] // DEPTH
    start = stride + 8
    deep = 2 * DEPTH

    def base(x):
        return start + x * stride

    below, above = by_side("sx", far_x_ref[...].astype(F32), near_x_ref[...].astype(F32))
    for end in range(2):
        own, outer = (DEPTH, 0) if end == 0 else (0, deep)
        inside = 0 if end == 0 else cells_x - deep
        beyond = above if end == 0 else below
        scale, beyond_gain = coefficients(beyond[:, slabs * LANES :], kappa_ref)
        for k in range(slabs + 1):
            to = wide.at[end, k] if k < slabs else gain.at[end]
            inner = wide_ref.at[k] if k < slabs else gain_ref
            first = (2 + inside) * stride
            to[base(0) - 8 : base(0)] = jnp.zeros((8, LANES), F32)
            to[base(3 * DEPTH) - 8 : base(3 * DEPTH)] = jnp.zeros((8, LANES), F32)
            to[base(own) - 8 : base(own + deep)] = inner[first - 8 : first + deep * stride]
            to[base(outer) - DEPTH : base(outer + DEPTH) - DEPTH] = (
                beyond[:, k * LANES : (k + 1) * LANES] * scale if k < slabs else beyond_gain
            )
    turned = []
    filler = -(deep * cells_y) % LANES
    for k in range(slabs):
        fields = []
        for end in range(2):
            source = wide.at[end, k]
            old, new = source, one.at[end, k]
            for x in range(1, DEPTH + 1):
                sweep(source, gain.at[end], old, new, base(x) - 8, base(3 * DEPTH - x), stride)
                old, new = new, (two.at[end, k] if x % 2 else one.at[end, k])
            field = old[base(DEPTH) : base(deep)].reshape(DEPTH, stride, LANES)[:, 0:cells_y]
            fields.append(field.reshape(DEPTH * cells_y, LANES))
        fields.append(jnp.zeros((filler, LANES), F32))
        turned.append(jnp.concatenate(fields, axis=0).T)
    forms = both_forms(jnp.concatenate(turned, axis=0), cols)
    groups = forms.shape[0] // freqs
    blank = jnp.zeros((filler, all_sensors), BF16)
    for f in range(freqs):
        right = []
        for part in range(2):
            for x in (0, cells_x - DEPTH):
                rows_here = spectra_ref[f, part, x : x + DEPTH]
                right.append(rows_here.reshape(DEPTH * cells_y, all_sensors))
            right.append(blank)
        got = jnp.dot(
            rows_of(forms, f, freqs), jnp.concatenate(right, axis=0), preferred_element_type=F32
        )
        for g in range(groups):
            at = (g * freqs + f) * 2 * cols
            sums[at : at + 2 * cols] = sums_ref[at : at + 2 * cols] + got[g * 2 * cols : (g + 1) * 2 * cols]
    back = sums[...].T
    halves, _, sensors, block = keep_ref.shape
    for g in range(groups):
        pair = back[:, g * block : (g + 1) * block].reshape(halves, 2, sensors, block)
        keep, send = by_parity("sy", pair[:, 0], pair[:, 1])
        keep_ref[:, g] = keep
        send_ref[:, g] = send.astype(BF16)


def residual_kernel(
    terms_ref,
    table_ref,
    noise_ref,
    solution_ref,
    residual_ref,
    direction_ref,
    step_ref,
    new_solution_ref,
    new_residual_ref,
    norm_ref,
):
    cols, sensors, steps = direction_ref.shape
    parts = []
    for b in range(terms_ref.shape[1]):
        parts.append(jnp.sum(terms_ref[:, b].astype(F32), axis=0))
    spectrum = jnp.concatenate(parts, axis=1)
    col_of = lane_ids(spectrum.shape[1]) % cols
    left = jnp.concatenate([jnp.where(col_of == c, spectrum, 0.0) for c in range(cols)], axis=0)
    returned = jnp.dot(left, table_ref[...], precision=HIGHEST, preferred_element_type=F32)
    lane = lane_ids(LANES)
    norms = jnp.zeros((1, LANES), F32)
    for c in range(cols):
        product = direction_ref[c] + noise_ref[...] * returned[c * sensors : (c + 1) * sensors]
        new_residual = residual_ref[c] - step_ref[c] * product
        new_residual_ref[c] = new_residual
        new_solution_ref[c] = solution_ref[c] + step_ref[c] * direction_ref[c]
        norm = jnp.sum(
            jnp.sum(new_residual * new_residual, axis=0, keepdims=True), axis=1, keepdims=True
        )
        norms = jnp.where(lane == c, norm, norms)
    norm_ref[...] = jnp.broadcast_to(norms[None], norm_ref.shape)


def direction_kernel(
    norms_ref,
    solution_ref,
    residual_ref,
    direction_ref,
    old_ref,
    solution_out,
    residual_out,
    direction_out,
    norm_out,
    held,
    norm_ref,
    sems,
):
    cols, sensors, steps = direction_ref.shape
    early = [
        pltpu.make_async_copy(solution_ref, solution_out, sems.at[0]),
        pltpu.make_async_copy(residual_ref, residual_out, sems.at[1]),
    ]
    for copy in early:
        copy.start()
    norm = jnp.sum(norms_ref[...], axis=0)
    norm_ref[...] = norm[0, 0:cols]
    final = pltpu.make_async_copy(norm_ref, norm_out, sems.at[3])
    final.start()
    for c in range(cols):
        held[c] = residual_ref[c] + (norm[:, c : c + 1] / old_ref[c]) * direction_ref[c]
    last = pltpu.make_async_copy(held, direction_out, sems.at[2])
    last.start()
    for copy in (*early, last, final):
        copy.wait()


def swap(axis, toward_partner, toward_other):
    count = lax.axis_size(axis)
    near = [(i, i ^ 1) for i in range(count) if (i ^ 1) < count]
    far = [(i, i + 1 if i % 2 else i - 1) for i in range(1, count - 1 + count % 2)]
    second = lax.ppermute(toward_other, axis, far)
    first = lax.ppermute(toward_partner, axis, near)
    return first, second


def partners(axis):
    return [(i, i ^ 1) for i in range(lax.axis_size(axis))]


def exchange_half(blocks):
    sx, sy, fq = (lax.axis_size(axis) for axis in ALL_AXES)
    groups = [
        [(x * sy + y) * fq + f for x in range(sx) for y in range(parity, sy, 2) for f in range(fq)]
        for parity in range(2)
    ]
    flat = blocks.reshape((-1,) + blocks.shape[2:])
    return lax.all_to_all(flat, ALL_AXES, 0, 0, axis_index_groups=groups, tiled=True).reshape(
        blocks.shape
    )


def on_device(
    spectra,
    noise_weight,
    class_map,
    class_kappa,
    solution,
    residual,
    direction,
    step_length,
    old_norm,
):
    local_freqs, _, cells_x, cells_y, all_sensors = spectra.shape
    cols, sensors, steps = direction.shape
    fq_blocks = lax.axis_size("fq")
    tiles = lax.axis_size("sx") * lax.axis_size("sy")
    halves = tiles // 2
    block = 2 * local_freqs * cols
    lanes = block * fq_blocks
    forward, inverse = tables(local_freqs * fq_blocks, local_freqs, cols, steps)
    group = 2 if fq_blocks % 2 == 0 else 1
    chunks = fq_blocks // group
    width = group * block
    stride = cells_y + 8
    wide = width + LANES
    cells = cells_x * cells_y

    like = jax.ShapeDtypeStruct(direction.shape, F32)
    held = pltpu.VMEM(direction.shape, F32)
    spec = pl.pallas_call(
        functools.partial(spectrum_kernel, halves, fq_blocks),
        out_shape=jax.ShapeDtypeStruct((halves, fq_blocks, sensors, block), BF16),
        in_specs=[HBM] * 3,
        out_specs=VMEM,
        scratch_shapes=[
            held,
            pltpu.VMEM(noise_weight.shape, F32),
            pltpu.VMEM(forward.shape, F32),
            pltpu.SemaphoreType.DMA((3,)),
        ],
        compiler_params=params(62),
        cost_estimate=pl.CostEstimate(
            flops=2 * spectra.size, bytes_accessed=4 * spectra.size, transcendentals=0
        ),
        name="spectrum",
    )(direction, noise_weight, forward)
    mine = exchange_half(spec)
    other = lax.ppermute(mine, "sy", partners("sy"))
    classes = pl.pallas_call(
        class_kernel,
        out_shape=jax.ShapeDtypeStruct((cells, LANES), F32),
        in_specs=[VMEM, ANY],
        out_specs=VMEM,
        compiler_params=params(),
        name="classes",
    )(class_map.T, mine)

    edge = jax.ShapeDtypeStruct((DEPTH * cells_x, wide), BF16)
    end = jax.ShapeDtypeStruct((DEPTH * stride, wide), BF16)
    total = (cells_x + 4) * stride
    strip = (3 * DEPTH + 2) * stride + 16
    slabs = width // LANES
    pieces = []
    for i in range(chunks):
        at = slice(i * group, (i + 1) * group)
        stacked = pl.pallas_call(
            functools.partial(order_kernel, cols),
            out_shape=jax.ShapeDtypeStruct((2 * all_sensors, width), BF16),
            in_specs=[HBM, VMEM, VMEM],
            out_specs=VMEM,
            compiler_params=params(48),
            cost_estimate=pl.CostEstimate(
                flops=2 * spectra.size, bytes_accessed=4 * spectra.size, transcendentals=0
            ),
            name="order",
        )(spectra, mine[:, at], other[:, at])
        source, far_y, near_y, ends = pl.pallas_call(
            functools.partial(adjoint_kernel, local_freqs, cols),
            out_shape=(
                jax.ShapeDtypeStruct((slabs + 1, cells_x * stride, LANES), F32),
                edge,
                edge,
                jax.ShapeDtypeStruct((2, DEPTH * stride, wide), F32),
            ),
            in_specs=[VMEM] * 3,
            out_specs=(VMEM,) * 4,
            compiler_params=params(),
            name="adjoint",
        )(spectra, stacked, classes)
        near_y, far_y = swap("sy", near_y, far_y)
        far_x, near_x = pl.pallas_call(
            ends_kernel,
            out_shape=(end, end),
            in_specs=[VMEM] * 3,
            out_specs=(VMEM,) * 2,
            scratch_shapes=[pltpu.VMEM((DEPTH * stride + 16, wide), F32)],
            compiler_params=params(),
            name="ends",
        )(ends, far_y, near_y)
        near_x, far_x = swap("sx", near_x, far_x)
        scaled, own_gain = pl.pallas_call(
            own_kernel,
            out_shape=(
                jax.ShapeDtypeStruct((slabs, cells_x * stride, LANES), F32),
                jax.ShapeDtypeStruct((cells_x * stride, LANES), F32),
            ),
            in_specs=[VMEM, SMEM],
            out_specs=(VMEM,) * 2,
            compiler_params=params(),
            name="own",
        )(source, class_kappa)
        sums, around, gains = pl.pallas_call(
            functools.partial(inner_kernel, local_freqs, cols),
            out_shape=(
                jax.ShapeDtypeStruct((width, all_sensors), F32),
                jax.ShapeDtypeStruct((slabs, total, LANES), F32),
                jax.ShapeDtypeStruct((total, LANES), F32),
            ),
            in_specs=[VMEM] * 5 + [SMEM],
            out_specs=(VMEM,) * 3,
            scratch_shapes=[
                pltpu.VMEM((slabs, total, LANES), F32),
                pltpu.VMEM((slabs, total, LANES), F32),
            ],
            compiler_params=params(),
            cost_estimate=pl.CostEstimate(
                flops=4 * spectra.size * width, bytes_accessed=2 * spectra.size, transcendentals=0
            ),
            name="inner",
        )(spectra, scaled, own_gain, far_y, near_y, class_kappa)
        pieces.append(
            pl.pallas_call(
                functools.partial(field_kernel, local_freqs, cols),
                out_shape=(
                    jax.ShapeDtypeStruct((halves, group, sensors, block), F32),
                    jax.ShapeDtypeStruct((halves, group, sensors, block), BF16),
                ),
                in_specs=[VMEM] * 6 + [SMEM],
                out_specs=(VMEM,) * 2,
                scratch_shapes=[
                    pltpu.VMEM((2, slabs, strip, LANES), F32),
                    pltpu.VMEM((2, strip, LANES), F32),
                    pltpu.VMEM((2, slabs, strip, LANES), F32),
                    pltpu.VMEM((2, slabs, strip, LANES), F32),
                    pltpu.VMEM((width, all_sensors), F32),
                ],
                compiler_params=params(),
                name="field",
            )(spectra, around, gains, sums, far_x, near_x, class_kappa)
        )
    keep = jnp.concatenate([piece[0] for piece in pieces], axis=1)
    send = jnp.concatenate([piece[1] for piece in pieces], axis=1)
    taken = lax.ppermute(send, "sy", partners("sy"))
    terms = exchange_half((keep + taken.astype(F32)).astype(BF16))
    new_solution, new_residual, norms = pl.pallas_call(
        residual_kernel,
        out_shape=(like, like, jax.ShapeDtypeStruct((tiles, 1, LANES), F32)),
        in_specs=[VMEM] * 6 + [SMEM],
        out_specs=(VMEM,) * 3,
        compiler_params=params(),
        name="residual",
    )(terms, inverse, noise_weight, solution, residual, direction, step_length)
    norms = lax.all_to_all(norms, GRID_AXES, 0, 0, tiled=True)
    new_solution, new_residual, new_direction, new_norm = pl.pallas_call(
        direction_kernel,
        out_shape=(like, like, like, jax.ShapeDtypeStruct((cols,), F32)),
        in_specs=[VMEM] * 4 + [SMEM],
        out_specs=(HBM,) * 4,
        scratch_shapes=[held, pltpu.VMEM((cols,), F32), pltpu.SemaphoreType.DMA((4,))],
        compiler_params=params(),
        name="direction",
    )(norms, new_solution, new_residual, direction, old_norm)
    return (new_solution, new_residual, new_direction, new_norm)


def solution(mesh):
    return jax.shard_map(
        on_device,
        mesh=mesh,
        in_specs=(
            P("fq", None, "sx", "sy", None),
            P(("sx", "sy"), None),
            P("sx", "sy"),
            P(),
            P("fq", ("sx", "sy"), None),
            P("fq", ("sx", "sy"), None),
            P("fq", ("sx", "sy"), None),
            P("fq"),
            P("fq"),
        ),
        out_specs=(
            P("fq", ("sx", "sy"), None),
            P("fq", ("sx", "sy"), None),
            P("fq", ("sx", "sy"), None),
            P("fq"),
        ),
        check_vma=False,
    )
```

```python
import functools
import math

import jax
import jax.numpy as jnp
from jax import lax
from jax.experimental import pallas as pl
from jax.experimental.pallas import tpu as pltpu
from jax.sharding import PartitionSpec as P
import numpy as np

SWEEPS = 4
DEPTH = SWEEPS - 1
HIGHEST = lax.Precision.HIGHEST
F32 = jnp.float32
BF16 = jnp.bfloat16
GRID_AXES = ("sx", "sy")
ALL_AXES = ("sx", "sy", "fq")
LANES = 128
MIB = 1024 * 1024
VMEM = pl.BlockSpec(memory_space=pltpu.VMEM)
SMEM = pl.BlockSpec(memory_space=pltpu.SMEM)
HBM = pl.BlockSpec(memory_space=pltpu.HBM)
ANY = pl.BlockSpec(memory_space=pl.ANY)


def params(mib=24):
    return pltpu.CompilerParams(vmem_limit_bytes=mib * MIB)


def tables(freq_count, local_freqs, local_cols, time_steps):
    freq = np.arange(freq_count)[:, None]
    step = np.arange(time_steps)[None, :]
    phases = (freq * step % time_steps) * (2.0 * math.pi / time_steps)
    factor = 1.0 / math.sqrt(time_steps)
    pair = np.stack([np.cos(phases) * factor, -np.sin(phases) * factor], 1)
    forward = np.repeat(pair.reshape(2 * freq_count, time_steps), local_cols, 0)
    doubling = np.where(np.arange(freq_count) == 0, 1.0, 2.0)[:, None, None]
    inverse = np.repeat((pair * doubling).reshape(2 * freq_count, time_steps), local_cols, 0)
    return forward.T.astype(np.float32), inverse.astype(np.float32)


def by_side(axis, low, high):
    even = lax.axis_index(axis) % 2 == 0
    return jnp.where(even, high, low), jnp.where(even, low, high)


def by_parity(axis, mine, other):
    even = lax.axis_index(axis) % 2 == 0
    return jnp.where(even, mine, other), jnp.where(even, other, mine)


def lane_ids(lanes):
    return lax.broadcasted_iota(jnp.int32, (1, lanes), 1)


def fetch_all(pairs, sems):
    copies = [pltpu.make_async_copy(a, b, sems.at[i]) for i, (a, b) in enumerate(pairs)]
    for copy in copies:
        copy.start()
    for copy in copies:
        copy.wait()


def spectrum_kernel(
    tiles, fq_blocks, direction_in, noise_in, table_in, out_ref, direction_ref, noise_ref, table_ref, sems
):
    fetch_all(
        ((direction_in, direction_ref), (noise_in, noise_ref), (table_in, table_ref)), sems
    )
    cols, sensors, steps = direction_ref.shape
    lanes = table_ref.shape[1]
    weighted = (noise_ref[...][None] * direction_ref[...]).reshape(cols * sensors, steps)
    full = jnp.dot(weighted, table_ref[...], precision=HIGHEST, preferred_element_type=F32)
    col_of = lane_ids(lanes) % cols
    spec = full[0:sensors]
    for col in range(1, cols):
        spec = jnp.where(col_of == col, full[col * sensors : (col + 1) * sensors], spec)
    spec = spec.astype(BF16)
    block = lanes // fq_blocks
    for b in range(fq_blocks):
        part = spec[:, b * block : (b + 1) * block]
        out_ref[:, b] = jnp.broadcast_to(part[None], (tiles, sensors, block))


def class_kernel(class_ref, after_ref, spectra_in, out_ref):
    cells_y, cells_x = class_ref.shape
    cells = cells_x * cells_y
    row = lax.broadcasted_iota(jnp.int32, (cells, cells_x), 0)
    pick = (row // cells_y == lax.broadcasted_iota(jnp.int32, (cells, cells_x), 1)).astype(F32)
    by_row = lax.dot_general(
        pick,
        class_ref[...].astype(F32) + 1.0,
        (((1,), (1,)), ((), ())),
        preferred_element_type=F32,
    )
    at = lax.broadcasted_iota(jnp.int32, (cells, cells_y), 0) % cells_y
    own = (at == lax.broadcasted_iota(jnp.int32, (cells, cells_y), 1)).astype(F32)
    out_ref[...] = jnp.dot(
        by_row * own, jnp.ones((cells_y, LANES), F32), preferred_element_type=F32
    )


def adjoint_of(part, stacked):
    _, cells_x, cells_y, all_sensors = part.shape
    both = part.reshape(2, cells_x * cells_y, all_sensors)
    both = jnp.concatenate([both[0], both[1]], axis=1)
    return jnp.dot(both, stacked, preferred_element_type=F32)


def freq_lanes(lanes, cols, freqs):
    return (lane_ids(lanes) // (2 * cols)) % freqs


def stacked_of(cols, mine_ref, other_ref):
    halves, group, sensors, block = mine_ref.shape
    lanes = group * block
    parts = []
    for b in range(group):
        pair = by_parity("sy", mine_ref[:, b], other_ref[:, b])
        parts.append(jnp.stack(pair, axis=1).reshape(2 * halves * sensors, block))
    direct = jnp.concatenate(parts, axis=1)
    wide = direct.astype(F32)
    is_real = (lane_ids(lanes) // cols) % 2 == 0
    turned = jnp.where(
        is_real, pltpu.roll(wide, lanes - cols, 1), -pltpu.roll(wide, cols, 1)
    ).astype(BF16)
    return jnp.concatenate([direct, turned], axis=0)


def adjoint_kernel(
    freqs, cols, spectra_ref, mine_ref, other_ref, class_ref, out_ref, far_ref, near_ref, ends_ref
):
    _, _, cells_x, cells_y, all_sensors = spectra_ref.shape
    stride = out_ref.shape[1] // cells_x
    lanes = mine_ref.shape[1] * mine_ref.shape[3]
    freq_of = freq_lanes(lanes, cols, freqs)
    stacked = stacked_of(cols, mine_ref, other_ref)
    acc = adjoint_of(spectra_ref[0], stacked)
    for f in range(1, freqs):
        acc = jnp.where(freq_of == f, adjoint_of(spectra_ref[f], stacked), acc)
    for k in range(out_ref.shape[0]):
        part = class_ref[...] if k * LANES == lanes else acc[:, k * LANES : (k + 1) * LANES]
        for x in range(cells_x):
            base = x * stride
            out_ref[k, base : base + cells_y] = part[x * cells_y : (x + 1) * cells_y]
            out_ref[k, base + cells_y : base + stride] = jnp.zeros((stride - cells_y, LANES), F32)
        at = slice(k * LANES, (k + 1) * LANES)
        for j in range(DEPTH):
            low = out_ref[k, pl.ds(j, cells_x, stride=stride), :]
            high = out_ref[k, pl.ds(cells_y - DEPTH + j, cells_x, stride=stride), :]
            near, far = by_side("sy", low, high)
            near_ref[j * cells_x : (j + 1) * cells_x, at] = near.astype(BF16)
            far_ref[j * cells_x : (j + 1) * cells_x, at] = far.astype(BF16)
        ends_ref[0, :, at] = out_ref[k, 0 : DEPTH * stride]
        ends_ref[1, :, at] = out_ref[k, (cells_x - DEPTH) * stride : cells_x * stride]


def ends_kernel(ends_ref, far_ref, near_ref, far_out, near_out, held):
    span = ends_ref.shape[1]
    stride = span // DEPTH
    cells_x = near_ref.shape[0] // DEPTH
    cells_y = stride - 8
    after, before = by_side("sy", far_ref[...].astype(F32), near_ref[...].astype(F32))
    built = []
    for side in range(2):
        held[...] = jnp.zeros_like(held)
        held[8 : 8 + span] = ends_ref[side]
        first = 0 if side == 0 else cells_x - DEPTH
        for x in range(DEPTH):
            for j in range(DEPTH):
                take = j * cells_x + first + x
                to = 8 + x * stride
                held[to + cells_y + j : to + cells_y + j + 1] = after[take : take + 1]
                held[to - DEPTH + j : to - DEPTH + j + 1] = before[take : take + 1]
        built.append(held[8 - DEPTH : 8 - DEPTH + span])
    near, far = by_side("sx", built[0], built[1])
    near_out[...] = near.astype(BF16)
    far_out[...] = far.astype(BF16)


def coefficients(classes, kappa_ref):
    kappa = jnp.zeros_like(classes)
    for n in range(kappa_ref.shape[0]):
        kappa = jnp.where(classes == n + 1.0, kappa_ref[n], kappa)
    scale = jnp.where(classes > 0.0, 1.0 / (1.0 + 4.0 * kappa), 0.0)
    return scale, kappa * scale


def sweep(source, gain, old, new, first, last, stride):
    near = (
        old[first - stride : last - stride]
        + old[first + stride : last + stride]
        + old[first - 1 : last - 1]
        + old[first + 1 : last + 1]
    )
    new[first:last] = source[first:last] + gain[first:last] * near


def both_forms(turned, cols):
    blocks, cells = turned.shape[0] // (2 * cols), turned.shape[1]
    pair = turned.reshape(blocks, 2, cols, cells)
    plain = pair.astype(BF16).reshape(blocks, 2 * cols, cells)
    crossed = jnp.stack([-pair[:, 1], pair[:, 0]], axis=1)
    crossed = crossed.astype(BF16).reshape(blocks, 2 * cols, cells)
    return jnp.concatenate([plain, crossed], axis=2)


def rows_of(forms, f, freqs):
    return jnp.concatenate([forms[b] for b in range(f, forms.shape[0], freqs)], axis=0)


def own_kernel(source_ref, kappa_ref, scaled_ref, gain_ref):
    slabs = scaled_ref.shape[0]
    scale, gain_ref[...] = coefficients(source_ref[slabs], kappa_ref)
    for k in range(slabs):
        scaled_ref[k] = source_ref[k] * scale


def inner_kernel(
    freqs,
    cols,
    spectra_ref,
    scaled_ref,
    own_gain_ref,
    far_y_ref,
    near_y_ref,
    kappa_ref,
    sums_ref,
    wide,
    gain,
    one,
    two,
):
    _, _, cells_x, cells_y, all_sensors = spectra_ref.shape
    cells = cells_x * cells_y
    slabs, rows, _ = scaled_ref.shape
    stride = rows // cells_x
    start = 2 * stride
    after, before = by_side("sy", far_y_ref[...].astype(F32), near_y_ref[...].astype(F32))
    gain[start - 8 : start] = jnp.zeros((8, LANES), F32)
    gain[start : start + rows] = own_gain_ref[...]
    for k in range(slabs):
        wide[k, start - 8 : start] = jnp.zeros((8, LANES), F32)
        wide[k, start : start + rows] = scaled_ref[k]
    for side, halo in ((0, before), (1, after)):
        scale, halo_gain = coefficients(halo[:, slabs * LANES :], kappa_ref)
        scaled = [halo[:, k * LANES : (k + 1) * LANES] * scale for k in range(slabs)]
        for j in range(DEPTH):
            part = slice(j * cells_x, (j + 1) * cells_x)
            to = pl.ds(start + j + (cells_y if side else -DEPTH), cells_x, stride=stride)
            gain[to, :] = halo_gain[part]
            for k in range(slabs):
                wide[k, to, :] = scaled[k][part]
    turned = []
    for k in range(slabs):
        old, new = wide.at[k], one.at[k]
        for x in range(1, DEPTH + 1):
            first, last = start + x * stride - 8, start + rows - x * stride
            sweep(wide.at[k], gain, old, new, first, last, stride)
            old, new = new, (two.at[k] if x % 2 else one.at[k])
        inner = old[start + DEPTH * stride : start + rows - DEPTH * stride]
        inner = inner.reshape(cells_x - 2 * DEPTH, stride, LANES)[:, 0:cells_y]
        edge = jnp.zeros((DEPTH * cells_y, LANES), F32)
        turned.append(
            jnp.concatenate([edge, inner.reshape(cells - 2 * DEPTH * cells_y, LANES), edge], axis=0).T
        )
    forms = both_forms(jnp.concatenate(turned, axis=0), cols)
    groups = forms.shape[0] // freqs
    for f in range(freqs):
        right = spectra_ref[f].reshape(2 * cells, all_sensors)
        got = jnp.dot(rows_of(forms, f, freqs), right, preferred_element_type=F32)
        for g in range(groups):
            at = (g * freqs + f) * 2 * cols
            sums_ref[at : at + 2 * cols] = got[g * 2 * cols : (g + 1) * 2 * cols]


def field_kernel(
    freqs,
    cols,
    spectra_ref,
    wide_ref,
    gain_ref,
    sums_ref,
    far_x_ref,
    near_x_ref,
    kappa_ref,
    keep_ref,
    send_ref,
    wide,
    gain,
    one,
    two,
    sums,
):
    _, _, cells_x, cells_y, all_sensors = spectra_ref.shape
    slabs = wide_ref.shape[0]
    stride = far_x_ref.shape[0] // DEPTH
    start = stride + 8
    deep = 2 * DEPTH

    def base(x):
        return start + x * stride

    below, above = by_side("sx", far_x_ref[...].astype(F32), near_x_ref[...].astype(F32))
    for end in range(2):
        own, outer = (DEPTH, 0) if end == 0 else (0, deep)
        inside = 0 if end == 0 else cells_x - deep
        beyond = above if end == 0 else below
        scale, beyond_gain = coefficients(beyond[:, slabs * LANES :], kappa_ref)
        for k in range(slabs + 1):
            to = wide.at[end, k] if k < slabs else gain.at[end]
            inner = wide_ref.at[k] if k < slabs else gain_ref
            first = (2 + inside) * stride
            to[base(0) - 8 : base(0)] = jnp.zeros((8, LANES), F32)
            to[base(3 * DEPTH) - 8 : base(3 * DEPTH)] = jnp.zeros((8, LANES), F32)
            to[base(own) - 8 : base(own + deep)] = inner[first - 8 : first + deep * stride]
            to[base(outer) - DEPTH : base(outer + DEPTH) - DEPTH] = (
                beyond[:, k * LANES : (k + 1) * LANES] * scale if k < slabs else beyond_gain
            )
    turned = []
    filler = -(deep * cells_y) % LANES
    for k in range(slabs):
        fields = []
        for end in range(2):
            source = wide.at[end, k]
            old, new = source, one.at[end, k]
            for x in range(1, DEPTH + 1):
                sweep(source, gain.at[end], old, new, base(x) - 8, base(3 * DEPTH - x), stride)
                old, new = new, (two.at[end, k] if x % 2 else one.at[end, k])
            field = old[base(DEPTH) : base(deep)].reshape(DEPTH, stride, LANES)[:, 0:cells_y]
            fields.append(field.reshape(DEPTH * cells_y, LANES))
        fields.append(jnp.zeros((filler, LANES), F32))
        turned.append(jnp.concatenate(fields, axis=0).T)
    forms = both_forms(jnp.concatenate(turned, axis=0), cols)
    groups = forms.shape[0] // freqs
    blank = jnp.zeros((filler, all_sensors), BF16)
    for f in range(freqs):
        right = []
        for part in range(2):
            for x in (0, cells_x - DEPTH):
                rows_here = spectra_ref[f, part, x : x + DEPTH]
                right.append(rows_here.reshape(DEPTH * cells_y, all_sensors))
            right.append(blank)
        got = jnp.dot(
            rows_of(forms, f, freqs), jnp.concatenate(right, axis=0), preferred_element_type=F32
        )
        for g in range(groups):
            at = (g * freqs + f) * 2 * cols
            sums[at : at + 2 * cols] = sums_ref[at : at + 2 * cols] + got[g * 2 * cols : (g + 1) * 2 * cols]
    back = sums[...].T
    halves, _, sensors, block = keep_ref.shape
    for g in range(groups):
        pair = back[:, g * block : (g + 1) * block].reshape(halves, 2, sensors, block)
        keep, send = by_parity("sy", pair[:, 0], pair[:, 1])
        keep_ref[:, g] = keep
        send_ref[:, g] = send.astype(BF16)


def residual_kernel(
    terms_ref,
    table_ref,
    noise_ref,
    solution_ref,
    residual_ref,
    direction_ref,
    step_ref,
    new_solution_ref,
    new_residual_ref,
    norm_ref,
):
    cols, sensors, steps = direction_ref.shape
    parts = []
    for b in range(terms_ref.shape[1]):
        parts.append(jnp.sum(terms_ref[:, b].astype(F32), axis=0))
    spectrum = jnp.concatenate(parts, axis=1)
    col_of = lane_ids(spectrum.shape[1]) % cols
    left = jnp.concatenate([jnp.where(col_of == c, spectrum, 0.0) for c in range(cols)], axis=0)
    returned = jnp.dot(left, table_ref[...], precision=HIGHEST, preferred_element_type=F32)
    lane = lane_ids(LANES)
    norms = jnp.zeros((1, LANES), F32)
    for c in range(cols):
        product = direction_ref[c] + noise_ref[...] * returned[c * sensors : (c + 1) * sensors]
        new_residual = residual_ref[c] - step_ref[c] * product
        new_residual_ref[c] = new_residual
        new_solution_ref[c] = solution_ref[c] + step_ref[c] * direction_ref[c]
        norm = jnp.sum(
            jnp.sum(new_residual * new_residual, axis=0, keepdims=True), axis=1, keepdims=True
        )
        norms = jnp.where(lane == c, norm, norms)
    norm_ref[...] = jnp.broadcast_to(norms[None], norm_ref.shape)


def direction_kernel(
    norms_ref,
    solution_ref,
    residual_ref,
    direction_ref,
    old_ref,
    solution_out,
    residual_out,
    direction_out,
    norm_out,
    held,
    norm_ref,
    sems,
):
    cols, sensors, steps = direction_ref.shape
    early = [
        pltpu.make_async_copy(solution_ref, solution_out, sems.at[0]),
        pltpu.make_async_copy(residual_ref, residual_out, sems.at[1]),
    ]
    for copy in early:
        copy.start()
    norm = jnp.sum(norms_ref[...], axis=0)
    norm_ref[...] = norm[0, 0:cols]
    final = pltpu.make_async_copy(norm_ref, norm_out, sems.at[3])
    final.start()
    for c in range(cols):
        held[c] = residual_ref[c] + (norm[:, c : c + 1] / old_ref[c]) * direction_ref[c]
    last = pltpu.make_async_copy(held, direction_out, sems.at[2])
    last.start()
    for copy in (*early, last, final):
        copy.wait()


def swap(axis, toward_partner, toward_other):
    count = lax.axis_size(axis)
    near = [(i, i ^ 1) for i in range(count) if (i ^ 1) < count]
    far = [(i, i + 1 if i % 2 else i - 1) for i in range(1, count - 1 + count % 2)]
    second = lax.ppermute(toward_other, axis, far)
    first = lax.ppermute(toward_partner, axis, near)
    return first, second


def partners(axis):
    return [(i, i ^ 1) for i in range(lax.axis_size(axis))]


def exchange_half(blocks):
    sx, sy, fq = (lax.axis_size(axis) for axis in ALL_AXES)
    groups = [
        [(x * sy + y) * fq + f for x in range(sx) for y in range(parity, sy, 2) for f in range(fq)]
        for parity in range(2)
    ]
    flat = blocks.reshape((-1,) + blocks.shape[2:])
    return lax.all_to_all(flat, ALL_AXES, 0, 0, axis_index_groups=groups, tiled=True).reshape(
        blocks.shape
    )


def on_device(
    spectra,
    noise_weight,
    class_map,
    class_kappa,
    solution,
    residual,
    direction,
    step_length,
    old_norm,
):
    local_freqs, _, cells_x, cells_y, all_sensors = spectra.shape
    cols, sensors, steps = direction.shape
    fq_blocks = lax.axis_size("fq")
    tiles = lax.axis_size("sx") * lax.axis_size("sy")
    halves = tiles // 2
    block = 2 * local_freqs * cols
    lanes = block * fq_blocks
    forward, inverse = tables(local_freqs * fq_blocks, local_freqs, cols, steps)
    group = 2 if fq_blocks % 2 == 0 else 1
    chunks = fq_blocks // group
    width = group * block
    stride = cells_y + 8
    wide = width + LANES
    cells = cells_x * cells_y

    like = jax.ShapeDtypeStruct(direction.shape, F32)
    held = pltpu.VMEM(direction.shape, F32)
    spec = pl.pallas_call(
        functools.partial(spectrum_kernel, halves, fq_blocks),
        out_shape=jax.ShapeDtypeStruct((halves, fq_blocks, sensors, block), BF16),
        in_specs=[HBM] * 3,
        out_specs=VMEM,
        scratch_shapes=[
            held,
            pltpu.VMEM(noise_weight.shape, F32),
            pltpu.VMEM(forward.shape, F32),
            pltpu.SemaphoreType.DMA((3,)),
        ],
        compiler_params=params(62),
        cost_estimate=pl.CostEstimate(
            flops=2 * spectra.size, bytes_accessed=4 * spectra.size, transcendentals=0
        ),
        name="spectrum",
    )(direction, noise_weight, forward)
    mine = exchange_half(spec)
    other = lax.ppermute(mine, "sy", partners("sy"))
    classes = pl.pallas_call(
        class_kernel,
        out_shape=jax.ShapeDtypeStruct((cells, LANES), F32),
        in_specs=[VMEM, ANY, HBM],
        out_specs=VMEM,
        compiler_params=params(48),
        name="classes",
    )(class_map.T, mine, spectra)

    edge = jax.ShapeDtypeStruct((DEPTH * cells_x, wide), BF16)
    end = jax.ShapeDtypeStruct((DEPTH * stride, wide), BF16)
    total = (cells_x + 4) * stride
    strip = (3 * DEPTH + 2) * stride + 16
    slabs = width // LANES
    pieces = []
    for i in range(chunks):
        at = slice(i * group, (i + 1) * group)
        source, far_y, near_y, ends = pl.pallas_call(
            functools.partial(adjoint_kernel, local_freqs, cols),
            out_shape=(
                jax.ShapeDtypeStruct((slabs + 1, cells_x * stride, LANES), F32),
                edge,
                edge,
                jax.ShapeDtypeStruct((2, DEPTH * stride, wide), F32),
            ),
            in_specs=[VMEM] * 4,
            out_specs=(VMEM,) * 4,
            compiler_params=params(),
            name="adjoint",
        )(spectra, mine[:, at], other[:, at], classes)
        near_y, far_y = swap("sy", near_y, far_y)
        far_x, near_x = pl.pallas_call(
            ends_kernel,
            out_shape=(end, end),
            in_specs=[VMEM] * 3,
            out_specs=(VMEM,) * 2,
            scratch_shapes=[pltpu.VMEM((DEPTH * stride + 16, wide), F32)],
            compiler_params=params(),
            name="ends",
        )(ends, far_y, near_y)
        near_x, far_x = swap("sx", near_x, far_x)
        scaled, own_gain = pl.pallas_call(
            own_kernel,
            out_shape=(
                jax.ShapeDtypeStruct((slabs, cells_x * stride, LANES), F32),
                jax.ShapeDtypeStruct((cells_x * stride, LANES), F32),
            ),
            in_specs=[VMEM, SMEM],
            out_specs=(VMEM,) * 2,
            compiler_params=params(),
            name="own",
        )(source, class_kappa)
        sums, around, gains = pl.pallas_call(
            functools.partial(inner_kernel, local_freqs, cols),
            out_shape=(
                jax.ShapeDtypeStruct((width, all_sensors), F32),
                jax.ShapeDtypeStruct((slabs, total, LANES), F32),
                jax.ShapeDtypeStruct((total, LANES), F32),
            ),
            in_specs=[VMEM] * 5 + [SMEM],
            out_specs=(VMEM,) * 3,
            scratch_shapes=[
                pltpu.VMEM((slabs, total, LANES), F32),
                pltpu.VMEM((slabs, total, LANES), F32),
            ],
            compiler_params=params(),
            cost_estimate=pl.CostEstimate(
                flops=4 * spectra.size * width, bytes_accessed=2 * spectra.size, transcendentals=0
            ),
            name="inner",
        )(spectra, scaled, own_gain, far_y, near_y, class_kappa)
        pieces.append(
            pl.pallas_call(
                functools.partial(field_kernel, local_freqs, cols),
                out_shape=(
                    jax.ShapeDtypeStruct((halves, group, sensors, block), F32),
                    jax.ShapeDtypeStruct((halves, group, sensors, block), BF16),
                ),
                in_specs=[VMEM] * 6 + [SMEM],
                out_specs=(VMEM,) * 2,
                scratch_shapes=[
                    pltpu.VMEM((2, slabs, strip, LANES), F32),
                    pltpu.VMEM((2, strip, LANES), F32),
                    pltpu.VMEM((2, slabs, strip, LANES), F32),
                    pltpu.VMEM((2, slabs, strip, LANES), F32),
                    pltpu.VMEM((width, all_sensors), F32),
                ],
                compiler_params=params(),
                name="field",
            )(spectra, around, gains, sums, far_x, near_x, class_kappa)
        )
    keep = jnp.concatenate([piece[0] for piece in pieces], axis=1)
    send = jnp.concatenate([piece[1] for piece in pieces], axis=1)
    taken = lax.ppermute(send, "sy", partners("sy"))
    terms = exchange_half((keep + taken.astype(F32)).astype(BF16))
    new_solution, new_residual, norms = pl.pallas_call(
        residual_kernel,
        out_shape=(like, like, jax.ShapeDtypeStruct((tiles, 1, LANES), F32)),
        in_specs=[VMEM] * 6 + [SMEM],
        out_specs=(VMEM,) * 3,
        compiler_params=params(),
        name="residual",
    )(terms, inverse, noise_weight, solution, residual, direction, step_length)
    norms = lax.all_to_all(norms, GRID_AXES, 0, 0, tiled=True)
    new_solution, new_residual, new_direction, new_norm = pl.pallas_call(
        direction_kernel,
        out_shape=(like, like, like, jax.ShapeDtypeStruct((cols,), F32)),
        in_specs=[VMEM] * 4 + [SMEM],
        out_specs=(HBM,) * 4,
        scratch_shapes=[held, pltpu.VMEM((cols,), F32), pltpu.SemaphoreType.DMA((4,))],
        compiler_params=params(),
        name="direction",
    )(norms, new_solution, new_residual, direction, old_norm)
    return (new_solution, new_residual, new_direction, new_norm)


def solution(mesh):
    return jax.shard_map(
        on_device,
        mesh=mesh,
        in_specs=(
            P("fq", None, "sx", "sy", None),
            P(("sx", "sy"), None),
            P("sx", "sy"),
            P(),
            P("fq", ("sx", "sy"), None),
            P("fq", ("sx", "sy"), None),
            P("fq", ("sx", "sy"), None),
            P("fq"),
            P("fq"),
        ),
        out_specs=(
            P("fq", ("sx", "sy"), None),
            P("fq", ("sx", "sy"), None),
            P("fq", ("sx", "sy"), None),
            P("fq"),
        ),
        check_vma=False,
    )
```

```python
import functools
import math

import jax
import jax.numpy as jnp
from jax import lax
from jax.experimental import pallas as pl
from jax.experimental.pallas import tpu as pltpu
from jax.sharding import PartitionSpec as P
import numpy as np

SWEEPS = 4
DEPTH = SWEEPS - 1
F32 = jnp.float32
BF16 = jnp.bfloat16
GRID_AXES = ("sx", "sy")
ALL_AXES = ("sx", "sy", "fq")
LANES = 128
MIB = 1024 * 1024
VMEM = pl.BlockSpec(memory_space=pltpu.VMEM)
SMEM = pl.BlockSpec(memory_space=pltpu.SMEM)
HBM = pl.BlockSpec(memory_space=pltpu.HBM)
ANY = pl.BlockSpec(memory_space=pl.ANY)


def params(mib=24):
    return pltpu.CompilerParams(vmem_limit_bytes=mib * MIB)


def tables(freq_count, local_freqs, local_cols, time_steps):
    freq = np.arange(freq_count)[:, None]
    step = np.arange(time_steps)[None, :]
    phases = (freq * step % time_steps) * (2.0 * math.pi / time_steps)
    factor = 1.0 / math.sqrt(time_steps)
    pair = np.stack([np.cos(phases) * factor, -np.sin(phases) * factor], 1)
    forward = np.repeat(pair.reshape(2 * freq_count, time_steps), local_cols, 0)
    doubling = np.where(np.arange(freq_count) == 0, 1.0, 2.0)[:, None, None]
    inverse = np.repeat((pair * doubling).reshape(2 * freq_count, time_steps), local_cols, 0)
    coarse = inverse.astype(jnp.bfloat16)
    fine = (inverse - coarse.astype(np.float64)).astype(jnp.bfloat16)
    rough = forward.T.astype(jnp.bfloat16)
    rest = (forward.T - rough.astype(np.float64)).astype(jnp.bfloat16)
    return np.stack([rough, rest]), np.concatenate([coarse, coarse, fine], axis=0)


def by_side(axis, low, high):
    even = lax.axis_index(axis) % 2 == 0
    return jnp.where(even, high, low), jnp.where(even, low, high)


def by_parity(axis, mine, other):
    even = lax.axis_index(axis) % 2 == 0
    return jnp.where(even, mine, other), jnp.where(even, other, mine)


def lane_ids(lanes):
    return lax.broadcasted_iota(jnp.int32, (1, lanes), 1)


def fetch_all(pairs, sems):
    copies = [pltpu.make_async_copy(a, b, sems.at[i]) for i, (a, b) in enumerate(pairs)]
    for copy in copies:
        copy.start()
    for copy in copies:
        copy.wait()


def spectrum_kernel(
    tiles, fq_blocks, direction_in, noise_in, table_in, out_ref, direction_ref, noise_ref, table_ref, sems
):
    fetch_all(
        ((direction_in, direction_ref), (noise_in, noise_ref), (table_in, table_ref)), sems
    )
    cols, sensors, steps = direction_ref.shape
    lanes = table_ref.shape[2]
    weighted = (noise_ref[...][None] * direction_ref[...]).reshape(cols * sensors, steps)
    coarse = weighted.astype(BF16)
    fine = (weighted - coarse.astype(F32)).astype(BF16)
    full = (
        jnp.dot(fine, table_ref[0], preferred_element_type=F32)
        + jnp.dot(coarse, table_ref[1], preferred_element_type=F32)
        + jnp.dot(coarse, table_ref[0], preferred_element_type=F32)
    )
    col_of = lane_ids(lanes) % cols
    spec = full[0:sensors]
    for col in range(1, cols):
        spec = jnp.where(col_of == col, full[col * sensors : (col + 1) * sensors], spec)
    spec = spec.astype(BF16)
    block = lanes // fq_blocks
    for b in range(fq_blocks):
        part = spec[:, b * block : (b + 1) * block]
        out_ref[:, b] = jnp.broadcast_to(part[None], (tiles, sensors, block))


def class_kernel(class_ref, after_ref, spectra_in, out_ref):
    cells_y, cells_x = class_ref.shape
    cells = cells_x * cells_y
    row = lax.broadcasted_iota(jnp.int32, (cells, cells_x), 0)
    pick = (row // cells_y == lax.broadcasted_iota(jnp.int32, (cells, cells_x), 1)).astype(F32)
    by_row = lax.dot_general(
        pick,
        class_ref[...].astype(F32) + 1.0,
        (((1,), (1,)), ((), ())),
        preferred_element_type=F32,
    )
    at = lax.broadcasted_iota(jnp.int32, (cells, cells_y), 0) % cells_y
    own = (at == lax.broadcasted_iota(jnp.int32, (cells, cells_y), 1)).astype(F32)
    out_ref[...] = jnp.dot(
        by_row * own, jnp.ones((cells_y, LANES), F32), preferred_element_type=F32
    )


def adjoint_of(part, stacked):
    _, cells_x, cells_y, all_sensors = part.shape
    both = part.reshape(2, cells_x * cells_y, all_sensors)
    both = jnp.concatenate([both[0], both[1]], axis=1)
    return jnp.dot(both, stacked, preferred_element_type=F32)


def freq_lanes(lanes, cols, freqs):
    return (lane_ids(lanes) // (2 * cols)) % freqs


def stacked_of(cols, mine_ref, other_ref):
    halves, group, sensors, block = mine_ref.shape
    lanes = group * block
    parts = []
    for b in range(group):
        pair = by_parity("sy", mine_ref[:, b], other_ref[:, b])
        parts.append(jnp.stack(pair, axis=1).reshape(2 * halves * sensors, block))
    direct = jnp.concatenate(parts, axis=1)
    wide = direct.astype(F32)
    is_real = (lane_ids(lanes) // cols) % 2 == 0
    turned = jnp.where(
        is_real, pltpu.roll(wide, lanes - cols, 1), -pltpu.roll(wide, cols, 1)
    ).astype(BF16)
    return jnp.concatenate([direct, turned], axis=0)


def adjoint_kernel(
    freqs, cols, spectra_ref, mine_ref, other_ref, class_ref, out_ref, far_ref, near_ref, ends_ref
):
    _, _, cells_x, cells_y, all_sensors = spectra_ref.shape
    stride = out_ref.shape[1] // cells_x
    lanes = mine_ref.shape[1] * mine_ref.shape[3]
    freq_of = freq_lanes(lanes, cols, freqs)
    stacked = stacked_of(cols, mine_ref, other_ref)
    acc = adjoint_of(spectra_ref[0], stacked)
    for f in range(1, freqs):
        acc = jnp.where(freq_of == f, adjoint_of(spectra_ref[f], stacked), acc)
    for k in range(out_ref.shape[0]):
        part = class_ref[...] if k * LANES == lanes else acc[:, k * LANES : (k + 1) * LANES]
        for x in range(cells_x):
            base = x * stride
            out_ref[k, base : base + cells_y] = part[x * cells_y : (x + 1) * cells_y]
            out_ref[k, base + cells_y : base + stride] = jnp.zeros((stride - cells_y, LANES), F32)
        at = slice(k * LANES, (k + 1) * LANES)
        for j in range(DEPTH):
            low = out_ref[k, pl.ds(j, cells_x, stride=stride), :]
            high = out_ref[k, pl.ds(cells_y - DEPTH + j, cells_x, stride=stride), :]
            near, far = by_side("sy", low, high)
            near_ref[j * cells_x : (j + 1) * cells_x, at] = near.astype(BF16)
            far_ref[j * cells_x : (j + 1) * cells_x, at] = far.astype(BF16)
        ends_ref[0, :, at] = out_ref[k, 0 : DEPTH * stride]
        ends_ref[1, :, at] = out_ref[k, (cells_x - DEPTH) * stride : cells_x * stride]


def ends_kernel(ends_ref, far_ref, near_ref, far_out, near_out, held):
    span = ends_ref.shape[1]
    stride = span // DEPTH
    cells_x = near_ref.shape[0] // DEPTH
    cells_y = stride - 8
    after, before = by_side("sy", far_ref[...].astype(F32), near_ref[...].astype(F32))
    built = []
    for side in range(2):
        held[...] = jnp.zeros_like(held)
        held[8 : 8 + span] = ends_ref[side]
        first = 0 if side == 0 else cells_x - DEPTH
        for x in range(DEPTH):
            for j in range(DEPTH):
                take = j * cells_x + first + x
                to = 8 + x * stride
                held[to + cells_y + j : to + cells_y + j + 1] = after[take : take + 1]
                held[to - DEPTH + j : to - DEPTH + j + 1] = before[take : take + 1]
        built.append(held[8 - DEPTH : 8 - DEPTH + span])
    near, far = by_side("sx", built[0], built[1])
    near_out[...] = near.astype(BF16)
    far_out[...] = far.astype(BF16)


def coefficients(classes, kappa_ref):
    kappa = jnp.zeros_like(classes)
    for n in range(kappa_ref.shape[0]):
        kappa = jnp.where(classes == n + 1.0, kappa_ref[n], kappa)
    scale = jnp.where(classes > 0.0, 1.0 / (1.0 + 4.0 * kappa), 0.0)
    return scale, kappa * scale


def sweep(source, gain, old, new, first, last, stride):
    near = (
        old[first - stride : last - stride]
        + old[first + stride : last + stride]
        + old[first - 1 : last - 1]
        + old[first + 1 : last + 1]
    )
    new[first:last] = source[first:last] + gain[first:last] * near


def both_forms(turned, cols):
    blocks, cells = turned.shape[0] // (2 * cols), turned.shape[1]
    pair = turned.reshape(blocks, 2, cols, cells)
    plain = pair.astype(BF16).reshape(blocks, 2 * cols, cells)
    crossed = jnp.stack([-pair[:, 1], pair[:, 0]], axis=1)
    crossed = crossed.astype(BF16).reshape(blocks, 2 * cols, cells)
    return jnp.concatenate([plain, crossed], axis=2)


def rows_of(forms, f, freqs):
    return jnp.concatenate([forms[b] for b in range(f, forms.shape[0], freqs)], axis=0)


def own_kernel(source_ref, kappa_ref, scaled_ref, gain_ref):
    slabs = scaled_ref.shape[0]
    scale, gain_ref[...] = coefficients(source_ref[slabs], kappa_ref)
    for k in range(slabs):
        scaled_ref[k] = source_ref[k] * scale


def inner_kernel(
    freqs,
    cols,
    spectra_ref,
    scaled_ref,
    own_gain_ref,
    far_y_ref,
    near_y_ref,
    kappa_ref,
    sums_ref,
    wide,
    gain,
    one,
    two,
):
    _, _, cells_x, cells_y, all_sensors = spectra_ref.shape
    cells = cells_x * cells_y
    slabs, rows, _ = scaled_ref.shape
    stride = rows // cells_x
    start = 2 * stride
    after, before = by_side("sy", far_y_ref[...].astype(F32), near_y_ref[...].astype(F32))
    gain[start - 8 : start] = jnp.zeros((8, LANES), F32)
    gain[start : start + rows] = own_gain_ref[...]
    for k in range(slabs):
        wide[k, start - 8 : start] = jnp.zeros((8, LANES), F32)
        wide[k, start : start + rows] = scaled_ref[k]
    for side, halo in ((0, before), (1, after)):
        scale, halo_gain = coefficients(halo[:, slabs * LANES :], kappa_ref)
        scaled = [halo[:, k * LANES : (k + 1) * LANES] * scale for k in range(slabs)]
        for j in range(DEPTH):
            part = slice(j * cells_x, (j + 1) * cells_x)
            to = pl.ds(start + j + (cells_y if side else -DEPTH), cells_x, stride=stride)
            gain[to, :] = halo_gain[part]
            for k in range(slabs):
                wide[k, to, :] = scaled[k][part]
    turned = []
    for k in range(slabs):
        old, new = wide.at[k], one.at[k]
        for x in range(1, DEPTH + 1):
            first, last = start + x * stride - 8, start + rows - x * stride
            sweep(wide.at[k], gain, old, new, first, last, stride)
            old, new = new, (two.at[k] if x % 2 else one.at[k])
        inner = old[start + DEPTH * stride : start + rows - DEPTH * stride]
        inner = inner.reshape(cells_x - 2 * DEPTH, stride, LANES)[:, 0:cells_y]
        edge = jnp.zeros((DEPTH * cells_y, LANES), F32)
        turned.append(
            jnp.concatenate([edge, inner.reshape(cells - 2 * DEPTH * cells_y, LANES), edge], axis=0).T
        )
    forms = both_forms(jnp.concatenate(turned, axis=0), cols)
    groups = forms.shape[0] // freqs
    for f in range(freqs):
        right = spectra_ref[f].reshape(2 * cells, all_sensors)
        got = jnp.dot(rows_of(forms, f, freqs), right, preferred_element_type=F32)
        for g in range(groups):
            at = (g * freqs + f) * 2 * cols
            sums_ref[at : at + 2 * cols] = got[g * 2 * cols : (g + 1) * 2 * cols]


def field_kernel(
    freqs,
    cols,
    spectra_ref,
    wide_ref,
    gain_ref,
    sums_ref,
    far_x_ref,
    near_x_ref,
    kappa_ref,
    keep_ref,
    send_ref,
    wide,
    gain,
    one,
    two,
    sums,
):
    _, _, cells_x, cells_y, all_sensors = spectra_ref.shape
    slabs = wide_ref.shape[0]
    stride = far_x_ref.shape[0] // DEPTH
    start = stride + 8
    deep = 2 * DEPTH

    def base(x):
        return start + x * stride

    below, above = by_side("sx", far_x_ref[...].astype(F32), near_x_ref[...].astype(F32))
    for end in range(2):
        own, outer = (DEPTH, 0) if end == 0 else (0, deep)
        inside = 0 if end == 0 else cells_x - deep
        beyond = above if end == 0 else below
        scale, beyond_gain = coefficients(beyond[:, slabs * LANES :], kappa_ref)
        for k in range(slabs + 1):
            to = wide.at[end, k] if k < slabs else gain.at[end]
            inner = wide_ref.at[k] if k < slabs else gain_ref
            first = (2 + inside) * stride
            to[base(0) - 8 : base(0)] = jnp.zeros((8, LANES), F32)
            to[base(3 * DEPTH) - 8 : base(3 * DEPTH)] = jnp.zeros((8, LANES), F32)
            to[base(own) - 8 : base(own + deep)] = inner[first - 8 : first + deep * stride]
            to[base(outer) - DEPTH : base(outer + DEPTH) - DEPTH] = (
                beyond[:, k * LANES : (k + 1) * LANES] * scale if k < slabs else beyond_gain
            )
    turned = []
    filler = -(deep * cells_y) % LANES
    for k in range(slabs):
        fields = []
        for end in range(2):
            source = wide.at[end, k]
            old, new = source, one.at[end, k]
            for x in range(1, DEPTH + 1):
                sweep(source, gain.at[end], old, new, base(x) - 8, base(3 * DEPTH - x), stride)
                old, new = new, (two.at[end, k] if x % 2 else one.at[end, k])
            field = old[base(DEPTH) : base(deep)].reshape(DEPTH, stride, LANES)[:, 0:cells_y]
            fields.append(field.reshape(DEPTH * cells_y, LANES))
        fields.append(jnp.zeros((filler, LANES), F32))
        turned.append(jnp.concatenate(fields, axis=0).T)
    forms = both_forms(jnp.concatenate(turned, axis=0), cols)
    groups = forms.shape[0] // freqs
    blank = jnp.zeros((filler, all_sensors), BF16)
    for f in range(freqs):
        right = []
        for part in range(2):
            for x in (0, cells_x - DEPTH):
                rows_here = spectra_ref[f, part, x : x + DEPTH]
                right.append(rows_here.reshape(DEPTH * cells_y, all_sensors))
            right.append(blank)
        got = jnp.dot(
            rows_of(forms, f, freqs), jnp.concatenate(right, axis=0), preferred_element_type=F32
        )
        for g in range(groups):
            at = (g * freqs + f) * 2 * cols
            sums[at : at + 2 * cols] = sums_ref[at : at + 2 * cols] + got[g * 2 * cols : (g + 1) * 2 * cols]
    back = sums[...].T
    halves, _, sensors, block = keep_ref.shape
    for g in range(groups):
        pair = back[:, g * block : (g + 1) * block].reshape(halves, 2, sensors, block)
        keep, send = by_parity("sy", pair[:, 0], pair[:, 1])
        keep_ref[:, g] = keep
        send_ref[:, g] = send.astype(BF16)


def residual_kernel(
    terms_ref,
    table_ref,
    noise_ref,
    solution_ref,
    residual_ref,
    direction_ref,
    step_ref,
    new_solution_ref,
    new_residual_ref,
    norm_ref,
):
    cols, sensors, steps = direction_ref.shape
    parts = []
    for b in range(terms_ref.shape[1]):
        parts.append(jnp.sum(terms_ref[:, b].astype(F32), axis=0))
    spectrum = jnp.concatenate(parts, axis=1)
    col_of = lane_ids(spectrum.shape[1]) % cols
    left = jnp.concatenate([jnp.where(col_of == c, spectrum, 0.0) for c in range(cols)], axis=0)
    coarse = left.astype(BF16)
    fine = (left - coarse.astype(F32)).astype(BF16)
    returned = jnp.dot(
        jnp.concatenate([coarse, fine, coarse], axis=1), table_ref[...], preferred_element_type=F32
    )
    lane = lane_ids(LANES)
    norms = jnp.zeros((1, LANES), F32)
    for c in range(cols):
        product = direction_ref[c] + noise_ref[...] * returned[c * sensors : (c + 1) * sensors]
        new_residual = residual_ref[c] - step_ref[c] * product
        new_residual_ref[c] = new_residual
        new_solution_ref[c] = solution_ref[c] + step_ref[c] * direction_ref[c]
        norm = jnp.sum(
            jnp.sum(new_residual * new_residual, axis=0, keepdims=True), axis=1, keepdims=True
        )
        norms = jnp.where(lane == c, norm, norms)
    norm_ref[...] = jnp.broadcast_to(norms[None], norm_ref.shape)


def direction_kernel(
    norms_ref,
    solution_ref,
    residual_ref,
    direction_ref,
    old_ref,
    solution_out,
    residual_out,
    direction_out,
    norm_out,
    held,
    norm_ref,
    sems,
):
    cols, sensors, steps = direction_ref.shape
    early = [
        pltpu.make_async_copy(solution_ref, solution_out, sems.at[0]),
        pltpu.make_async_copy(residual_ref, residual_out, sems.at[1]),
    ]
    for copy in early:
        copy.start()
    norm = jnp.sum(norms_ref[...], axis=0)
    norm_ref[...] = norm[0, 0:cols]
    final = pltpu.make_async_copy(norm_ref, norm_out, sems.at[3])
    final.start()
    for c in range(cols):
        held[c] = residual_ref[c] + (norm[:, c : c + 1] / old_ref[c]) * direction_ref[c]
    last = pltpu.make_async_copy(held, direction_out, sems.at[2])
    last.start()
    for copy in (*early, last, final):
        copy.wait()


def swap(axis, toward_partner, toward_other):
    count = lax.axis_size(axis)
    near = [(i, i ^ 1) for i in range(count) if (i ^ 1) < count]
    far = [(i, i + 1 if i % 2 else i - 1) for i in range(1, count - 1 + count % 2)]
    second = lax.ppermute(toward_other, axis, far)
    first = lax.ppermute(toward_partner, axis, near)
    return first, second


def partners(axis):
    return [(i, i ^ 1) for i in range(lax.axis_size(axis))]


def exchange_half(blocks):
    sx, sy, fq = (lax.axis_size(axis) for axis in ALL_AXES)
    groups = [
        [(x * sy + y) * fq + f for x in range(sx) for y in range(parity, sy, 2) for f in range(fq)]
        for parity in range(2)
    ]
    flat = blocks.reshape((-1,) + blocks.shape[2:])
    return lax.all_to_all(flat, ALL_AXES, 0, 0, axis_index_groups=groups, tiled=True).reshape(
        blocks.shape
    )


def on_device(
    spectra,
    noise_weight,
    class_map,
    class_kappa,
    solution,
    residual,
    direction,
    step_length,
    old_norm,
):
    local_freqs, _, cells_x, cells_y, all_sensors = spectra.shape
    cols, sensors, steps = direction.shape
    fq_blocks = lax.axis_size("fq")
    tiles = lax.axis_size("sx") * lax.axis_size("sy")
    halves = tiles // 2
    block = 2 * local_freqs * cols
    lanes = block * fq_blocks
    forward, inverse = tables(local_freqs * fq_blocks, local_freqs, cols, steps)
    group = 2 if fq_blocks % 2 == 0 else 1
    chunks = fq_blocks // group
    width = group * block
    stride = cells_y + 8
    wide = width + LANES
    cells = cells_x * cells_y

    like = jax.ShapeDtypeStruct(direction.shape, F32)
    held = pltpu.VMEM(direction.shape, F32)
    spec = pl.pallas_call(
        functools.partial(spectrum_kernel, halves, fq_blocks),
        out_shape=jax.ShapeDtypeStruct((halves, fq_blocks, sensors, block), BF16),
        in_specs=[HBM] * 3,
        out_specs=VMEM,
        scratch_shapes=[
            held,
            pltpu.VMEM(noise_weight.shape, F32),
            pltpu.VMEM(forward.shape, BF16),
            pltpu.SemaphoreType.DMA((3,)),
        ],
        compiler_params=params(62),
        cost_estimate=pl.CostEstimate(
            flops=2 * spectra.size, bytes_accessed=4 * spectra.size, transcendentals=0
        ),
        name="spectrum",
    )(direction, noise_weight, forward)
    mine = exchange_half(spec)
    other = lax.ppermute(mine, "sy", partners("sy"))
    classes = pl.pallas_call(
        class_kernel,
        out_shape=jax.ShapeDtypeStruct((cells, LANES), F32),
        in_specs=[VMEM, ANY, HBM],
        out_specs=VMEM,
        compiler_params=params(48),
        name="classes",
    )(class_map.T, mine, spectra)

    edge = jax.ShapeDtypeStruct((DEPTH * cells_x, wide), BF16)
    end = jax.ShapeDtypeStruct((DEPTH * stride, wide), BF16)
    total = (cells_x + 4) * stride
    strip = (3 * DEPTH + 2) * stride + 16
    slabs = width // LANES
    pieces = []
    for i in range(chunks):
        at = slice(i * group, (i + 1) * group)
        source, far_y, near_y, ends = pl.pallas_call(
            functools.partial(adjoint_kernel, local_freqs, cols),
            out_shape=(
                jax.ShapeDtypeStruct((slabs + 1, cells_x * stride, LANES), F32),
                edge,
                edge,
                jax.ShapeDtypeStruct((2, DEPTH * stride, wide), F32),
            ),
            in_specs=[VMEM] * 4,
            out_specs=(VMEM,) * 4,
            compiler_params=params(),
            name="adjoint",
        )(spectra, mine[:, at], other[:, at], classes)
        near_y, far_y = swap("sy", near_y, far_y)
        far_x, near_x = pl.pallas_call(
            ends_kernel,
            out_shape=(end, end),
            in_specs=[VMEM] * 3,
            out_specs=(VMEM,) * 2,
            scratch_shapes=[pltpu.VMEM((DEPTH * stride + 16, wide), F32)],
            compiler_params=params(),
            name="ends",
        )(ends, far_y, near_y)
        near_x, far_x = swap("sx", near_x, far_x)
        scaled, own_gain = pl.pallas_call(
            own_kernel,
            out_shape=(
                jax.ShapeDtypeStruct((slabs, cells_x * stride, LANES), F32),
                jax.ShapeDtypeStruct((cells_x * stride, LANES), F32),
            ),
            in_specs=[VMEM, SMEM],
            out_specs=(VMEM,) * 2,
            compiler_params=params(),
            name="own",
        )(source, class_kappa)
        sums, around, gains = pl.pallas_call(
            functools.partial(inner_kernel, local_freqs, cols),
            out_shape=(
                jax.ShapeDtypeStruct((width, all_sensors), F32),
                jax.ShapeDtypeStruct((slabs, total, LANES), F32),
                jax.ShapeDtypeStruct((total, LANES), F32),
            ),
            in_specs=[VMEM] * 5 + [SMEM],
            out_specs=(VMEM,) * 3,
            scratch_shapes=[
                pltpu.VMEM((slabs, total, LANES), F32),
                pltpu.VMEM((slabs, total, LANES), F32),
            ],
            compiler_params=params(),
            cost_estimate=pl.CostEstimate(
                flops=4 * spectra.size * width, bytes_accessed=2 * spectra.size, transcendentals=0
            ),
            name="inner",
        )(spectra, scaled, own_gain, far_y, near_y, class_kappa)
        pieces.append(
            pl.pallas_call(
                functools.partial(field_kernel, local_freqs, cols),
                out_shape=(
                    jax.ShapeDtypeStruct((halves, group, sensors, block), F32),
                    jax.ShapeDtypeStruct((halves, group, sensors, block), BF16),
                ),
                in_specs=[VMEM] * 6 + [SMEM],
                out_specs=(VMEM,) * 2,
                scratch_shapes=[
                    pltpu.VMEM((2, slabs, strip, LANES), F32),
                    pltpu.VMEM((2, strip, LANES), F32),
                    pltpu.VMEM((2, slabs, strip, LANES), F32),
                    pltpu.VMEM((2, slabs, strip, LANES), F32),
                    pltpu.VMEM((width, all_sensors), F32),
                ],
                compiler_params=params(),
                name="field",
            )(spectra, around, gains, sums, far_x, near_x, class_kappa)
        )
    keep = jnp.concatenate([piece[0] for piece in pieces], axis=1)
    send = jnp.concatenate([piece[1] for piece in pieces], axis=1)
    taken = lax.ppermute(send, "sy", partners("sy"))
    terms = exchange_half((keep + taken.astype(F32)).astype(BF16))
    new_solution, new_residual, norms = pl.pallas_call(
        residual_kernel,
        out_shape=(like, like, jax.ShapeDtypeStruct((tiles, 1, LANES), F32)),
        in_specs=[VMEM] * 6 + [SMEM],
        out_specs=(VMEM,) * 3,
        compiler_params=params(),
        name="residual",
    )(terms, inverse, noise_weight, solution, residual, direction, step_length)
    norms = lax.all_to_all(norms, GRID_AXES, 0, 0, tiled=True)
    new_solution, new_residual, new_direction, new_norm = pl.pallas_call(
        direction_kernel,
        out_shape=(like, like, like, jax.ShapeDtypeStruct((cols,), F32)),
        in_specs=[VMEM] * 4 + [SMEM],
        out_specs=(HBM,) * 4,
        scratch_shapes=[held, pltpu.VMEM((cols,), F32), pltpu.SemaphoreType.DMA((4,))],
        compiler_params=params(),
        name="direction",
    )(norms, new_solution, new_residual, direction, old_norm)
    return (new_solution, new_residual, new_direction, new_norm)


def solution(mesh):
    return jax.shard_map(
        on_device,
        mesh=mesh,
        in_specs=(
            P("fq", None, "sx", "sy", None),
            P(("sx", "sy"), None),
            P("sx", "sy"),
            P(),
            P("fq", ("sx", "sy"), None),
            P("fq", ("sx", "sy"), None),
            P("fq", ("sx", "sy"), None),
            P("fq"),
            P("fq"),
        ),
        out_specs=(
            P("fq", ("sx", "sy"), None),
            P("fq", ("sx", "sy"), None),
            P("fq", ("sx", "sy"), None),
            P("fq"),
        ),
        check_vma=False,
    )
```

```python
import functools
import math

import jax
import jax.numpy as jnp
from jax import lax
from jax.experimental import pallas as pl
from jax.experimental.pallas import tpu as pltpu
from jax.sharding import PartitionSpec as P
import numpy as np

SWEEPS = 4
DEPTH = SWEEPS - 1
F32 = jnp.float32
BF16 = jnp.bfloat16
GRID_AXES = ("sx", "sy")
ALL_AXES = ("sx", "sy", "fq")
LANES = 128
MIB = 1024 * 1024
VMEM = pl.BlockSpec(memory_space=pltpu.VMEM)
SMEM = pl.BlockSpec(memory_space=pltpu.SMEM)
HBM = pl.BlockSpec(memory_space=pltpu.HBM)
ANY = pl.BlockSpec(memory_space=pl.ANY)


def params(mib=24):
    return pltpu.CompilerParams(vmem_limit_bytes=mib * MIB)


def tables(freq_count, local_freqs, local_cols, time_steps):
    freq = np.arange(freq_count)[:, None]
    step = np.arange(time_steps)[None, :]
    phases = (freq * step % time_steps) * (2.0 * math.pi / time_steps)
    factor = 1.0 / math.sqrt(time_steps)
    pair = np.stack([np.cos(phases) * factor, -np.sin(phases) * factor], 1)
    forward = np.repeat(pair.reshape(2 * freq_count, time_steps), local_cols, 0)
    doubling = np.where(np.arange(freq_count) == 0, 1.0, 2.0)[:, None, None]
    inverse = np.repeat((pair * doubling).reshape(2 * freq_count, time_steps), local_cols, 0)
    coarse = inverse.astype(jnp.bfloat16)
    fine = (inverse - coarse.astype(np.float64)).astype(jnp.bfloat16)
    rough = forward.T.astype(jnp.bfloat16)
    rest = (forward.T - rough.astype(np.float64)).astype(jnp.bfloat16)
    return np.stack([rough, rest]), np.concatenate([coarse, coarse, fine], axis=0)


def by_side(axis, low, high):
    even = lax.axis_index(axis) % 2 == 0
    return jnp.where(even, high, low), jnp.where(even, low, high)


def by_parity(axis, mine, other):
    even = lax.axis_index(axis) % 2 == 0
    return jnp.where(even, mine, other), jnp.where(even, other, mine)


def lane_ids(lanes):
    return lax.broadcasted_iota(jnp.int32, (1, lanes), 1)


def fetch_all(pairs, sems):
    copies = [pltpu.make_async_copy(a, b, sems.at[i]) for i, (a, b) in enumerate(pairs)]
    for copy in copies:
        copy.start()
    for copy in copies:
        copy.wait()


def spectrum_kernel(
    tiles, fq_blocks, direction_in, noise_in, table_in, out_ref, direction_ref, noise_ref, table_ref, sems
):
    fetch_all(
        ((direction_in, direction_ref), (noise_in, noise_ref), (table_in, table_ref)), sems
    )
    cols, sensors, steps = direction_ref.shape
    lanes = table_ref.shape[2]
    weighted = (noise_ref[...][None] * direction_ref[...]).reshape(cols * sensors, steps)
    coarse = weighted.astype(BF16)
    fine = (weighted - coarse.astype(F32)).astype(BF16)
    full = (
        jnp.dot(fine, table_ref[0], preferred_element_type=F32)
        + jnp.dot(coarse, table_ref[1], preferred_element_type=F32)
        + jnp.dot(coarse, table_ref[0], preferred_element_type=F32)
    )
    col_of = lane_ids(lanes) % cols
    spec = full[0:sensors]
    for col in range(1, cols):
        spec = jnp.where(col_of == col, full[col * sensors : (col + 1) * sensors], spec)
    spec = spec.astype(BF16)
    block = lanes // fq_blocks
    for b in range(fq_blocks):
        part = spec[:, b * block : (b + 1) * block]
        out_ref[:, b] = jnp.broadcast_to(part[None], (tiles, sensors, block))


def class_kernel(class_ref, after_ref, spectra_in, out_ref):
    cells_y, cells_x = class_ref.shape
    cells = cells_x * cells_y
    row = lax.broadcasted_iota(jnp.int32, (cells, cells_x), 0)
    pick = (row // cells_y == lax.broadcasted_iota(jnp.int32, (cells, cells_x), 1)).astype(F32)
    by_row = lax.dot_general(
        pick,
        class_ref[...].astype(F32) + 1.0,
        (((1,), (1,)), ((), ())),
        preferred_element_type=F32,
    )
    at = lax.broadcasted_iota(jnp.int32, (cells, cells_y), 0) % cells_y
    own = (at == lax.broadcasted_iota(jnp.int32, (cells, cells_y), 1)).astype(F32)
    out_ref[...] = jnp.dot(
        by_row * own, jnp.ones((cells_y, LANES), F32), preferred_element_type=F32
    )


def adjoint_of(part, stacked):
    _, cells_x, cells_y, all_sensors = part.shape
    both = part.reshape(2, cells_x * cells_y, all_sensors)
    both = jnp.concatenate([both[0], both[1]], axis=1)
    return jnp.dot(both, stacked, preferred_element_type=F32)


def freq_lanes(lanes, cols, freqs):
    return (lane_ids(lanes) // (2 * cols)) % freqs


def stacked_of(cols, mine_ref, other_ref):
    halves, group, sensors, block = mine_ref.shape
    lanes = group * block
    parts = []
    for b in range(group):
        pair = by_parity("sy", mine_ref[:, b], other_ref[:, b])
        parts.append(jnp.stack(pair, axis=1).reshape(2 * halves * sensors, block))
    direct = jnp.concatenate(parts, axis=1)
    wide = direct.astype(F32)
    is_real = (lane_ids(lanes) // cols) % 2 == 0
    turned = jnp.where(
        is_real, pltpu.roll(wide, lanes - cols, 1), -pltpu.roll(wide, cols, 1)
    ).astype(BF16)
    return jnp.concatenate([direct, turned], axis=0)


def adjoint_kernel(
    freqs, cols, spectra_ref, mine_ref, other_ref, class_ref, out_ref, far_ref, near_ref, ends_ref
):
    _, _, cells_x, cells_y, all_sensors = spectra_ref.shape
    stride = out_ref.shape[1] // cells_x
    lanes = mine_ref.shape[1] * mine_ref.shape[3]
    freq_of = freq_lanes(lanes, cols, freqs)
    stacked = stacked_of(cols, mine_ref, other_ref)
    acc = adjoint_of(spectra_ref[0], stacked)
    for f in range(1, freqs):
        acc = jnp.where(freq_of == f, adjoint_of(spectra_ref[f], stacked), acc)
    for k in range(out_ref.shape[0]):
        part = class_ref[...] if k * LANES == lanes else acc[:, k * LANES : (k + 1) * LANES]
        for x in range(cells_x):
            base = x * stride
            out_ref[k, base : base + cells_y] = part[x * cells_y : (x + 1) * cells_y]
            out_ref[k, base + cells_y : base + stride] = jnp.zeros((stride - cells_y, LANES), F32)
        at = slice(k * LANES, (k + 1) * LANES)
        for j in range(DEPTH):
            low = out_ref[k, pl.ds(j, cells_x, stride=stride), :]
            high = out_ref[k, pl.ds(cells_y - DEPTH + j, cells_x, stride=stride), :]
            near, far = by_side("sy", low, high)
            near_ref[j * cells_x : (j + 1) * cells_x, at] = near.astype(BF16)
            far_ref[j * cells_x : (j + 1) * cells_x, at] = far.astype(BF16)
        ends_ref[0, :, at] = out_ref[k, 0 : DEPTH * stride]
        ends_ref[1, :, at] = out_ref[k, (cells_x - DEPTH) * stride : cells_x * stride]


def ends_kernel(ends_ref, far_ref, near_ref, far_out, near_out, held):
    span = ends_ref.shape[1]
    stride = span // DEPTH
    cells_x = near_ref.shape[0] // DEPTH
    cells_y = stride - 8
    after, before = by_side("sy", far_ref[...].astype(F32), near_ref[...].astype(F32))
    built = []
    for side in range(2):
        held[...] = jnp.zeros_like(held)
        held[8 : 8 + span] = ends_ref[side]
        first = 0 if side == 0 else cells_x - DEPTH
        for x in range(DEPTH):
            for j in range(DEPTH):
                take = j * cells_x + first + x
                to = 8 + x * stride
                held[to + cells_y + j : to + cells_y + j + 1] = after[take : take + 1]
                held[to - DEPTH + j : to - DEPTH + j + 1] = before[take : take + 1]
        built.append(held[8 - DEPTH : 8 - DEPTH + span])
    near, far = by_side("sx", built[0], built[1])
    near_out[...] = near.astype(BF16)
    far_out[...] = far.astype(BF16)


def coefficients(classes, kappa_ref):
    kappa = jnp.zeros_like(classes)
    for n in range(kappa_ref.shape[0]):
        kappa = jnp.where(classes == n + 1.0, kappa_ref[n], kappa)
    scale = jnp.where(classes > 0.0, 1.0 / (1.0 + 4.0 * kappa), 0.0)
    return scale, kappa * scale


def sweep(source, gain, old, new, first, last, stride):
    near = (
        old[first - stride : last - stride]
        + old[first + stride : last + stride]
        + old[first - 1 : last - 1]
        + old[first + 1 : last + 1]
    )
    new[first:last] = source[first:last] + gain[first:last] * near


def both_forms(turned, cols):
    blocks, cells = turned.shape[0] // (2 * cols), turned.shape[1]
    pair = turned.reshape(blocks, 2, cols, cells)
    plain = pair.astype(BF16).reshape(blocks, 2 * cols, cells)
    crossed = jnp.stack([-pair[:, 1], pair[:, 0]], axis=1)
    crossed = crossed.astype(BF16).reshape(blocks, 2 * cols, cells)
    return jnp.concatenate([plain, crossed], axis=2)


def rows_of(forms, f, freqs):
    return jnp.concatenate([forms[b] for b in range(f, forms.shape[0], freqs)], axis=0)


def own_kernel(source_ref, kappa_ref, scaled_ref, gain_ref):
    slabs = scaled_ref.shape[0]
    scale, gain_ref[...] = coefficients(source_ref[slabs], kappa_ref)
    for k in range(slabs):
        scaled_ref[k] = source_ref[k] * scale


def inner_kernel(
    freqs,
    cols,
    spectra_ref,
    scaled_ref,
    own_gain_ref,
    far_y_ref,
    near_y_ref,
    kappa_ref,
    sums_ref,
    wide,
    gain,
    one,
    two,
):
    _, _, cells_x, cells_y, all_sensors = spectra_ref.shape
    cells = cells_x * cells_y
    slabs, rows, _ = scaled_ref.shape
    stride = rows // cells_x
    start = 2 * stride
    after, before = by_side("sy", far_y_ref[...].astype(F32), near_y_ref[...].astype(F32))
    gain[start - 8 : start] = jnp.zeros((8, LANES), F32)
    gain[start : start + rows] = own_gain_ref[...]
    for k in range(slabs):
        wide[k, start - 8 : start] = jnp.zeros((8, LANES), F32)
        wide[k, start : start + rows] = scaled_ref[k]
    for side, halo in ((0, before), (1, after)):
        scale, halo_gain = coefficients(halo[:, slabs * LANES :], kappa_ref)
        scaled = [halo[:, k * LANES : (k + 1) * LANES] * scale for k in range(slabs)]
        for j in range(DEPTH):
            part = slice(j * cells_x, (j + 1) * cells_x)
            to = pl.ds(start + j + (cells_y if side else -DEPTH), cells_x, stride=stride)
            gain[to, :] = halo_gain[part]
            for k in range(slabs):
                wide[k, to, :] = scaled[k][part]
    turned = []
    for k in range(slabs):
        old, new = wide.at[k], one.at[k]
        for x in range(1, DEPTH + 1):
            first, last = start + x * stride - 8, start + rows - x * stride
            sweep(wide.at[k], gain, old, new, first, last, stride)
            old, new = new, (two.at[k] if x % 2 else one.at[k])
        inner = old[start + DEPTH * stride : start + rows - DEPTH * stride]
        inner = inner.reshape(cells_x - 2 * DEPTH, stride, LANES)[:, 0:cells_y]
        edge = jnp.zeros((DEPTH * cells_y, LANES), F32)
        turned.append(
            jnp.concatenate([edge, inner.reshape(cells - 2 * DEPTH * cells_y, LANES), edge], axis=0).T
        )
    forms = both_forms(jnp.concatenate(turned, axis=0), cols)
    groups = forms.shape[0] // freqs
    for f in range(freqs):
        right = spectra_ref[f].reshape(2 * cells, all_sensors)
        got = jnp.dot(rows_of(forms, f, freqs), right, preferred_element_type=F32)
        for g in range(groups):
            at = (g * freqs + f) * 2 * cols
            sums_ref[at : at + 2 * cols] = got[g * 2 * cols : (g + 1) * 2 * cols]


def field_kernel(
    freqs,
    cols,
    spectra_ref,
    wide_ref,
    gain_ref,
    sums_ref,
    far_x_ref,
    near_x_ref,
    kappa_ref,
    keep_ref,
    send_ref,
    wide,
    gain,
    one,
    two,
    sums,
):
    _, _, cells_x, cells_y, all_sensors = spectra_ref.shape
    slabs = wide_ref.shape[0]
    stride = far_x_ref.shape[0] // DEPTH
    start = stride + 8
    deep = 2 * DEPTH

    def base(x):
        return start + x * stride

    below, above = by_side("sx", far_x_ref[...].astype(F32), near_x_ref[...].astype(F32))
    for end in range(2):
        own, outer = (DEPTH, 0) if end == 0 else (0, deep)
        inside = 0 if end == 0 else cells_x - deep
        beyond = above if end == 0 else below
        scale, beyond_gain = coefficients(beyond[:, slabs * LANES :], kappa_ref)
        for k in range(slabs + 1):
            to = wide.at[end, k] if k < slabs else gain.at[end]
            inner = wide_ref.at[k] if k < slabs else gain_ref
            first = (2 + inside) * stride
            to[base(0) - 8 : base(0)] = jnp.zeros((8, LANES), F32)
            to[base(3 * DEPTH) - 8 : base(3 * DEPTH)] = jnp.zeros((8, LANES), F32)
            to[base(own) - 8 : base(own + deep)] = inner[first - 8 : first + deep * stride]
            to[base(outer) - DEPTH : base(outer + DEPTH) - DEPTH] = (
                beyond[:, k * LANES : (k + 1) * LANES] * scale if k < slabs else beyond_gain
            )
    turned = []
    filler = -(deep * cells_y) % LANES
    for k in range(slabs):
        fields = []
        for end in range(2):
            source = wide.at[end, k]
            old, new = source, one.at[end, k]
            for x in range(1, DEPTH + 1):
                sweep(source, gain.at[end], old, new, base(x) - 8, base(3 * DEPTH - x), stride)
                old, new = new, (two.at[end, k] if x % 2 else one.at[end, k])
            field = old[base(DEPTH) : base(deep)].reshape(DEPTH, stride, LANES)[:, 0:cells_y]
            fields.append(field.reshape(DEPTH * cells_y, LANES))
        fields.append(jnp.zeros((filler, LANES), F32))
        turned.append(jnp.concatenate(fields, axis=0).T)
    forms = both_forms(jnp.concatenate(turned, axis=0), cols)
    groups = forms.shape[0] // freqs
    blank = jnp.zeros((filler, all_sensors), BF16)
    for f in range(freqs):
        right = []
        for part in range(2):
            for x in (0, cells_x - DEPTH):
                rows_here = spectra_ref[f, part, x : x + DEPTH]
                right.append(rows_here.reshape(DEPTH * cells_y, all_sensors))
            right.append(blank)
        got = jnp.dot(
            rows_of(forms, f, freqs), jnp.concatenate(right, axis=0), preferred_element_type=F32
        )
        for g in range(groups):
            at = (g * freqs + f) * 2 * cols
            sums[at : at + 2 * cols] = sums_ref[at : at + 2 * cols] + got[g * 2 * cols : (g + 1) * 2 * cols]
    back = sums[...].T
    halves, _, sensors, block = keep_ref.shape
    for g in range(groups):
        pair = back[:, g * block : (g + 1) * block].reshape(halves, 2, sensors, block)
        keep, send = by_parity("sy", pair[:, 0], pair[:, 1])
        keep_ref[:, g] = keep
        send_ref[:, g] = send.astype(BF16)


def residual_kernel(
    terms_ref,
    table_ref,
    noise_ref,
    solution_ref,
    residual_ref,
    direction_ref,
    step_ref,
    new_solution_ref,
    new_residual_ref,
    norm_ref,
):
    cols, sensors, steps = direction_ref.shape
    parts = []
    for b in range(terms_ref.shape[1]):
        parts.append(jnp.sum(terms_ref[:, b].astype(F32), axis=0))
    spectrum = jnp.concatenate(parts, axis=1)
    col_of = lane_ids(spectrum.shape[1]) % cols
    left = jnp.concatenate([jnp.where(col_of == c, spectrum, 0.0) for c in range(cols)], axis=0)
    coarse = left.astype(BF16)
    fine = (left - coarse.astype(F32)).astype(BF16)
    returned = jnp.dot(
        jnp.concatenate([coarse, fine, coarse], axis=1), table_ref[...], preferred_element_type=F32
    )
    squares = []
    for c in range(cols):
        product = direction_ref[c] + noise_ref[...] * returned[c * sensors : (c + 1) * sensors]
        new_residual = residual_ref[c] - step_ref[c] * product
        new_residual_ref[c] = new_residual
        new_solution_ref[c] = solution_ref[c] + step_ref[c] * direction_ref[c]
        squares.append(jnp.sum(new_residual * new_residual, axis=0, keepdims=True))
    norms = jnp.sum(jnp.concatenate(squares, axis=0), axis=1, keepdims=True)
    on_lane = lax.broadcasted_iota(jnp.int32, (cols, LANES), 0) == lane_ids(LANES)
    norms = jnp.sum(jnp.where(on_lane, norms, 0.0), axis=0, keepdims=True)
    norm_ref[...] = jnp.broadcast_to(norms[None], norm_ref.shape)


def direction_kernel(
    norms_ref,
    solution_ref,
    residual_ref,
    direction_ref,
    old_ref,
    solution_out,
    residual_out,
    direction_out,
    norm_out,
    held,
    norm_ref,
    sems,
):
    cols, sensors, steps = direction_ref.shape
    early = [
        pltpu.make_async_copy(solution_ref, solution_out, sems.at[0]),
        pltpu.make_async_copy(residual_ref, residual_out, sems.at[1]),
    ]
    for copy in early:
        copy.start()
    norm = jnp.sum(norms_ref[...], axis=0)
    norm_ref[...] = norm[0, 0:cols]
    final = pltpu.make_async_copy(norm_ref, norm_out, sems.at[3])
    final.start()
    for c in range(cols):
        held[c] = residual_ref[c] + (norm[:, c : c + 1] / old_ref[c]) * direction_ref[c]
    last = pltpu.make_async_copy(held, direction_out, sems.at[2])
    last.start()
    for copy in (*early, last, final):
        copy.wait()


def swap(axis, toward_partner, toward_other):
    count = lax.axis_size(axis)
    near = [(i, i ^ 1) for i in range(count) if (i ^ 1) < count]
    far = [(i, i + 1 if i % 2 else i - 1) for i in range(1, count - 1 + count % 2)]
    second = lax.ppermute(toward_other, axis, far)
    first = lax.ppermute(toward_partner, axis, near)
    return first, second


def partners(axis):
    return [(i, i ^ 1) for i in range(lax.axis_size(axis))]


def exchange_half(blocks):
    sx, sy, fq = (lax.axis_size(axis) for axis in ALL_AXES)
    groups = [
        [(x * sy + y) * fq + f for x in range(sx) for y in range(parity, sy, 2) for f in range(fq)]
        for parity in range(2)
    ]
    flat = blocks.reshape((-1,) + blocks.shape[2:])
    return lax.all_to_all(flat, ALL_AXES, 0, 0, axis_index_groups=groups, tiled=True).reshape(
        blocks.shape
    )


def on_device(
    spectra,
    noise_weight,
    class_map,
    class_kappa,
    solution,
    residual,
    direction,
    step_length,
    old_norm,
):
    local_freqs, _, cells_x, cells_y, all_sensors = spectra.shape
    cols, sensors, steps = direction.shape
    fq_blocks = lax.axis_size("fq")
    tiles = lax.axis_size("sx") * lax.axis_size("sy")
    halves = tiles // 2
    block = 2 * local_freqs * cols
    lanes = block * fq_blocks
    forward, inverse = tables(local_freqs * fq_blocks, local_freqs, cols, steps)
    group = 2 if fq_blocks % 2 == 0 else 1
    chunks = fq_blocks // group
    width = group * block
    stride = cells_y + 8
    wide = width + LANES
    cells = cells_x * cells_y

    like = jax.ShapeDtypeStruct(direction.shape, F32)
    held = pltpu.VMEM(direction.shape, F32)
    spec = pl.pallas_call(
        functools.partial(spectrum_kernel, halves, fq_blocks),
        out_shape=jax.ShapeDtypeStruct((halves, fq_blocks, sensors, block), BF16),
        in_specs=[HBM] * 3,
        out_specs=VMEM,
        scratch_shapes=[
            held,
            pltpu.VMEM(noise_weight.shape, F32),
            pltpu.VMEM(forward.shape, BF16),
            pltpu.SemaphoreType.DMA((3,)),
        ],
        compiler_params=params(62),
        cost_estimate=pl.CostEstimate(
            flops=2 * spectra.size, bytes_accessed=4 * spectra.size, transcendentals=0
        ),
        name="spectrum",
    )(direction, noise_weight, forward)
    mine = exchange_half(spec)
    other = lax.ppermute(mine, "sy", partners("sy"))
    classes = pl.pallas_call(
        class_kernel,
        out_shape=jax.ShapeDtypeStruct((cells, LANES), F32),
        in_specs=[VMEM, ANY, HBM],
        out_specs=VMEM,
        compiler_params=params(48),
        name="classes",
    )(class_map.T, mine, spectra)

    edge = jax.ShapeDtypeStruct((DEPTH * cells_x, wide), BF16)
    end = jax.ShapeDtypeStruct((DEPTH * stride, wide), BF16)
    total = (cells_x + 4) * stride
    strip = (3 * DEPTH + 2) * stride + 16
    slabs = width // LANES
    pieces = []
    for i in range(chunks):
        at = slice(i * group, (i + 1) * group)
        source, far_y, near_y, ends = pl.pallas_call(
            functools.partial(adjoint_kernel, local_freqs, cols),
            out_shape=(
                jax.ShapeDtypeStruct((slabs + 1, cells_x * stride, LANES), F32),
                edge,
                edge,
                jax.ShapeDtypeStruct((2, DEPTH * stride, wide), F32),
            ),
            in_specs=[VMEM] * 4,
            out_specs=(VMEM,) * 4,
            compiler_params=params(),
            name="adjoint",
        )(spectra, mine[:, at], other[:, at], classes)
        near_y, far_y = swap("sy", near_y, far_y)
        far_x, near_x = pl.pallas_call(
            ends_kernel,
            out_shape=(end, end),
            in_specs=[VMEM] * 3,
            out_specs=(VMEM,) * 2,
            scratch_shapes=[pltpu.VMEM((DEPTH * stride + 16, wide), F32)],
            compiler_params=params(),
            name="ends",
        )(ends, far_y, near_y)
        near_x, far_x = swap("sx", near_x, far_x)
        scaled, own_gain = pl.pallas_call(
            own_kernel,
            out_shape=(
                jax.ShapeDtypeStruct((slabs, cells_x * stride, LANES), F32),
                jax.ShapeDtypeStruct((cells_x * stride, LANES), F32),
            ),
            in_specs=[VMEM, SMEM],
            out_specs=(VMEM,) * 2,
            compiler_params=params(),
            name="own",
        )(source, class_kappa)
        sums, around, gains = pl.pallas_call(
            functools.partial(inner_kernel, local_freqs, cols),
            out_shape=(
                jax.ShapeDtypeStruct((width, all_sensors), F32),
                jax.ShapeDtypeStruct((slabs, total, LANES), F32),
                jax.ShapeDtypeStruct((total, LANES), F32),
            ),
            in_specs=[VMEM] * 5 + [SMEM],
            out_specs=(VMEM,) * 3,
            scratch_shapes=[
                pltpu.VMEM((slabs, total, LANES), F32),
                pltpu.VMEM((slabs, total, LANES), F32),
            ],
            compiler_params=params(),
            cost_estimate=pl.CostEstimate(
                flops=4 * spectra.size * width, bytes_accessed=2 * spectra.size, transcendentals=0
            ),
            name="inner",
        )(spectra, scaled, own_gain, far_y, near_y, class_kappa)
        pieces.append(
            pl.pallas_call(
                functools.partial(field_kernel, local_freqs, cols),
                out_shape=(
                    jax.ShapeDtypeStruct((halves, group, sensors, block), F32),
                    jax.ShapeDtypeStruct((halves, group, sensors, block), BF16),
                ),
                in_specs=[VMEM] * 6 + [SMEM],
                out_specs=(VMEM,) * 2,
                scratch_shapes=[
                    pltpu.VMEM((2, slabs, strip, LANES), F32),
                    pltpu.VMEM((2, strip, LANES), F32),
                    pltpu.VMEM((2, slabs, strip, LANES), F32),
                    pltpu.VMEM((2, slabs, strip, LANES), F32),
                    pltpu.VMEM((width, all_sensors), F32),
                ],
                compiler_params=params(),
                name="field",
            )(spectra, around, gains, sums, far_x, near_x, class_kappa)
        )
    keep = jnp.concatenate([piece[0] for piece in pieces], axis=1)
    send = jnp.concatenate([piece[1] for piece in pieces], axis=1)
    taken = lax.ppermute(send, "sy", partners("sy"))
    terms = exchange_half((keep + taken.astype(F32)).astype(BF16))
    new_solution, new_residual, norms = pl.pallas_call(
        residual_kernel,
        out_shape=(like, like, jax.ShapeDtypeStruct((tiles, 1, LANES), F32)),
        in_specs=[VMEM] * 6 + [SMEM],
        out_specs=(VMEM,) * 3,
        compiler_params=params(),
        name="residual",
    )(terms, inverse, noise_weight, solution, residual, direction, step_length)
    norms = lax.all_to_all(norms, GRID_AXES, 0, 0, tiled=True)
    new_solution, new_residual, new_direction, new_norm = pl.pallas_call(
        direction_kernel,
        out_shape=(like, like, like, jax.ShapeDtypeStruct((cols,), F32)),
        in_specs=[VMEM] * 4 + [SMEM],
        out_specs=(HBM,) * 4,
        scratch_shapes=[held, pltpu.VMEM((cols,), F32), pltpu.SemaphoreType.DMA((4,))],
        compiler_params=params(),
        name="direction",
    )(norms, new_solution, new_residual, direction, old_norm)
    return (new_solution, new_residual, new_direction, new_norm)


def solution(mesh):
    return jax.shard_map(
        on_device,
        mesh=mesh,
        in_specs=(
            P("fq", None, "sx", "sy", None),
            P(("sx", "sy"), None),
            P("sx", "sy"),
            P(),
            P("fq", ("sx", "sy"), None),
            P("fq", ("sx", "sy"), None),
            P("fq", ("sx", "sy"), None),
            P("fq"),
            P("fq"),
        ),
        out_specs=(
            P("fq", ("sx", "sy"), None),
            P("fq", ("sx", "sy"), None),
            P("fq", ("sx", "sy"), None),
            P("fq"),
        ),
        check_vma=False,
    )
```
